256 devices in a mesh: panel: 2 (over core), lat: 8 (over y_hi, x), lon: 16 (over y_lo, z).
Axes of the slice: x: 4, y: 4 (y_hi: 2, y_lo: 2; y = y_hi * 2 + y_lo), z: 8, core: 2. Of those that a mesh axis runs over, the one named last changes fastest.
Arguments:
- scalars: float32 [2, 2, 24, 128, 2048], P('panel', None, None, 'lat', 'lon'), may hold values from 0.5 to 2
- vectors: float32 [2, 6, 24, 128, 2048], P('panel', None, None, 'lat', 'lon'), may hold values from -4 to 4
- corner_rows: int32 [8, 16, 16, 19], P('lat', 'lon'), may hold values from 0 to 14
- corner_cols: int32 [8, 16, 16, 19], P('lat', 'lon'), may hold values from 0 to 126
- send_weights: float32 [2, 8, 16, 16, 19], P(None, 'lat', 'lon'), may hold values from 0 to 1
- recv_source: int32 [8, 16, 592], P('lat', 'lon'), may hold values from -1 to 303, as said below
Outputs:
- scalar_rate: float32 [2, 2, 24, 128, 2048], P('panel', None, None, 'lat', 'lon')
- vector_rate: float32 [2, 6, 24, 128, 2048], P('panel', None, None, 'lat', 'lon')
The draws below stay inside these ranges and needn't reach their ends.
Inputs may be any that keep to these rules, and one draw needn't show every extreme that they name: `recv_source`: -1 exactly at the frame cells of block (i, r) that lie inside the panel; every other entry is q * 19 + j, slot j of donor block q of the same lat row on the other panel; no (q, j) twice for one block; some block takes all 19 slots of one donor; one table serves both panels.
All inputs are finite; a program needn't handle non-finite values.
Results may differ from the reference program's by a relative error of at most 0.0003.
Values sent between devices are 32-bit elements; how exact they have to be, the bound alone decides.
No kernel may reach another device: no remote copies, remote signals or barrier semaphores. Data moves between devices by JAX's collectives and lax.ppermute only.
A program may use at most 128 MiB of HBM per device.

```python
import math
from functools import partial
import jax
import jax.numpy as jnp
from jax import lax

CT = 16
CP = 128
R = 24
NT = 128
NP = 2048
CAP = 19
N_LAT = 8
N_LON = 16


def cycle_layout_drawn(n_rows, n_cols):
    all_cols = jnp.arange(n_cols + 4, dtype=jnp.int32)
    mid_rows = jnp.arange(n_rows, dtype=jnp.int32) + 2
    zero_row = jnp.zeros(n_cols + 4, jnp.int32)
    cycle_rows = jnp.concatenate([zero_row, zero_row + 1, zero_row + n_rows + 2, zero_row + n_rows + 3, jnp.repeat(mid_rows, 2), jnp.repeat(mid_rows, 2)])
    pair_cols = jnp.arange(2 * n_rows, dtype=jnp.int32) % 2
    cycle_cols = jnp.concatenate([all_cols, all_cols, all_cols, all_cols, pair_cols, pair_cols + n_cols + 2])
    return (cycle_rows, cycle_cols)


def draw_recv_source(key, part):
    key = jax.random.fold_in(key, 7)
    key_rank, key_order, key_shift = jax.random.split(key, 3)
    cycle_rows, cycle_cols = cycle_layout_drawn(CT, CP)
    cycle_size = cycle_rows.shape[0]
    lat_first = jnp.arange(N_LAT, dtype=jnp.int32)[:, None, None] * CT
    lon_index = jnp.arange(N_LON, dtype=jnp.int32)[None, :, None]
    grid_row = lat_first - 2 + cycle_rows[None, None, :]
    grid_col = lon_index * CP - 2 + cycle_cols[None, None, :]
    is_live = (grid_row < 0) | (grid_row >= CT * N_LAT) | (grid_col < 0) | (grid_col >= CP * N_LON)
    jitter = jax.random.randint(key_rank, (N_LAT, N_LON, cycle_size), 0, cycle_size)
    scores = jitter * cycle_size + jnp.arange(cycle_size, dtype=jnp.int32) + jnp.where(is_live, 0, cycle_size * cycle_size)
    ordering = jnp.argsort(scores, axis=-1)
    ranking = jnp.argsort(ordering, axis=-1).astype(jnp.int32)
    groups = jnp.minimum(ranking // CAP, N_LON - 1)
    offsets = jnp.concatenate([jnp.array([N_LON - 1], jnp.int32), jax.random.permutation(key_order, N_LON - 1).astype(jnp.int32)])
    donors = (lon_index + offsets[groups]) % N_LON
    rotate = jax.random.randint(key_shift, (N_LAT, N_LON, 1), 0, CAP)
    slot_index = (ranking % CAP + rotate) % CAP
    return jnp.where(is_live, donors * CAP + slot_index, -1).astype(jnp.int32)


def place_ends(entries, stream_key, low, top_value):
    spot = [jax.random.randint(jax.random.fold_in(stream_key, axis), (), 0, length) for axis, length in enumerate(entries.shape)]
    widest = entries.shape.index(max(entries.shape))
    next_to = spot[:widest] + [(spot[widest] + 1) % entries.shape[widest]] + spot[widest + 1:]
    return entries.at[tuple(spot)].set(low).at[tuple(next_to)].set(top_value)


def steps_of(key, shape, pieces, least, largest):
    loudness, own = 1.0, jax.random.fold_in(key, 6)
    for dim, blocks in pieces:
        heights = jnp.exp(jax.random.uniform(jax.random.fold_in(own, dim), (blocks,), jnp.float32, least / len(pieces), largest / len(pieces)))
        loudness = loudness * jnp.repeat(heights, shape[dim] // blocks).reshape([-1 if axis == dim else 1 for axis in range(len(shape))])
    return loudness


def bell_draw(stream_key, shape, spread, limit, cuts=(), kind=jnp.bfloat16):
    values = spread * jax.random.normal(stream_key, shape, jnp.float32)
    if cuts:
        values = values * steps_of(stream_key, shape, cuts, -0.22, 0.18)
    return jnp.clip(values, -limit, limit).astype(kind)


def setup_inputs(seed: int = 0) -> dict:
    seeds = jax.random.split(jax.random.key(seed), 7)
    return {
        "scalars": jnp.clip(jnp.exp(math.log(2.0) - 1.3862944 * jax.random.uniform(seeds[0], (2, 2, R, NT, NP), jnp.float32) ** steps_of(seeds[0], (2, 2, R, NT, NP), ((0, 2), (3, 8), (4, 16)), -0.2, 0.2)), 0.5, 2.0),
        "vectors": bell_draw(seeds[1], (2, 6, R, NT, NP), 1.0, 4.0, ((0, 2), (3, 8), (4, 16)), jnp.float32),
        "corner_rows": place_ends(jax.random.randint(seeds[2], (N_LAT, N_LON, N_LON, CAP), 0, CT - 1), jax.random.fold_in(seeds[2], 1), 0, (CT - 1) - 1).astype(jnp.int32),
        "corner_cols": place_ends(jax.random.randint(seeds[3], (N_LAT, N_LON, N_LON, CAP), 0, CP - 1), jax.random.fold_in(seeds[3], 1), 0, (CP - 1) - 1).astype(jnp.int32),
        "send_weights": jnp.clip(1.0 * jax.random.uniform(seeds[4], (2, N_LAT, N_LON, N_LON, CAP), jnp.float32) ** steps_of(seeds[4], (2, N_LAT, N_LON, N_LON, CAP), ((1, 8), (2, 16)), -0.2, 0.2), 0.0, 1.0),
        "recv_source": draw_recv_source(jax.random.fold_in(seeds[6], 71), 0),
    }


GAMMA = 5.0 / 3.0
shell_block = 8


def spacing(n_theta, n_phi):
    step_theta = 0.5 * math.pi / n_theta
    step_phi = 1.5 * math.pi / n_phi
    step_radius = 0.6 * step_theta
    smallest = min(step_radius, 0.6 * math.sin(0.25 * math.pi - 2.0 * step_theta) * step_phi)
    return step_theta, step_phi, step_radius, 0.3 * smallest


def angle_at(index_vals, anchor, step_size):
    return anchor + (index_vals.astype(jnp.float32) + 0.5) * step_size


def coordinate(first_row, length, anchor, step_size):
    return angle_at(jnp.arange(length, dtype=jnp.int32) + first_row, anchor, step_size)


def crop_one(field_in):
    return field_in[..., 1:-1, 1:-1, 1:-1]


def level_geometry(coords, cut):
    radius_all, theta_all, phi_all = coords
    radius = radius_all[cut:radius_all.shape[0] - cut][:, None, None]
    theta_vals = theta_all[cut:theta_all.shape[0] - cut][None, :, None]
    phi_vals = phi_all[cut:phi_all.shape[0] - cut][None, None, :]
    sin_the = jnp.sin(theta_vals)
    cos_the = jnp.cos(theta_vals)
    return radius, sin_the, cos_the / sin_the, phi_vals, cos_the


def derivatives(field_in, geometry, spacings):
    radius, sin_the = geometry[0], geometry[1]
    d_rad = (field_in[..., 2:, 1:-1, 1:-1] - field_in[..., :-2, 1:-1, 1:-1]) / (2.0 * spacings[2])
    d_the = (field_in[..., 1:-1, 2:, 1:-1] - field_in[..., 1:-1, :-2, 1:-1]) / (2.0 * spacings[0] * radius)
    d_phi = (field_in[..., 1:-1, 1:-1, 2:] - field_in[..., 1:-1, 1:-1, :-2]) / (2.0 * spacings[1] * radius * sin_the)
    return d_rad, d_the, d_phi


def curl_of(vector, geometry, spacings):
    d_rad, d_the, d_phi = derivatives(vector, geometry, spacings)
    middle = crop_one(vector)
    radius, cot_the = geometry[0], geometry[2]
    return jnp.stack([d_the[2] + middle[2] * cot_the / radius - d_phi[1],
                      d_phi[0] - d_rad[2] - middle[2] / radius,
                      d_rad[1] + middle[1] / radius - d_the[0]])


def divergence(vector, geometry, spacings):
    d_rad, d_the, d_phi = derivatives(vector, geometry, spacings)
    middle = crop_one(vector)
    radius, cot_the = geometry[0], geometry[2]
    return d_rad[0] + 2.0 * middle[0] / radius + d_the[1] + middle[1] * cot_the / radius + d_phi[2]


def cross_product(first_vec, second_vec):
    return jnp.stack([first_vec[1] * second_vec[2] - first_vec[2] * second_vec[1],
                      first_vec[2] * second_vec[0] - first_vec[0] * second_vec[2],
                      first_vec[0] * second_vec[1] - first_vec[1] * second_vec[0]])


def tendency(slab_state, coords, yang_flag, spacings):
    time_step = spacings[3]
    viscosity = time_step / 0.9
    gravity = 0.036 / time_step
    rotation = 0.05 / time_step
    outer = level_geometry(coords, 1)
    inner = level_geometry(coords, 2)
    velocity = slab_state[2:5]
    magnet = slab_state[5:8]
    current_one = curl_of(magnet, outer, spacings)
    vortic_one = curl_of(velocity, outer, spacings)
    expand_one = divergence(velocity, outer, spacings)
    density_one = crop_one(slab_state[0])
    pressure_one = crop_one(slab_state[1])
    velocity_one = crop_one(velocity)
    magnet_one = crop_one(magnet)
    electric_one = cross_product(velocity_one, magnet_one) - viscosity * current_one
    flux_one = density_one[None] * velocity_one
    radius, sin_the, cot_the, phi_vals, cos_the = inner
    density_zero = crop_one(density_one)
    pressure_zero = crop_one(pressure_one)
    velocity_zero = crop_one(velocity_one)
    magnet_zero = crop_one(magnet_one)
    mass_rate = -divergence(flux_one, inner, spacings)
    grad_rad, grad_the, grad_phi = derivatives(velocity_one, inner, spacings)
    advect = velocity_zero[0] * grad_rad + velocity_zero[1] * grad_the + velocity_zero[2] * grad_phi
    curvature = jnp.stack([-(velocity_zero[1] * velocity_zero[1] + velocity_zero[2] * velocity_zero[2]) / radius,
                           (velocity_zero[0] * velocity_zero[1] - velocity_zero[2] * velocity_zero[2] * cot_the) / radius,
                           (velocity_zero[0] * velocity_zero[2] + velocity_zero[1] * velocity_zero[2] * cot_the) / radius])
    press_grad = jnp.stack(derivatives(pressure_one, inner, spacings))
    expand_grad = jnp.stack(derivatives(expand_one, inner, spacings))
    twice_curl = curl_of(vortic_one, inner, spacings)
    out_shape = density_zero.shape
    spin_axis = jnp.stack([
        jnp.broadcast_to((1.0 - yang_flag) * cos_the + yang_flag * sin_the * jnp.sin(phi_vals), out_shape),
        jnp.broadcast_to((1.0 - yang_flag) * (-sin_the) + yang_flag * cos_the * jnp.sin(phi_vals), out_shape),
        jnp.broadcast_to(yang_flag * jnp.cos(phi_vals), out_shape)])
    lorentz = cross_product(crop_one(current_one), magnet_zero)
    acceleration = -(advect + curvature) + (lorentz - press_grad + viscosity * (4.0 / 3.0 * expand_grad - twice_curl)) / density_zero[None] + 2.0 * rotation * cross_product(velocity_zero, spin_axis)
    acceleration = jnp.stack([acceleration[0] - gravity / (radius * radius), acceleration[1], acceleration[2]])
    pressure_rate = -(velocity_zero[0] * press_grad[0] + velocity_zero[1] * press_grad[1] + velocity_zero[2] * press_grad[2]) - GAMMA * pressure_zero * crop_one(expand_one)
    induction = curl_of(electric_one, inner, spacings)
    return time_step * jnp.stack([mass_rate, pressure_rate]), time_step * jnp.concatenate([acceleration, induction], axis=0)


def slab_rates(extended, theta_all, phi_all, yang_flag, spacings):
    shells = extended.shape[1]
    slab_count = shells // shell_block
    n_rows, n_cols = extended.shape[2] - 4, extended.shape[3] - 4

    def one_slab(slab_index, outputs):
        slab_start = (slab_index * shell_block).astype(jnp.int32)
        shell_ids = jnp.clip(slab_start - 2 + jnp.arange(shell_block + 4, dtype=jnp.int32), 0, shells - 1).astype(jnp.int32)
        slab_piece = jnp.take(extended, shell_ids, axis=1)
        radius_all = coordinate(slab_start - 2, shell_block + 4, 0.6, spacings[2])
        scalar_part, vector_part = tendency(slab_piece, (radius_all, theta_all, phi_all), yang_flag, spacings)
        return (lax.dynamic_update_slice_in_dim(outputs[0], scalar_part.astype(outputs[0].dtype), slab_start, 1),
                lax.dynamic_update_slice_in_dim(outputs[1], vector_part.astype(outputs[1].dtype), slab_start, 1))

    start_vals = (jnp.zeros((2, shells, n_rows, n_cols), extended.dtype),
                  jnp.zeros((6, shells, n_rows, n_cols), extended.dtype))
    return lax.fori_loop(0, slab_count, one_slab, start_vals)


def to_cartesian(radial, polar_c, azimuth, theta_at, phi_at):
    sin_the, cos_the = jnp.sin(theta_at), jnp.cos(theta_at)
    sin_phi, cos_phi = jnp.sin(phi_at), jnp.cos(phi_at)
    along_x = radial * sin_the * cos_phi + polar_c * cos_the * cos_phi - azimuth * sin_phi
    along_y = radial * sin_the * sin_phi + polar_c * cos_the * sin_phi + azimuth * cos_phi
    along_z = radial * cos_the - polar_c * sin_the
    return along_x, along_y, along_z


def to_spherical(along_x, along_y, along_z, theta_at, phi_at):
    sin_the, cos_the = jnp.sin(theta_at), jnp.cos(theta_at)
    sin_phi, cos_phi = jnp.sin(phi_at), jnp.cos(phi_at)
    radial = along_x * sin_the * cos_phi + along_y * sin_the * sin_phi + along_z * cos_the
    polar_c = along_x * cos_the * cos_phi + along_y * cos_the * sin_phi - along_z * sin_the
    azimuth = -along_x * sin_phi + along_y * cos_phi
    return radial, polar_c, azimuth


def donor_table(own_state, theta_own, phi_own):
    shells, n_rows, n_cols = own_state.shape[1], own_state.shape[2], own_state.shape[3]
    theta_at = theta_own[:, None]
    phi_at = phi_own[None, :]
    velocity = to_cartesian(own_state[2], own_state[3], own_state[4], theta_at, phi_at)
    magnet = to_cartesian(own_state[5], own_state[6], own_state[7], theta_at, phi_at)
    cartesian = jnp.stack([own_state[0], own_state[1], velocity[0], velocity[1], velocity[2], magnet[0], magnet[1], magnet[2]])
    return cartesian.reshape(8 * shells, n_rows * n_cols)


def corner_terms(lookup, corner_row, corner_col, weights, n_cols):
    base_index = (corner_row * n_cols + corner_col).reshape(-1).astype(jnp.int32)
    weight_the = weights[0].reshape(1, -1)
    weight_phi = weights[1].reshape(1, -1)
    return [(1.0 - weight_the) * (1.0 - weight_phi) * jnp.take(lookup, base_index, axis=1),
            (1.0 - weight_the) * weight_phi * jnp.take(lookup, base_index + 1, axis=1),
            weight_the * (1.0 - weight_phi) * jnp.take(lookup, base_index + n_cols, axis=1),
            weight_the * weight_phi * jnp.take(lookup, base_index + n_cols + 1, axis=1)]


def cycle_layout(n_rows, n_cols):
    all_cols = jnp.arange(n_cols + 4, dtype=jnp.int32)
    mid_rows = jnp.arange(n_rows, dtype=jnp.int32) + 2
    zero_row = jnp.zeros(n_cols + 4, jnp.int32)
    cycle_rows = jnp.concatenate([zero_row, zero_row + 1, zero_row + n_rows + 2, zero_row + n_rows + 3,
                                 jnp.repeat(mid_rows, 2), jnp.repeat(mid_rows, 2)])
    pair_cols = jnp.arange(2 * n_rows, dtype=jnp.int32) % 2
    cycle_cols = jnp.concatenate([all_cols, all_cols, all_cols, all_cols, pair_cols, pair_cols + n_cols + 2])
    return cycle_rows, cycle_cols


def assemble(halo_block, cycle_vals, first_row, first_col, n_theta, n_phi, spacings):
    shells = halo_block.shape[1]
    n_rows, n_cols = halo_block.shape[2] - 4, halo_block.shape[3] - 4
    cycle_rows, cycle_cols = cycle_layout(n_rows, n_cols)
    grid_row = first_row - 2 + cycle_rows
    grid_col = first_col - 2 + cycle_cols
    theta_cycle = angle_at(grid_row, 0.25 * math.pi, spacings[0])[None, :]
    phi_cycle = angle_at(grid_col, -0.75 * math.pi, spacings[1])[None, :]
    values = cycle_vals.reshape(8, shells, cycle_rows.shape[0])
    velocity = to_spherical(-values[2], values[4], values[3], theta_cycle, phi_cycle)
    magnet = to_spherical(-values[5], values[7], values[6], theta_cycle, phi_cycle)
    cycle_fields = jnp.stack([values[0], values[1], velocity[0], velocity[1], velocity[2],
                             magnet[0], magnet[1], magnet[2]])
    outside = (grid_row < 0) | (grid_row >= n_theta) | (grid_col < 0) | (grid_col >= n_phi)
    current = halo_block[:, :, cycle_rows, cycle_cols]
    return halo_block.at[:, :, cycle_rows, cycle_cols].set(jnp.where(outside, cycle_fields, current))


def reference(scalars, vectors, corner_rows, corner_cols, send_weights, recv_source):
    spacings = spacing(NT, NP)
    state_all = jnp.concatenate([scalars, vectors], axis=1)
    row_width = 8 * R
    zero_index = jnp.int32(0)

    def donate(panel_id, flat_block):
        lat_block = (flat_block // N_LON).astype(jnp.int32)
        lon_block = (flat_block % N_LON).astype(jnp.int32)
        own_state = lax.dynamic_slice(state_all[panel_id], (zero_index, zero_index, lat_block * CT, lon_block * CP), (8, R, CT, CP))
        lookup = donor_table(own_state, coordinate(lat_block * CT, CT, 0.25 * math.pi, spacings[0]),
                             coordinate(lon_block * CP, CP, -0.75 * math.pi, spacings[1]))
        corner_parts = corner_terms(lookup, corner_rows[lat_block, lon_block], corner_cols[lat_block, lon_block],
                                    send_weights[:, lat_block, lon_block], CP)
        summed = ((corner_parts[0] + corner_parts[1]) + corner_parts[2]) + corner_parts[3]
        return summed.reshape(row_width, N_LON, CAP)

    scalar_out = []
    vector_out = []
    for panel_id in range(2):
        donor_sends = lax.map(partial(donate, 1 - panel_id), jnp.arange(N_LAT * N_LON, dtype=jnp.int32))
        donor_sends = donor_sends.reshape(N_LAT, N_LON, row_width, N_LON, CAP)
        padded = jnp.pad(state_all[panel_id], ((0, 0), (0, 0), (2, 2), (2, 2)))

        def receive(flat_block, donor_sends=donor_sends, padded=padded, panel_id=panel_id):
            lat_block = (flat_block // N_LON).astype(jnp.int32)
            lon_block = (flat_block % N_LON).astype(jnp.int32)
            received = donor_sends[lat_block, :, :, lon_block]
            flat_rows = jnp.transpose(received, (1, 0, 2)).reshape(row_width, N_LON * CAP)
            picked = jnp.take(flat_rows, jnp.maximum(recv_source[lat_block, lon_block], 0).astype(jnp.int32), axis=1)
            halo_block = lax.dynamic_slice(padded, (zero_index, zero_index, lat_block * CT, lon_block * CP), (8, R, CT + 4, CP + 4))
            extended = assemble(halo_block, picked, lat_block * CT, lon_block * CP, NT, NP, spacings)
            theta_all = coordinate(lat_block * CT - 2, CT + 4, 0.25 * math.pi, spacings[0])
            phi_all = coordinate(lon_block * CP - 2, CP + 4, -0.75 * math.pi, spacings[1])
            return slab_rates(extended, theta_all, phi_all, float(panel_id), spacings)

        scalar_part, vector_part = lax.map(receive, jnp.arange(N_LAT * N_LON, dtype=jnp.int32))
        scalar_out.append(scalar_part.reshape(N_LAT, N_LON, 2, R, CT, CP).transpose(2, 3, 0, 4, 1, 5).reshape(2, R, NT, NP))
        vector_out.append(vector_part.reshape(N_LAT, N_LON, 6, R, CT, CP).transpose(2, 3, 0, 4, 1, 5).reshape(6, R, NT, NP))
    return jnp.stack(scalar_out), jnp.stack(vector_out)
```

```python
import math

import jax
import jax.numpy as jnp
import numpy as np
from jax import lax
from jax.experimental import pallas as pl
from jax.experimental.pallas import tpu as pltpu
from jax.sharding import PartitionSpec as P

GAMMA = 5.0 / 3.0
F32 = jnp.float32
BF16 = jnp.bfloat16
SH = 24
NR = 16
NC = 128
N_LAT = 8
N_LON = 16
CAP = 19
CHUNK = 32
EXT = NR + 4
ROW_SCALARS = 4

D_TH = 0.5 * math.pi / (NR * N_LAT)
D_PH = 1.5 * math.pi / (NC * N_LON)
D_R = 0.6 * D_TH
DT = 0.3 * min(D_R, 0.6 * math.sin(0.25 * math.pi - 2.0 * D_TH) * D_PH)
MU = DT / 0.9
GRAV = 0.036 / DT
OMEGA = 0.05 / DT


def theta_of(k):
    return 0.25 * math.pi + (k + 0.5) * D_TH


def phi_of(m):
    return -0.75 * math.pi + (m + 0.5) * D_PH


def radius_table():
    s = np.arange(SH, dtype=np.float64)
    r = 0.6 + (s + 0.5) * D_R
    ratio = np.ones(SH)
    ratio[0] = r[0] / (0.6 - 0.5 * D_R)
    ratio[-1] = r[-1] / (0.6 + (SH + 0.5) * D_R)
    cols = [1.0 / r, ratio, DT * GRAV / (r * r)]
    return np.concatenate([np.repeat(c[:, None], NC, 1) for c in cols], 0).astype(np.float32)


def row_table():
    out = np.zeros((N_LAT, EXT, ROW_SCALARS))
    for i in range(N_LAT):
        th = theta_of(i * NR - 2 + np.arange(EXT))
        out[i] = np.stack([np.sin(th), np.cos(th), np.cos(th) / np.sin(th), 1.0 / np.sin(th)], 1)
    return out.reshape(N_LAT, 1, EXT * ROW_SCALARS).astype(np.float32)


def lane_rows(shift):
    lane = (np.arange(NC) + shift) % NC
    return lane // 6, lane % 6


def theta_pack_table():
    out = np.zeros((N_LAT, 8, NC))
    for i in range(N_LAT):
        for side in range(2):
            r, _ = lane_rows(2 * side)
            th = theta_of(i * NR - 2 + np.minimum(r, EXT - 1))
            out[i, 4 * side : 4 * side + 4] = [
                np.sin(th),
                np.cos(th),
                np.cos(th) / np.sin(th),
                1.0 / np.sin(th),
            ]
    return out.astype(np.float32)


def phi_table():
    out = np.zeros((N_LON, 8, NC))
    for q in range(N_LON):
        ph = phi_of(q * NC + np.arange(NC))
        out[q, 0], out[q, 1] = np.sin(ph), np.cos(ph)
        for side in range(2):
            _, c = lane_rows(2 * side)
            ph = phi_of(q * NC + (c - 2 if side == 0 else c + NC - 4))
            out[q, 2 + 2 * side], out[q, 3 + 2 * side] = np.sin(ph), np.cos(ph)
    return out.astype(np.float32)


class Geo:
    def __init__(self, rad_ref, sin, cos, cot, isin, sphi, cphi, yang):
        self.rinv = rad_ref[0:SH, :]
        self.ratio = rad_ref[SH : 2 * SH, :]
        self.grav = rad_ref[2 * SH : 3 * SH, :]
        self.ct = self.rinv * (0.5 / D_TH)
        self.cp = self.rinv * (0.5 / D_PH) * isin
        self.cotr = self.rinv * cot
        self.n_r = (1.0 - yang) * cos + yang * (sin * sphi)
        self.n_t = (yang - 1.0) * sin + yang * (cos * sphi)
        self.n_p = yang * cphi


def lane_roll(x, shift):
    return pltpu.roll(x, shift % NC, 1)


def diff_p(x):
    return lane_roll(x, -1) - lane_roll(x, 1)


def diff_r(x, ghost, edges):
    first, last = edges
    return jnp.where(last, ghost, pltpu.roll(x, SH - 1, 0)) - jnp.where(
        first, ghost, pltpu.roll(x, 1, 0)
    )


def cross(a, b):
    return (
        a[1] * b[2] - a[2] * b[1],
        a[2] * b[0] - a[0] * b[2],
        a[0] * b[1] - a[1] * b[0],
    )


def stage_one(u, diff_t, geo, edges, full):
    rinv, ct, cp, cotr = geo.rinv, geo.ct, geo.cp, geo.cotr
    cr = 0.5 / D_R
    rho, pr = u[0], u[1]
    v, b = u[2:5], u[5:8]

    def d_r(x):
        return diff_r(x, x, edges) * cr

    def d_t(fn):
        return diff_t(fn) * ct

    def d_p(x):
        return diff_p(x) * cp

    bt_r, bp_r = d_r(b[1]), d_r(b[2])
    j_r = d_t(lambda w: w[7]) + b[2] * cotr - d_p(b[1])
    jt_ang = d_p(b[0]) - b[2] * rinv
    jp_ang = b[1] * rinv - d_t(lambda w: w[5])
    jj = (j_r, jt_ang - bp_r, bt_r + jp_ang)
    vr = [d_r(x) for x in v]
    vt = [d_t(lambda w, i=i: w[2 + i]) for i in range(3)]
    vp = [d_p(x) for x in v]
    wt_ang = vp[0] - v[2] * rinv
    wp_ang = v[1] * rinv - vt[0]
    ww = (vt[2] + v[2] * cotr - vp[1], wt_ang - vr[2], vr[1] + wp_ang)
    e_ang = 2.0 * v[0] * rinv + vt[1] + v[1] * cotr + vp[2]
    ee = vr[0] + e_ang
    vxb = cross(v, b)
    el = [vxb[i] - MU * jj[i] for i in range(3)]
    ratio = geo.ratio
    level = list(ww) + [ee] + el
    level += [
        wt_ang * ratio,
        wp_ang * ratio,
        e_ang * ratio,
        vxb[1] - MU * (jt_ang * ratio),
        vxb[2] - MU * (jp_ang * ratio),
    ]
    if not full:
        return level, None, None
    fr, fp = rho * v[0], rho * v[2]
    mass = (
        d_r(fr)
        + 2.0 * fr * rinv
        + d_t(lambda w: w[0] * w[3])
        + rho * v[1] * cotr
        + d_p(fp)
    )
    gp = (d_r(pr), d_t(lambda w: w[1]), d_p(pr))
    press = -(v[0] * gp[0] + v[1] * gp[1] + v[2] * gp[2]) - GAMMA * pr * ee
    lor = cross(jj, b)
    spin = cross(v, (geo.n_r, geo.n_t, geo.n_p))
    curv = (
        -(v[1] * v[1] + v[2] * v[2]) * rinv,
        v[0] * v[1] * rinv - v[2] * v[2] * cotr,
        v[0] * v[2] * rinv + v[1] * v[2] * cotr,
    )
    irho = DT / rho
    rest = []
    for i in range(3):
        adv = v[0] * vr[i] + v[1] * vt[i] + v[2] * vp[i] + curv[i]
        x = (lor[i] - gp[i]) * irho - DT * adv + (2.0 * OMEGA * DT) * spin[i]
        rest.append(x - geo.grav if i == 0 else x)
    rest.append(irho * MU)
    return level, rest, (-DT * mass, DT * press)


def stage_two(q, diff_t, rest, geo, edges):
    rinv, ct, cp, cotr = geo.rinv, geo.ct, geo.cp, geo.cotr
    cr = 0.5 / D_R

    def d_r(i, g):
        return diff_r(q[i], q[g], edges) * cr

    def d_t(i):
        return diff_t(i) * ct

    def d_p(i):
        return diff_p(q[i]) * cp

    def curl(o, gt, gp):
        return (
            d_t(o + 2) + q[o + 2] * cotr - d_p(o + 1),
            d_p(o) - d_r(o + 2, gp) - q[o + 2] * rinv,
            d_r(o + 1, gt) + q[o + 1] * rinv - d_t(o),
        )

    cw = curl(0, 7, 8)
    grad_e = (d_r(3, 9), d_t(3), d_p(3))
    ce = curl(4, 10, 11)
    acc = [rest[i] + rest[3] * (4.0 / 3.0 * grad_e[i] - cw[i]) for i in range(3)]
    return acc + [DT * ce[i] for i in range(3)]


def shell_edges():
    s = lax.broadcasted_iota(jnp.int32, (SH, NC), 0)
    return s == 0, s == SH - 1


def load_row(sc_ref, ve_ref, f, k):
    ref, g = (sc_ref, f) if f < 2 else (ve_ref, f - 2)
    return ref[pl.ds(g * (SH * NR) + k, SH, stride=NR), :]


def store_row(sc_ref, ve_ref, f, k, val):
    ref, g = (sc_ref, f) if f < 2 else (ve_ref, f - 2)
    ref[pl.ds(g * (SH * NR) + k, SH, stride=NR), :] = val


def aligned(i):
    return i if isinstance(i, int) else pl.multiple_of(i, 8)


def tile(ref, i):
    return ref[pl.ds(aligned(i * SH), SH), :]


def put(ref, i, val):
    ref[pl.ds(aligned(i * SH), SH), :] = val


def row_geo(rad_ref, rows_ref, phi_ref, e, yang):
    sc = [rows_ref[0, e * ROW_SCALARS + j] for j in range(ROW_SCALARS)]
    return Geo(rad_ref, sc[0], sc[1], sc[2], sc[3], phi_ref[0:1, :], phi_ref[1:2, :], yang)


def rows_one(u_ref, q_ref, r_ref, depth, geo, edges, slot, full):
    def fields(at):
        return [tile(u_ref, f * depth + at) for f in range(8)]

    up, dn = fields(slot + 1), fields(slot - 1)
    level, rest, scal = stage_one(
        fields(slot), lambda fn: fn(up) - fn(dn), geo, edges, full
    )
    for i, x in enumerate(level):
        put(q_ref, i * depth + slot, x)
    if full:
        for i, x in enumerate(rest):
            put(r_ref, i * depth + slot, x)
    return scal


def rows_two(q_ref, r_ref, depth, geo, edges, slot):
    q = [tile(q_ref, i * depth + slot) for i in range(12)]

    def diff_t(i):
        return tile(q_ref, i * depth + slot + 1) - tile(q_ref, i * depth + slot - 1)

    rest = [tile(r_ref, i * depth + slot) for i in range(4)]
    return stage_two(q, diff_t, rest, geo, edges)


def donor_kernel(sc_ref, ve_ref, tab_ref, rows_ref, phi_ref, pay_ref, up_ref, dn_ref,
                 s_hi, s_lo, c_hi, c_lo):
    sphi, cphi = phi_ref[0:1, :], phi_ref[1:2, :]
    for k in range(NR):
        u = [load_row(sc_ref, ve_ref, f, k) for f in range(8)]
        for rows, ref in (((0, 1), dn_ref), ((NR - 2, NR - 1), up_ref)):
            if k in rows:
                for f in range(8):
                    put(ref, f * 2 + k - rows[0], u[f])
        sin = rows_ref[0, (k + 2) * ROW_SCALARS]
        cos = rows_ref[0, (k + 2) * ROW_SCALARS + 1]
        c = [u[0], u[1]]
        for o in (2, 5):
            flat = u[o] * sin + u[o + 1] * cos
            c += [
                flat * cphi - u[o + 2] * sphi,
                flat * sphi + u[o + 2] * cphi,
                u[o] * cos - u[o + 1] * sin,
            ]
        c = jnp.concatenate(c, axis=0)
        hi = c.astype(BF16)
        c_hi[:, k * NC : (k + 1) * NC] = hi
        c_lo[:, k * NC : (k + 1) * NC] = (c - hi.astype(F32)).astype(BF16)
    cols = jnp.transpose(tab_ref[...])
    lane = lax.broadcasted_iota(jnp.int32, (48, NC), 1).astype(F32)
    for pair in range(N_LON // 2):
        a, b, wt, wp = [
            jnp.concatenate(
                [
                    jnp.broadcast_to(cols[0:24, o : o + 1], (24, NC))
                    for o in (j * N_LON + 2 * pair, j * N_LON + 2 * pair + 1)
                ],
                axis=0,
            )
            for j in range(4)
        ]
        along = jnp.where(lane == b, 1.0 - wp, jnp.where(lane == b + 1.0, wp, 0.0))
        first, second = along * (1.0 - wt), along * wt
        for k in range(NR):
            s = jnp.where(a == float(k), first, jnp.where(a == float(k - 1), second, 0.0))
            hi = s.astype(BF16)
            s_hi[48 * pair : 48 * pair + 48, k * NC : (k + 1) * NC] = hi
            s_lo[48 * pair : 48 * pair + 48, k * NC : (k + 1) * NC] = (
                s - hi.astype(F32)
            ).astype(BF16)

    def dot(x, y):
        return lax.dot_general(
            x[...], y[...], (((1,), (1,)), ((), ())), preferred_element_type=F32
        )

    sent = dot(s_hi, c_hi) + dot(s_hi, c_lo) + dot(s_lo, c_hi)
    for t in range(N_LON):
        pay_ref[t, 0:24, :] = sent[24 * t : 24 * t + 24, 0:NC]
        part = sent[24 * t : 24 * t + 24, NC : NC + 64]
        pay_ref[t, 24:32, :] = jnp.zeros((8, NC), F32)
        pay_ref[t, 19:29, 0:64] = part[0:10]
        pay_ref[t, 19:28, 64:128] = part[10:19]


def pack_kernel(sc_ref, ve_ref, top_ref, bot_ref, left_ref, right_ref):
    lane = lax.broadcasted_iota(jnp.int32, (SH, NC), 1)
    for f in range(8):
        left = jnp.zeros((SH, NC), F32)
        right = jnp.zeros((SH, NC), F32)
        for e in range(EXT):
            if e < 2:
                x = tile(top_ref, f * 2 + e)
            elif e >= NR + 2:
                x = tile(bot_ref, f * 2 + e - NR - 2)
            else:
                x = load_row(sc_ref, ve_ref, f, e - 2)
            x = lane_roll(x, 6 * e + 2)
            base = 6 * e
            left = jnp.where((lane >= base + 2) & (lane < base + 6), x, left)
            if e == 0:
                right = jnp.where((lane >= NC - 2) | (lane < 2), x, right)
            else:
                right = jnp.where((lane >= base - 2) & (lane < base + 2), x, right)
        put(left_ref, f, left)
        put(right_ref, f, right)


def main_kernel(sc_ref, ve_ref, top_ref, bot_ref, rad_ref, rows_ref, phi_ref, osc_ref, ove_ref,
                u_ref, q_ref, r_ref):
    yang = lax.axis_index("panel").astype(F32)
    edges = shell_edges()
    for f in range(8):
        for e in range(EXT):
            if e < 2:
                x = tile(top_ref, f * 2 + e)
            elif e >= NR + 2:
                x = tile(bot_ref, f * 2 + e - NR - 2)
            else:
                x = load_row(sc_ref, ve_ref, f, e - 2)
            put(u_ref, f * EXT + e, x)

    def one(e, full):
        geo = row_geo(rad_ref, rows_ref, phi_ref, e, yang)
        return rows_one(u_ref, q_ref, r_ref, EXT, geo, edges, e, full)

    one(1, False)
    one(NR + 2, False)

    @pl.loop(2, NR + 2)
    def _(e):
        scal = one(e, True)
        for i in range(2):
            store_row(osc_ref, ove_ref, i, e - 2, scal[i])

    @pl.loop(2, NR + 2)
    def _(e):
        geo = row_geo(rad_ref, rows_ref, phi_ref, e, yang)
        vec = rows_two(q_ref, r_ref, EXT, geo, edges, e)
        for i in range(6):
            store_row(osc_ref, ove_ref, 2 + i, e - 2, vec[i])


def to_spherical(x, y, z, sin, cos, sphi, cphi):
    flat = x * cphi + y * sphi
    return [flat * sin + z * cos, flat * cos - z * sin, y * cphi - x * sphi]


def border_fields(w, sin, cos, sphi, cphi):
    out = [w[0], w[1]]
    for o in (2, 5):
        out += to_spherical(-w[o], w[o + 2], w[o + 1], sin, cos, sphi, cphi)
    return out


STRIP = 6


def edge_kernel(sc_ref, ve_ref, top_ref, bot_ref, left_ref, right_ref, fromleft_ref, fromright_ref,
                don_ref, idx_ref, rad_ref, rows_ref, thp_ref, phi_ref, isc_ref, ive_ref,
                osc_ref, ove_ref, bord_ref, u_ref, q_ref, r_ref):
    yang = lax.axis_index("panel").astype(F32)
    lat = lax.axis_index("lat")
    lon = lax.axis_index("lon")
    edges = shell_edges()
    row_edge = (lat == 0) | (lat == N_LAT - 1)
    col_edge = (lon == 0) | (lon == N_LON - 1)
    wide = 4 * NC

    @pl.when(row_edge | col_edge)
    def _():
        recv = jnp.transpose(don_ref[...])
        hi = recv.astype(BF16)
        lo = (recv - hi.astype(F32)).astype(BF16)
        g = idx_ref[0:1, :]
        donor, slot = idx_ref[1:2, :], idx_ref[2:3, :]
        at = lax.broadcasted_iota(jnp.int32, (N_LON * CHUNK, wide), 0)
        here = jnp.where(g >= 0, donor * CHUNK + slot, -1)
        low = jnp.where((g >= 0) & (slot < 10), donor * CHUNK + 19 + slot, -1)
        high = jnp.where((g >= 0) & (slot >= 10), donor * CHUNK + 9 + slot, -1)

        def pick(where, lo_row, hi_row):
            hot = jnp.where(at == where, 1.0, 0.0).astype(BF16)
            return jnp.dot(hi[lo_row:hi_row], hot, preferred_element_type=F32) + jnp.dot(
                lo[lo_row:hi_row], hot, preferred_element_type=F32
            )

        bord_ref[0:NC, :] = pick(here, 0, NC)
        bord_ref[NC : NC + 64, :] = pick(low, 0, 64) + pick(high, 64, NC)

    def border(col, sin, cos, sphi, cphi):
        w = [bord_ref[f * SH : f * SH + SH, col * NC : (col + 1) * NC] for f in range(8)]
        return border_fields(w, sin, cos, sphi, cphi)

    def scalars_at(e):
        return [rows_ref[0, e * ROW_SCALARS + j] for j in range(ROW_SCALARS)]

    lane = lax.broadcasted_iota(jnp.int32, (SH, NC), 1)
    place = lane % 6
    merged = None
    for side in range(2):
        own_ref, other_ref = (
            (left_ref, fromleft_ref) if side == 0 else (right_ref, fromright_ref)
        )
        theirs = (place < 2) if side == 0 else ((place == 2) | (place == 3))
        th = [thp_ref[4 * side + j : 4 * side + j + 1, :] for j in range(4)]
        ph = [phi_ref[2 + 2 * side + j : 3 + 2 * side + j, :] for j in range(2)]
        g = jnp.broadcast_to(idx_ref[0:1, (2 + side) * NC : (3 + side) * NC], (SH, NC))
        donated = border(2 + side, th[0], th[1], ph[0], ph[1])
        u = []
        for f in range(8):
            x = jnp.where(theirs, tile(other_ref, f), tile(own_ref, f))
            u.append(jnp.where(g >= 0, donated[f], x))
        geo = Geo(rad_ref, th[0], th[1], th[2], th[3], ph[0], ph[1], yang)

        def diff_six(x):
            return lane_roll(x, -6) - lane_roll(x, 6)

        level, rest, scal = stage_one(u, lambda fn: diff_six(fn(u)), geo, edges, True)
        vec = stage_two(level, lambda i: diff_six(level[i]), rest, geo, edges)
        vals = list(scal) + vec
        if side == 0:
            merged = vals
        else:
            merged = [jnp.where(place < 2, y, x) for x, y in zip(merged, vals)]
    edge_lane = (lane < 2) | (lane >= NC - 2)
    for f in range(8):
        for k in range(NR):
            x = lane_roll(merged[f], -(6 * (k + 2) + 2))
            old = load_row(isc_ref, ive_ref, f, k)
            store_row(osc_ref, ove_ref, f, k, jnp.where(edge_lane, x, old))

    def merge_row(f, k, val):
        old = load_row(osc_ref, ove_ref, f, k)
        store_row(osc_ref, ove_ref, f, k, jnp.where(edge_lane, old, val))

    @pl.when(row_edge)
    def _():
        top = lat == 0
        e0 = jnp.where(top, 0, NR - 2)
        for i in range(2):
            sc = scalars_at(jnp.where(top, i, NR + 2 + i))
            w = border(i, sc[0], sc[1], phi_ref[0:1, :], phi_ref[1:2, :])
            for f in range(8):
                put(u_ref, f * STRIP + jnp.where(top, i, 4 + i), w[f])
        for j in range(4):
            for f in range(8):
                x = load_row(sc_ref, ve_ref, f, jnp.where(top, j, NR - 4 + j))
                put(u_ref, f * STRIP + jnp.where(top, 2 + j, j), x)

        def geo_at(slot):
            return row_geo(rad_ref, rows_ref, phi_ref, e0 + slot, yang)

        for slot in (1, 2, 3, 4):
            full = slot in (2, 3)
            scal = rows_one(u_ref, q_ref, r_ref, STRIP, geo_at(slot), edges, slot, full)
            if full:
                for i in range(2):
                    merge_row(i, e0 + slot - 2, scal[i])
        for slot in (2, 3):
            vec = rows_two(q_ref, r_ref, STRIP, geo_at(slot), edges, slot)
            for i in range(6):
                merge_row(2 + i, e0 + slot - 2, vec[i])


VM = pl.BlockSpec(memory_space=pltpu.VMEM)
SM = pl.BlockSpec(memory_space=pltpu.SMEM)


def call(kernel, n_in, smem, outs, scratch, name, flops, aliases=None):
    return pl.pallas_call(
        kernel,
        out_shape=[jax.ShapeDtypeStruct(s, F32) for s in outs],
        in_specs=[SM if i in smem else VM for i in range(n_in)],
        out_specs=[VM] * len(outs),
        scratch_shapes=scratch,
        input_output_aliases=aliases or {},
        name=name,
        compiler_params=pltpu.CompilerParams(vmem_limit_bytes=48 * 1024 * 1024),
        cost_estimate=pl.CostEstimate(flops=flops, bytes_accessed=3000000, transcendentals=0),
    )


def shifted(x, axis, step):
    n = lax.axis_size(axis)
    return lax.ppermute(x, axis, [(i, (i + step) % n) for i in range(n)])


def frame_places(recv, lat):
    top = jnp.stack([recv[2 : NC + 2], recv[NC + 6 : 2 * NC + 6]])
    at = 2 * (NC + 4)
    bottom = jnp.stack([recv[at + 2 : at + NC + 2], recv[at + NC + 6 : at + 2 * NC + 6]])
    strip = jnp.where(lat == 0, top, bottom)
    mid = 4 * (NC + 4)
    rows = [recv[i * (NC + 4) : (i + 1) * (NC + 4)] for i in range(4)]

    def side(cut, sides, pad):
        body = jnp.pad(sides.reshape(NR, 2), ((0, 0), pad), constant_values=-1)
        edge = jnp.stack([r[cut] for r in rows])
        return jnp.concatenate([edge[:2], body, edge[2:]]).reshape(-1)

    left = side(slice(0, 6), recv[mid : mid + 2 * NR], (0, 4))
    right = side(slice(NC - 2, NC + 4), recv[mid + 2 * NR : mid + 4 * NR], (4, 0))
    none = jnp.full((NC - 6 * EXT,), -1, jnp.int32)
    left = jnp.concatenate([left, none])
    right = jnp.concatenate([right[2:], none, right[:2]])
    g = jnp.concatenate([strip.reshape(-1), left, right])
    return jnp.pad(jnp.stack([g, g // CAP, g % CAP]), ((0, 5), (0, 0)))


def body(scalars, vectors, corner_rows, corner_cols, send_weights, recv_source):
    lat, lon = lax.axis_index("lat"), lax.axis_index("lon")
    sc = scalars.reshape(2 * SH * NR, NC)
    ve = vectors.reshape(6 * SH * NR, NC)
    rad = jnp.asarray(radius_table())
    rows = lax.dynamic_index_in_dim(jnp.asarray(row_table()), lat, 0, False)
    thp = lax.dynamic_index_in_dim(jnp.asarray(theta_pack_table()), lat, 0, False)
    phi = lax.dynamic_index_in_dim(jnp.asarray(phi_table()), lon, 0, False)
    tab = jnp.concatenate(
        [
            corner_rows[0, 0].astype(F32),
            corner_cols[0, 0].astype(F32),
            send_weights[0, 0, 0],
            send_weights[1, 0, 0],
        ]
    )
    tab = jnp.pad(tab, ((0, NC - 4 * N_LON), (0, NC - CAP)))
    halo = (8 * 2 * SH, NC)
    pack = (8 * SH, NC)

    pay, up, dn = call(
        donor_kernel, 5, (3,), [(N_LON, CHUNK, NC), halo, halo],
        [
            pltpu.VMEM((24 * N_LON, NR * NC), BF16),
            pltpu.VMEM((24 * N_LON, NR * NC), BF16),
            pltpu.VMEM((8 * SH, NR * NC), BF16),
            pltpu.VMEM((8 * SH, NR * NC), BF16),
        ],
        "donor", 400000000,
    )(sc, ve, tab, rows, phi)
    pay = lax.ppermute(pay, "panel", [(0, 1), (1, 0)])
    don = lax.all_to_all(pay, "lon", 0, 0, tiled=True).reshape(N_LON * CHUNK, NC)
    top = shifted(up, "lat", 1)
    bot = shifted(dn, "lat", -1)
    left, right = call(pack_kernel, 4, (), [pack, pack], [], "packs", 1000000)(sc, ve, top, bot)
    from_left = shifted(right, "lon", 1)
    from_right = shifted(left, "lon", -1)
    osc, ove = call(
        main_kernel, 7, (5,), [sc.shape, ve.shape],
        [
            pltpu.VMEM((8 * EXT * SH, NC), F32),
            pltpu.VMEM((12 * EXT * SH, NC), F32),
            pltpu.VMEM((4 * EXT * SH, NC), F32),
        ],
        "interior", 30000000,
    )(sc, ve, top, bot, rad, rows, phi)
    osc, ove = call(
        edge_kernel, 16, (11,), [sc.shape, ve.shape],
        [
            pltpu.VMEM((8 * SH, 4 * NC), F32),
            pltpu.VMEM((8 * STRIP * SH, NC), F32),
            pltpu.VMEM((12 * STRIP * SH, NC), F32),
            pltpu.VMEM((4 * STRIP * SH, NC), F32),
        ],
        "edges", 10000000,
    )(sc, ve, top, bot, left, right, from_left, from_right, don,
      frame_places(recv_source[0, 0], lat), rad, rows, thp, phi, osc, ove)
    return osc.reshape(scalars.shape), ove.reshape(vectors.shape)


def solution(mesh):
    return jax.shard_map(
        body,
        mesh=mesh,
        in_specs=(
            P("panel", None, None, "lat", "lon"),
            P("panel", None, None, "lat", "lon"),
            P("lat", "lon", None, None),
            P("lat", "lon", None, None),
            P(None, "lat", "lon", None, None),
            P("lat", "lon", None),
        ),
        out_specs=(P("panel", None, None, "lat", "lon"), P("panel", None, None, "lat", "lon")),
        check_vma=False,
    )
```

```python
import math

import jax
import jax.numpy as jnp
import numpy as np
from jax import lax
from jax.experimental import pallas as pl
from jax.experimental.pallas import tpu as pltpu
from jax.sharding import PartitionSpec as P

GAMMA = 5.0 / 3.0
F32 = jnp.float32
BF16 = jnp.bfloat16
SH = 24
NR = 16
NC = 128
N_LAT = 8
N_LON = 16
CAP = 19
CHUNK = 32
EXT = NR + 4
ROW_SCALARS = 4

D_TH = 0.5 * math.pi / (NR * N_LAT)
D_PH = 1.5 * math.pi / (NC * N_LON)
D_R = 0.6 * D_TH
DT = 0.3 * min(D_R, 0.6 * math.sin(0.25 * math.pi - 2.0 * D_TH) * D_PH)
MU = DT / 0.9
GRAV = 0.036 / DT
OMEGA = 0.05 / DT


def theta_of(k):
    return 0.25 * math.pi + (k + 0.5) * D_TH


def phi_of(m):
    return -0.75 * math.pi + (m + 0.5) * D_PH


def lane_rows(shift):
    lane = (np.arange(NC) + shift) % NC
    return lane // 6, lane % 6


G_ROWS = 0
G_RAD = EXT * ROW_SCALARS
G_PACK = G_RAD + 3 * SH
G_FRAME = G_PACK + 8
G_PHI = G_FRAME + 16
G_ALL = G_PHI + 8


def frame_table(i):
    wide = NC + 4
    at = np.full((4, NC), -1)
    row = 0 if i == 0 else 2
    for j in range(2):
        at[j] = (row + j) * wide + 2 + np.arange(NC)
    for side in range(2):
        r, c = lane_rows(2 * side)
        for lane in range(NC):
            col = c[lane] if side == 0 else NC - 2 + c[lane]
            if r[lane] in (0, 1):
                at[2 + side, lane] = r[lane] * wide + col
            elif r[lane] in (EXT - 2, EXT - 1):
                at[2 + side, lane] = (r[lane] - NR) * wide + col
            elif r[lane] < EXT and side == 0 and c[lane] < 2:
                at[2, lane] = 4 * wide + 2 * (r[lane] - 2) + c[lane]
            elif r[lane] < EXT and side == 1 and c[lane] >= 4:
                at[3, lane] = 4 * wide + 2 * NR + 2 * (r[lane] - 2) + c[lane] - 4
    out = np.zeros((16, NC))
    out[8:] = -1
    out[0:4] = np.where(at >= 0, at % NC, 0)
    out[8:12] = np.where(at >= 0, at // NC, -1)
    return out


def lat_table():
    out = np.zeros((N_LAT, G_PHI, NC))
    s = np.arange(SH, dtype=np.float64)
    r = 0.6 + (s + 0.5) * D_R
    ratio = np.ones(SH)
    ratio[0] = r[0] / (0.6 - 0.5 * D_R)
    ratio[-1] = r[-1] / (0.6 + (SH + 0.5) * D_R)
    out[:, G_RAD:G_PACK] = np.concatenate([1.0 / r, ratio, DT * GRAV / (r * r)])[:, None]

    def four(th):
        return np.stack([np.sin(th), np.cos(th), np.cos(th) / np.sin(th), 1.0 / np.sin(th)])

    for i in range(N_LAT):
        th = theta_of(i * NR - 2 + np.arange(EXT))
        out[i, G_ROWS:G_RAD] = four(th).T.reshape(-1)[:, None]
        for side in range(2):
            rr, _ = lane_rows(2 * side)
            at = G_PACK + 4 * side
            out[i, at : at + 4] = four(theta_of(i * NR - 2 + np.minimum(rr, EXT - 1)))
        out[i, G_FRAME:G_PHI] = frame_table(i)
    return out.astype(np.float32)


def lon_table():
    out = np.zeros((N_LON, 8, NC))
    for q in range(N_LON):
        ph = phi_of(q * NC + np.arange(NC))
        out[q, 0], out[q, 1] = np.sin(ph), np.cos(ph)
        for side in range(2):
            _, c = lane_rows(2 * side)
            ph = phi_of(q * NC + (c - 2 if side == 0 else c + NC - 4))
            out[q, 2 + 2 * side], out[q, 3 + 2 * side] = np.sin(ph), np.cos(ph)
    return out.astype(np.float32)


class Geo:
    def __init__(self, geo_ref, sin, cos, cot, isin, sphi, cphi, yang):
        self.rinv = geo_ref[G_RAD : G_RAD + SH, :]
        self.ratio = geo_ref[G_RAD + SH : G_RAD + 2 * SH, :]
        self.grav = geo_ref[G_RAD + 2 * SH : G_RAD + 3 * SH, :]
        self.ct = self.rinv * (0.5 / D_TH)
        self.cp = self.rinv * (0.5 / D_PH) * isin
        self.cotr = self.rinv * cot
        self.n_r = (1.0 - yang) * cos + yang * (sin * sphi)
        self.n_t = (yang - 1.0) * sin + yang * (cos * sphi)
        self.n_p = yang * cphi


def lane_roll(x, shift):
    return pltpu.roll(x, shift % NC, 1)


def diff_p(x):
    return lane_roll(x, -1) - lane_roll(x, 1)


def diff_r(x, ghost, edges):
    first, last = edges
    return jnp.where(last, ghost, pltpu.roll(x, SH - 1, 0)) - jnp.where(
        first, ghost, pltpu.roll(x, 1, 0)
    )


def cross(a, b):
    return (
        a[1] * b[2] - a[2] * b[1],
        a[2] * b[0] - a[0] * b[2],
        a[0] * b[1] - a[1] * b[0],
    )


def stage_one(u, diff_t, geo, edges, full):
    rinv, ct, cp, cotr = geo.rinv, geo.ct, geo.cp, geo.cotr
    cr = 0.5 / D_R
    rho, pr = u[0], u[1]
    v, b = u[2:5], u[5:8]

    def d_r(x):
        return diff_r(x, x, edges) * cr

    def d_t(fn):
        return diff_t(fn) * ct

    def d_p(x):
        return diff_p(x) * cp

    bt_r, bp_r = d_r(b[1]), d_r(b[2])
    j_r = d_t(lambda w: w[7]) + b[2] * cotr - d_p(b[1])
    jt_ang = d_p(b[0]) - b[2] * rinv
    jp_ang = b[1] * rinv - d_t(lambda w: w[5])
    jj = (j_r, jt_ang - bp_r, bt_r + jp_ang)
    vr = [d_r(x) for x in v]
    vt = [d_t(lambda w, i=i: w[2 + i]) for i in range(3)]
    vp = [d_p(x) for x in v]
    wt_ang = vp[0] - v[2] * rinv
    wp_ang = v[1] * rinv - vt[0]
    ww = (vt[2] + v[2] * cotr - vp[1], wt_ang - vr[2], vr[1] + wp_ang)
    e_ang = 2.0 * v[0] * rinv + vt[1] + v[1] * cotr + vp[2]
    ee = vr[0] + e_ang
    vxb = cross(v, b)
    el = [vxb[i] - MU * jj[i] for i in range(3)]
    ratio = geo.ratio
    level = list(ww) + [ee] + el
    level += [
        wt_ang * ratio,
        wp_ang * ratio,
        e_ang * ratio,
        vxb[1] - MU * (jt_ang * ratio),
        vxb[2] - MU * (jp_ang * ratio),
    ]
    if not full:
        return level, None, None
    fr, fp = rho * v[0], rho * v[2]
    mass = (
        d_r(fr)
        + 2.0 * fr * rinv
        + d_t(lambda w: w[0] * w[3])
        + rho * v[1] * cotr
        + d_p(fp)
    )
    gp = (d_r(pr), d_t(lambda w: w[1]), d_p(pr))
    press = -(v[0] * gp[0] + v[1] * gp[1] + v[2] * gp[2]) - GAMMA * pr * ee
    lor = cross(jj, b)
    spin = cross(v, (geo.n_r, geo.n_t, geo.n_p))
    curv = (
        -(v[1] * v[1] + v[2] * v[2]) * rinv,
        v[0] * v[1] * rinv - v[2] * v[2] * cotr,
        v[0] * v[2] * rinv + v[1] * v[2] * cotr,
    )
    irho = DT / rho
    rest = []
    for i in range(3):
        adv = v[0] * vr[i] + v[1] * vt[i] + v[2] * vp[i] + curv[i]
        x = (lor[i] - gp[i]) * irho - DT * adv + (2.0 * OMEGA * DT) * spin[i]
        rest.append(x - geo.grav if i == 0 else x)
    rest.append(irho * MU)
    return level, rest, (-DT * mass, DT * press)


def stage_two(q, diff_t, rest, geo, edges):
    rinv, ct, cp, cotr = geo.rinv, geo.ct, geo.cp, geo.cotr
    cr = 0.5 / D_R

    def d_r(i, g):
        return diff_r(q[i], q[g], edges) * cr

    def d_t(i):
        return diff_t(i) * ct

    def d_p(i):
        return diff_p(q[i]) * cp

    def curl(o, gt, gp):
        return (
            d_t(o + 2) + q[o + 2] * cotr - d_p(o + 1),
            d_p(o) - d_r(o + 2, gp) - q[o + 2] * rinv,
            d_r(o + 1, gt) + q[o + 1] * rinv - d_t(o),
        )

    cw = curl(0, 7, 8)
    grad_e = (d_r(3, 9), d_t(3), d_p(3))
    ce = curl(4, 10, 11)
    acc = [rest[i] + rest[3] * (4.0 / 3.0 * grad_e[i] - cw[i]) for i in range(3)]
    return acc + [DT * ce[i] for i in range(3)]


def shell_edges():
    s = lax.broadcasted_iota(jnp.int32, (SH, NC), 0)
    return s == 0, s == SH - 1


def aligned(i):
    return i if isinstance(i, int) else pl.multiple_of(i, 8)


def tile(ref, i):
    return ref[pl.ds(aligned(i * SH), SH), :]


def put(ref, i, val):
    ref[pl.ds(aligned(i * SH), SH), :] = val


def row_values(geo_ref, e):
    return [geo_ref[pl.ds(e * ROW_SCALARS + j, 1), :] for j in range(ROW_SCALARS)]


def row_geo(geo_ref, e, yang):
    return Geo(
        geo_ref, *row_values(geo_ref, e), geo_ref[G_PHI : G_PHI + 1, :],
        geo_ref[G_PHI + 1 : G_PHI + 2, :], yang,
    )


def rows_one(fields, q_ref, r_ref, depth, geo, edges, slot, full):
    up, dn = fields(1), fields(-1)
    level, rest, scal = stage_one(fields(0), lambda fn: fn(up) - fn(dn), geo, edges, full)
    for i, x in enumerate(level):
        put(q_ref, i * depth + slot, x)
    if full:
        for i, x in enumerate(rest):
            put(r_ref, i * depth + slot, x)
    return scal


def rows_two(q_ref, r_ref, depth, geo, edges, slot):
    q = [tile(q_ref, i * depth + slot) for i in range(12)]

    def diff_t(i):
        return tile(q_ref, i * depth + slot + 1) - tile(q_ref, i * depth + slot - 1)

    rest = [tile(r_ref, i * depth + slot) for i in range(4)]
    return stage_two(q, diff_t, rest, geo, edges)


def native_row(f, k):
    return pl.ds(f * (SH * NR) + k, SH, stride=NR)


def donor_kernel(sc_hbm, ve_hbm, cr_hbm, cc_hbm, sw_hbm, rs_hbm, lat_hbm, lon_hbm,
                 pay_ref, up_ref, dn_ref, own_ref, geo_ref, idx_ref,
                 blk, cr, cc, sw, rs, tab, s_hi, s_lo, c_hi, c_lo, sems):
    lat, lon = lax.axis_index("lat"), lax.axis_index("lon")
    n_sc = 2 * SH * NR
    moves = [
        (cr_hbm.at[0, 0], cr),
        (cc_hbm.at[0, 0], cc),
        (sw_hbm.at[:, 0, 0], sw),
        (rs_hbm, rs),
        (lat_hbm.at[lat], geo_ref.at[0:G_PHI]),
        (lon_hbm.at[lon], geo_ref.at[G_PHI:G_ALL]),
        (sc_hbm, blk.at[0:n_sc]),
        (ve_hbm, blk.at[n_sc : 4 * n_sc]),
    ]
    copies = [pltpu.make_async_copy(a, b, sems.at[i]) for i, (a, b) in enumerate(moves)]
    for c in copies:
        c.start()
    tab[...] = jnp.zeros((NC, NC), F32)
    for c in copies[:3]:
        c.wait()
    tab[0:16, 0:CAP] = cr[...].astype(F32)
    tab[16:32, 0:CAP] = cc[...].astype(F32)
    tab[32:48, 0:CAP] = sw[0]
    tab[48:64, 0:CAP] = sw[1]
    cols = jnp.transpose(tab[...])
    lane = lax.broadcasted_iota(jnp.int32, (48, NC), 1).astype(F32)
    for pair in range(N_LON // 2):
        a, b, wt, wp = [
            jnp.concatenate(
                [
                    jnp.broadcast_to(cols[0:24, o : o + 1], (24, NC))
                    for o in (j * N_LON + 2 * pair, j * N_LON + 2 * pair + 1)
                ],
                axis=0,
            )
            for j in range(4)
        ]
        along = jnp.where(lane == b, 1.0 - wp, jnp.where(lane == b + 1.0, wp, 0.0))
        first, second = along * (1.0 - wt), along * wt
        for k in range(NR):
            s = jnp.where(a == float(k), first, jnp.where(a == float(k - 1), second, 0.0))
            hi = s.astype(BF16)
            s_hi[48 * pair : 48 * pair + 48, k * NC : (k + 1) * NC] = hi
            s_lo[48 * pair : 48 * pair + 48, k * NC : (k + 1) * NC] = (
                s - hi.astype(F32)
            ).astype(BF16)
    for c in copies[3:]:
        c.wait()
    at = geo_ref[G_FRAME : G_FRAME + 8, :].astype(jnp.int32)
    group = geo_ref[G_FRAME + 8 : G_FRAME + 16, :]
    g = jnp.full((8, NC), -1, jnp.int32)
    for i in range(5):
        end = min((i + 1) * NC, rs.shape[2])
        src = rs[0, :, i * NC : end]
        if end - i * NC < NC:
            src = jnp.concatenate([src, jnp.zeros((1, (i + 1) * NC - end), jnp.int32)], axis=1)
        src = jnp.broadcast_to(src, (8, NC))
        g = jnp.where(group == float(i), jnp.take_along_axis(src, at, axis=1), g)
    idx_ref[...] = g
    sphi, cphi = geo_ref[G_PHI : G_PHI + 1, :], geo_ref[G_PHI + 1 : G_PHI + 2, :]
    for k in range(NR):
        u = [blk[native_row(f, k), :] for f in range(8)]
        for f in range(8):
            put(own_ref, f * NR + k, u[f])
        for first, ref in ((0, dn_ref), (NR - 2, up_ref)):
            if k - first in (0, 1):
                for f in range(8):
                    put(ref, f * 2 + k - first, u[f])
        sin, cos = row_values(geo_ref, k + 2)[:2]
        c = [u[0], u[1]]
        for o in (2, 5):
            flat = u[o] * sin + u[o + 1] * cos
            c += [
                flat * cphi - u[o + 2] * sphi,
                flat * sphi + u[o + 2] * cphi,
                u[o] * cos - u[o + 1] * sin,
            ]
        c = jnp.concatenate(c, axis=0)
        hi = c.astype(BF16)
        c_hi[:, k * NC : (k + 1) * NC] = hi
        c_lo[:, k * NC : (k + 1) * NC] = (c - hi.astype(F32)).astype(BF16)

    def dot(x, y):
        return lax.dot_general(
            x[...], y[...], (((1,), (1,)), ((), ())), preferred_element_type=F32
        )

    sent = dot(s_hi, c_hi) + dot(s_hi, c_lo) + dot(s_lo, c_hi)
    for t in range(N_LON):
        pay_ref[t, 0:24, :] = sent[24 * t : 24 * t + 24, 0:NC]
        part = sent[24 * t : 24 * t + 24, NC : NC + 64]
        pay_ref[t, 24:32, :] = jnp.zeros((8, NC), F32)
        pay_ref[t, 19:29, 0:64] = part[0:10]
        pay_ref[t, 19:28, 64:128] = part[10:19]


def row_of(own_ref, top_ref, bot_ref, f, e):
    if isinstance(e, int) and e < 2:
        return tile(top_ref, f * 2 + e)
    if isinstance(e, int) and e >= NR + 2:
        return tile(bot_ref, f * 2 + e - NR - 2)
    return tile(own_ref, f * NR + e - 2)


def pack_kernel(own_ref, top_ref, bot_ref, left_ref, right_ref):
    lane = lax.broadcasted_iota(jnp.int32, (SH, NC), 1)
    for f in range(8):
        left = jnp.zeros((SH, NC), F32)
        right = jnp.zeros((SH, NC), F32)
        for e in range(EXT):
            x = lane_roll(row_of(own_ref, top_ref, bot_ref, f, e), 6 * e + 2)
            base = 6 * e
            left = jnp.where((lane >= base + 2) & (lane < base + 6), x, left)
            if e == 0:
                right = jnp.where((lane >= NC - 2) | (lane < 2), x, right)
            else:
                right = jnp.where((lane >= base - 2) & (lane < base + 2), x, right)
        put(left_ref, f, left)
        put(right_ref, f, right)


def main_kernel(own_ref, top_ref, bot_ref, geo_ref, out_ref, q_ref, r_ref):
    yang = lax.axis_index("panel").astype(F32)
    edges = shell_edges()

    def one(e, full):
        def fields(step):
            return [row_of(own_ref, top_ref, bot_ref, f, e + step) for f in range(8)]

        geo = row_geo(geo_ref, e, yang)
        scal = rows_one(fields, q_ref, r_ref, EXT, geo, edges, e, full)
        if full:
            for i in range(2):
                put(out_ref, i * NR + e - 2, scal[i])

    one(1, False)
    one(2, True)
    one(NR + 1, True)
    one(NR + 2, False)

    @pl.loop(3, NR + 1)
    def _(e):
        one(e, True)

    @pl.loop(2, NR + 2)
    def _(e):
        vec = rows_two(q_ref, r_ref, EXT, row_geo(geo_ref, e, yang), edges, e)
        for i in range(6):
            put(out_ref, (2 + i) * NR + e - 2, vec[i])


def to_spherical(x, y, z, sin, cos, sphi, cphi):
    flat = x * cphi + y * sphi
    return [flat * sin + z * cos, flat * cos - z * sin, y * cphi - x * sphi]


def border_fields(w, sin, cos, sphi, cphi):
    out = [w[0], w[1]]
    for o in (2, 5):
        out += to_spherical(-w[o], w[o + 2], w[o + 1], sin, cos, sphi, cphi)
    return out


STRIP = 6


def edge_kernel(own_ref, left_hbm, right_hbm, fromleft_hbm, fromright_hbm,
                don_ref, idx_ref, geo_ref, int_ref, osc_hbm, ove_hbm,
                out_ref, pack_ref, bord_ref, u_ref, q_ref, r_ref, sems):
    yang = lax.axis_index("panel").astype(F32)
    lat = lax.axis_index("lat")
    lon = lax.axis_index("lon")
    edges = shell_edges()
    row_edge = (lat == 0) | (lat == N_LAT - 1)
    col_edge = (lon == 0) | (lon == N_LON - 1)
    per = SH * NR
    fetches = [
        pltpu.make_async_copy(src, pack_ref.at[i], sems.at[8 + i])
        for i, src in enumerate((left_hbm, fromleft_hbm, right_hbm, fromright_hbm))
    ]
    for c in fetches:
        c.start()

    @pl.when(row_edge | col_edge)
    def _():
        recv = jnp.transpose(don_ref[...])
        hi = recv.astype(BF16)
        lo = (recv - hi.astype(F32)).astype(BF16)
        at = lax.broadcasted_iota(jnp.int32, (N_LON * CHUNK, NC), 0)
        for col in range(4):
            g = idx_ref[col : col + 1, :]
            donor = jnp.floor((g.astype(F32) + 0.5) * (1.0 / CAP)).astype(jnp.int32)
            slot = g - donor * CAP
            first = donor * CHUNK + slot
            here = jnp.where(g >= 0, first, -1)
            low = jnp.where((g >= 0) & (slot < 10), first + 19, -1)
            high = jnp.where((g >= 0) & (slot >= 10), first + 9, -1)

            def pick(where, lo_row, hi_row):
                hot = jnp.where(at == where, 1.0, 0.0).astype(BF16)
                return jnp.dot(hi[lo_row:hi_row], hot, preferred_element_type=F32) + jnp.dot(
                    lo[lo_row:hi_row], hot, preferred_element_type=F32
                )

            here_at = slice(col * NC, (col + 1) * NC)
            bord_ref[0:NC, here_at] = pick(here, 0, NC)
            bord_ref[NC : NC + 64, here_at] = pick(low, 0, 64) + pick(high, 64, NC)

    def border(col, sin, cos, sphi, cphi):
        w = [bord_ref[f * SH : f * SH + SH, col * NC : (col + 1) * NC] for f in range(8)]
        return border_fields(w, sin, cos, sphi, cphi)

    for c in fetches:
        c.wait()
    lane = lax.broadcasted_iota(jnp.int32, (SH, NC), 1)
    place = lane % 6
    merged = None
    for side in range(2):
        own, other = pack_ref.at[2 * side], pack_ref.at[2 * side + 1]
        theirs = (place < 2) if side == 0 else ((place == 2) | (place == 3))
        at = G_PACK + 4 * side
        th = [geo_ref[at + j : at + j + 1, :] for j in range(4)]
        at = G_PHI + 2 + 2 * side
        ph = [geo_ref[at + j : at + j + 1, :] for j in range(2)]
        g = jnp.broadcast_to(idx_ref[2 + side : 3 + side, :], (SH, NC))
        donated = border(2 + side, th[0], th[1], ph[0], ph[1])
        u = []
        for f in range(8):
            x = jnp.where(theirs, tile(other, f), tile(own, f))
            u.append(jnp.where(g >= 0, donated[f], x))
        geo = Geo(geo_ref, *th, *ph, yang)

        def diff_six(x):
            return lane_roll(x, -6) - lane_roll(x, 6)

        level, rest, scal = stage_one(u, lambda fn: diff_six(fn(u)), geo, edges, True)
        vec = stage_two(level, lambda i: diff_six(level[i]), rest, geo, edges)
        vals = list(scal) + vec
        if side == 0:
            merged = vals
        else:
            merged = [jnp.where(place < 2, y, x) for x, y in zip(merged, vals)]
    for f in range(8):
        put(u_ref, 8 * STRIP + f, merged[f])

    @pl.when(row_edge)
    def _():
        top = lat == 0
        e0 = jnp.where(top, 0, NR - 2)
        for i in range(2):
            sc = row_values(geo_ref, jnp.where(top, i, NR + 2 + i))
            phi = [geo_ref[G_PHI + j : G_PHI + j + 1, :] for j in range(2)]
            w = border(i, sc[0], sc[1], phi[0], phi[1])
            for f in range(8):
                put(u_ref, f * STRIP + jnp.where(top, i, 4 + i), w[f])
        for j in range(4):
            for f in range(8):
                x = tile(own_ref, f * NR + jnp.where(top, j, NR - 4 + j))
                put(u_ref, f * STRIP + jnp.where(top, 2 + j, j), x)

        for slot in (1, 2, 3, 4):
            def fields(step, slot=slot):
                return [tile(u_ref, f * STRIP + slot + step) for f in range(8)]

            full = slot in (2, 3)
            geo = row_geo(geo_ref, e0 + slot, yang)
            scal = rows_one(fields, q_ref, r_ref, STRIP, geo, edges, slot, full)
            if full:
                for i in range(2):
                    put(r_ref, (4 + i) * STRIP + slot, scal[i])
        for slot in (2, 3):
            vec = rows_two(q_ref, r_ref, STRIP, row_geo(geo_ref, e0 + slot, yang), edges, slot)
            for i in range(6):
                put(r_ref, (6 + i) * STRIP + slot, vec[i])

    edge_lane = (lane < 2) | (lane >= NC - 2)
    sends = []
    for f in range(8):
        cols = tile(u_ref, 8 * STRIP + f)
        for k in range(NR):
            x = lane_roll(cols, -(6 * (k + 2) + 2))
            out_ref[native_row(f, k), :] = jnp.where(edge_lane, x, tile(int_ref, f * NR + k))

        @pl.when(row_edge)
        def _(f=f):
            k0 = jnp.where(lat == 0, 0, NR - 2)
            for j in range(2):
                at = native_row(f, k0 + j)
                val = tile(r_ref, (4 + f) * STRIP + 2 + j)
                out_ref[at, :] = jnp.where(edge_lane, out_ref[at, :], val)

        dst = osc_hbm.at[pl.ds(f * per, per)] if f < 2 else ove_hbm.at[pl.ds((f - 2) * per, per)]
        sends.append(pltpu.make_async_copy(out_ref.at[pl.ds(f * per, per)], dst, sems.at[f]))
        sends[-1].start()
    for c in sends:
        c.wait()


VM = pl.BlockSpec(memory_space=pltpu.VMEM)
HBM = pl.BlockSpec(memory_space=pltpu.HBM)


def call(kernel, ins, outs, scratch, name, flops, mib):
    return pl.pallas_call(
        kernel,
        out_shape=[jax.ShapeDtypeStruct(s, t) for s, t, _ in outs],
        in_specs=ins,
        out_specs=[o[2] for o in outs],
        scratch_shapes=scratch,
        name=name,
        compiler_params=pltpu.CompilerParams(vmem_limit_bytes=mib * 1024 * 1024),
        cost_estimate=pl.CostEstimate(flops=flops, bytes_accessed=100000, transcendentals=0),
    )


def rows(n):
    return pltpu.VMEM((n * SH, NC), F32)


def shifted(x, axis, step):
    n = lax.axis_size(axis)
    return lax.ppermute(x, axis, [(i, (i + step) % n) for i in range(n)])


def body(scalars, vectors, corner_rows, corner_cols, send_weights, recv_source):
    sc = scalars.reshape(2 * SH * NR, NC)
    ve = vectors.reshape(6 * SH * NR, NC)
    halo = ((8 * 2 * SH, NC), F32, VM)
    pack = ((8 * SH, NC), F32, VM)
    block = ((8 * NR * SH, NC), F32, VM)
    table = pltpu.VMEM((N_LON, CAP), jnp.int32)

    def in_hbm(*arrays):
        return [pltpu.with_memory_space_constraint(a, pltpu.HBM) for a in arrays]

    pay, up, dn, own, geo, idx = call(
        donor_kernel, [HBM] * 8,
        [
            ((N_LON, CHUNK, NC), F32, VM), halo, halo, block,
            ((G_ALL, NC), F32, VM), ((8, NC), jnp.int32, VM),
        ],
        [
            rows(8 * NR), table, table,
            pltpu.VMEM((2, N_LON, CAP), F32),
            pltpu.VMEM((1, 1, 592), jnp.int32),
            pltpu.VMEM((NC, NC), F32),
            pltpu.VMEM((24 * N_LON, NR * NC), BF16),
            pltpu.VMEM((24 * N_LON, NR * NC), BF16),
            pltpu.VMEM((8 * SH, NR * NC), BF16),
            pltpu.VMEM((8 * SH, NR * NC), BF16),
            pltpu.SemaphoreType.DMA((8,)),
        ],
        "donor", 400000000, 20,
    )(*in_hbm(sc, ve, corner_rows, corner_cols, send_weights, recv_source,
              jnp.asarray(lat_table()), jnp.asarray(lon_table())))
    pay = lax.ppermute(pay, "panel", [(0, 1), (1, 0)])
    don = lax.all_to_all(pay, "lon", 0, 0, tiled=True).reshape(N_LON * CHUNK, NC)
    top = shifted(up, "lat", 1)
    bot = shifted(dn, "lat", -1)
    left, right = call(pack_kernel, [VM] * 3, [pack, pack], [], "packs", 50000000000, 12)(
        own, top, bot
    )
    from_left = shifted(right, "lon", 1)
    from_right = shifted(left, "lon", -1)
    (inner,) = call(
        main_kernel, [VM] * 4, [block], [rows(12 * EXT), rows(4 * EXT)],
        "interior", 300000, 16,
    )(own, top, bot, geo)
    osc, ove = call(
        edge_kernel, [VM] + [HBM] * 4 + [VM] * 4,
        [(sc.shape, F32, HBM), (ve.shape, F32, HBM)],
        [
            rows(8 * NR),
            pltpu.VMEM((4, 8 * SH, NC), F32),
            pltpu.VMEM((8 * SH, 4 * NC), F32),
            rows(8 * STRIP + 8), rows(12 * STRIP), rows(12 * STRIP),
            pltpu.SemaphoreType.DMA((12,)),
        ],
        "edges", 10000000, 16,
    )(own, *in_hbm(left, right, from_left, from_right), don, idx, geo, inner)
    return osc.reshape(scalars.shape), ove.reshape(vectors.shape)


def solution(mesh):
    return jax.shard_map(
        body,
        mesh=mesh,
        in_specs=(
            P("panel", None, None, "lat", "lon"),
            P("panel", None, None, "lat", "lon"),
            P("lat", "lon", None, None),
            P("lat", "lon", None, None),
            P(None, "lat", "lon", None, None),
            P("lat", "lon", None),
        ),
        out_specs=(P("panel", None, None, "lat", "lon"), P("panel", None, None, "lat", "lon")),
        check_vma=False,
    )
```

```python
import math

import jax
import jax.numpy as jnp
import numpy as np
from jax import lax
from jax.experimental import pallas as pl
from jax.experimental.pallas import tpu as pltpu
from jax.sharding import PartitionSpec as P

GAMMA = 5.0 / 3.0
F32 = jnp.float32
BF16 = jnp.bfloat16
SH = 24
NR = 16
NC = 128
N_LAT = 8
N_LON = 16
CAP = 19
CHUNK = 32
EXT = NR + 4
ROW_SCALARS = 4

D_TH = 0.5 * math.pi / (NR * N_LAT)
D_PH = 1.5 * math.pi / (NC * N_LON)
D_R = 0.6 * D_TH
DT = 0.3 * min(D_R, 0.6 * math.sin(0.25 * math.pi - 2.0 * D_TH) * D_PH)
MU = DT / 0.9
GRAV = 0.036 / DT
OMEGA = 0.05 / DT


def theta_of(k):
    return 0.25 * math.pi + (k + 0.5) * D_TH


def phi_of(m):
    return -0.75 * math.pi + (m + 0.5) * D_PH


def lane_rows(shift):
    lane = (np.arange(NC) + shift) % NC
    return lane // 6, lane % 6


G_ROWS = 0
G_RAD = EXT * ROW_SCALARS
G_PACK = G_RAD + 3 * SH
G_FRAME = G_PACK + 8
G_PHI = G_FRAME + 16
G_ALL = G_PHI + 8


def frame_table(i):
    wide = NC + 4
    at = np.full((4, NC), -1)
    row = 0 if i == 0 else 2
    for j in range(2):
        at[j] = (row + j) * wide + 2 + np.arange(NC)
    for side in range(2):
        r, c = lane_rows(2 * side)
        for lane in range(NC):
            col = c[lane] if side == 0 else NC - 2 + c[lane]
            if r[lane] in (0, 1):
                at[2 + side, lane] = r[lane] * wide + col
            elif r[lane] in (EXT - 2, EXT - 1):
                at[2 + side, lane] = (r[lane] - NR) * wide + col
            elif r[lane] < EXT and side == 0 and c[lane] < 2:
                at[2, lane] = 4 * wide + 2 * (r[lane] - 2) + c[lane]
            elif r[lane] < EXT and side == 1 and c[lane] >= 4:
                at[3, lane] = 4 * wide + 2 * NR + 2 * (r[lane] - 2) + c[lane] - 4
    out = np.zeros((16, NC))
    out[8:] = -1
    out[0:4] = np.where(at >= 0, at % NC, 0)
    out[8:12] = np.where(at >= 0, at // NC, -1)
    return out


def lat_table():
    out = np.zeros((N_LAT, G_PHI, NC))
    s = np.arange(SH, dtype=np.float64)
    r = 0.6 + (s + 0.5) * D_R
    ratio = np.ones(SH)
    ratio[0] = r[0] / (0.6 - 0.5 * D_R)
    ratio[-1] = r[-1] / (0.6 + (SH + 0.5) * D_R)
    out[:, G_RAD:G_PACK] = np.concatenate([1.0 / r, ratio, DT * GRAV / (r * r)])[:, None]

    def four(th):
        return np.stack([np.sin(th), np.cos(th), np.cos(th) / np.sin(th), 1.0 / np.sin(th)])

    for i in range(N_LAT):
        th = theta_of(i * NR - 2 + np.arange(EXT))
        out[i, G_ROWS:G_RAD] = four(th).T.reshape(-1)[:, None]
        for side in range(2):
            rr, _ = lane_rows(2 * side)
            at = G_PACK + 4 * side
            out[i, at : at + 4] = four(theta_of(i * NR - 2 + np.minimum(rr, EXT - 1)))
        out[i, G_FRAME:G_PHI] = frame_table(i)
    return out.astype(np.float32)


def lon_table():
    out = np.zeros((N_LON, 8, NC))
    for q in range(N_LON):
        ph = phi_of(q * NC + np.arange(NC))
        out[q, 0], out[q, 1] = np.sin(ph), np.cos(ph)
        for side in range(2):
            _, c = lane_rows(2 * side)
            ph = phi_of(q * NC + (c - 2 if side == 0 else c + NC - 4))
            out[q, 2 + 2 * side], out[q, 3 + 2 * side] = np.sin(ph), np.cos(ph)
    return out.astype(np.float32)


class Geo:
    def __init__(self, geo_ref, sin, cos, cot, isin, sphi, cphi, yang):
        self.rinv = geo_ref[G_RAD : G_RAD + SH, :]
        self.ratio = geo_ref[G_RAD + SH : G_RAD + 2 * SH, :]
        self.grav = geo_ref[G_RAD + 2 * SH : G_RAD + 3 * SH, :]
        self.ct = self.rinv * (0.5 / D_TH)
        self.cp = self.rinv * (0.5 / D_PH) * isin
        self.cotr = self.rinv * cot
        self.n_r = (1.0 - yang) * cos + yang * (sin * sphi)
        self.n_t = (yang - 1.0) * sin + yang * (cos * sphi)
        self.n_p = yang * cphi


def lane_roll(x, shift):
    return pltpu.roll(x, shift % NC, 1)


def diff_p(x):
    return lane_roll(x, -1) - lane_roll(x, 1)


def diff_r(x, ghost, edges):
    first, last = edges
    return jnp.where(last, ghost, pltpu.roll(x, SH - 1, 0)) - jnp.where(
        first, ghost, pltpu.roll(x, 1, 0)
    )


def cross(a, b):
    return (
        a[1] * b[2] - a[2] * b[1],
        a[2] * b[0] - a[0] * b[2],
        a[0] * b[1] - a[1] * b[0],
    )


def stage_one(u, diff_t, geo, edges, full):
    rinv, ct, cp, cotr = geo.rinv, geo.ct, geo.cp, geo.cotr
    cr = 0.5 / D_R
    rho, pr = u[0], u[1]
    v, b = u[2:5], u[5:8]

    def d_r(x):
        return diff_r(x, x, edges) * cr

    def d_t(fn):
        return diff_t(fn) * ct

    def d_p(x):
        return diff_p(x) * cp

    bt_r, bp_r = d_r(b[1]), d_r(b[2])
    j_r = d_t(lambda w: w[7]) + b[2] * cotr - d_p(b[1])
    jt_ang = d_p(b[0]) - b[2] * rinv
    jp_ang = b[1] * rinv - d_t(lambda w: w[5])
    jj = (j_r, jt_ang - bp_r, bt_r + jp_ang)
    vr = [d_r(x) for x in v]
    vt = [d_t(lambda w, i=i: w[2 + i]) for i in range(3)]
    vp = [d_p(x) for x in v]
    wt_ang = vp[0] - v[2] * rinv
    wp_ang = v[1] * rinv - vt[0]
    ww = (vt[2] + v[2] * cotr - vp[1], wt_ang - vr[2], vr[1] + wp_ang)
    e_ang = 2.0 * v[0] * rinv + vt[1] + v[1] * cotr + vp[2]
    ee = vr[0] + e_ang
    vxb = cross(v, b)
    el = [vxb[i] - MU * jj[i] for i in range(3)]
    ratio = geo.ratio
    level = list(ww) + [ee] + el
    level += [
        wt_ang * ratio,
        wp_ang * ratio,
        e_ang * ratio,
        vxb[1] - MU * (jt_ang * ratio),
        vxb[2] - MU * (jp_ang * ratio),
    ]
    if not full:
        return level, None, None
    fr, fp = rho * v[0], rho * v[2]
    mass = (
        d_r(fr)
        + 2.0 * fr * rinv
        + d_t(lambda w: w[0] * w[3])
        + rho * v[1] * cotr
        + d_p(fp)
    )
    gp = (d_r(pr), d_t(lambda w: w[1]), d_p(pr))
    press = -(v[0] * gp[0] + v[1] * gp[1] + v[2] * gp[2]) - GAMMA * pr * ee
    lor = cross(jj, b)
    spin = cross(v, (geo.n_r, geo.n_t, geo.n_p))
    curv = (
        -(v[1] * v[1] + v[2] * v[2]) * rinv,
        v[0] * v[1] * rinv - v[2] * v[2] * cotr,
        v[0] * v[2] * rinv + v[1] * v[2] * cotr,
    )
    irho = DT / rho
    rest = []
    for i in range(3):
        adv = v[0] * vr[i] + v[1] * vt[i] + v[2] * vp[i] + curv[i]
        x = (lor[i] - gp[i]) * irho - DT * adv + (2.0 * OMEGA * DT) * spin[i]
        rest.append(x - geo.grav if i == 0 else x)
    rest.append(irho * MU)
    return level, rest, (-DT * mass, DT * press)


def stage_two(q, diff_t, rest, geo, edges):
    rinv, ct, cp, cotr = geo.rinv, geo.ct, geo.cp, geo.cotr
    cr = 0.5 / D_R

    def d_r(i, g):
        return diff_r(q[i], q[g], edges) * cr

    def d_t(i):
        return diff_t(i) * ct

    def d_p(i):
        return diff_p(q[i]) * cp

    def curl(o, gt, gp):
        return (
            d_t(o + 2) + q[o + 2] * cotr - d_p(o + 1),
            d_p(o) - d_r(o + 2, gp) - q[o + 2] * rinv,
            d_r(o + 1, gt) + q[o + 1] * rinv - d_t(o),
        )

    cw = curl(0, 7, 8)
    grad_e = (d_r(3, 9), d_t(3), d_p(3))
    ce = curl(4, 10, 11)
    acc = [rest[i] + rest[3] * (4.0 / 3.0 * grad_e[i] - cw[i]) for i in range(3)]
    return acc + [DT * ce[i] for i in range(3)]


def shell_edges():
    s = lax.broadcasted_iota(jnp.int32, (SH, NC), 0)
    return s == 0, s == SH - 1


def aligned(i):
    return i if isinstance(i, int) else pl.multiple_of(i, 8)


def tile(ref, i):
    return ref[pl.ds(aligned(i * SH), SH), :]


def put(ref, i, val):
    ref[pl.ds(aligned(i * SH), SH), :] = val


def row_values(geo_ref, e):
    return [geo_ref[pl.ds(e * ROW_SCALARS + j, 1), :] for j in range(ROW_SCALARS)]


def row_geo(geo_ref, e, yang):
    return Geo(
        geo_ref, *row_values(geo_ref, e), geo_ref[G_PHI : G_PHI + 1, :],
        geo_ref[G_PHI + 1 : G_PHI + 2, :], yang,
    )


def rows_one(fields, q_ref, r_ref, depth, geo, edges, slot, full):
    up, dn = fields(1), fields(-1)
    level, rest, scal = stage_one(fields(0), lambda fn: fn(up) - fn(dn), geo, edges, full)
    for i, x in enumerate(level):
        put(q_ref, i * depth + slot, x)
    if full:
        for i, x in enumerate(rest):
            put(r_ref, i * depth + slot, x)
    return scal


def rows_two(q_ref, r_ref, depth, geo, edges, slot):
    q = [tile(q_ref, i * depth + slot) for i in range(12)]

    def diff_t(i):
        return tile(q_ref, i * depth + slot + 1) - tile(q_ref, i * depth + slot - 1)

    rest = [tile(r_ref, i * depth + slot) for i in range(4)]
    return stage_two(q, diff_t, rest, geo, edges)


def native_row(f, k):
    return pl.ds(f * (SH * NR) + k, SH, stride=NR)


def donor_kernel(sc_hbm, ve_hbm, cr_hbm, cc_hbm, sw_hbm, rs_hbm, lat_hbm, lon_hbm,
                 pay_ref, up_ref, dn_ref, own_ref, geo_ref, idx_ref,
                 blk, cr, cc, sw, rs, s_hi, s_lo, c_hi, c_lo, sent_a, sent_b, sems):
    lat, lon = lax.axis_index("lat"), lax.axis_index("lon")
    n_sc = 2 * SH * NR
    moves = [
        (cr_hbm.at[0, 0], cr),
        (cc_hbm.at[0, 0], cc),
        (sw_hbm.at[:, 0, 0], sw),
        (rs_hbm, rs),
        (lat_hbm.at[lat], geo_ref.at[0:G_PHI]),
        (lon_hbm.at[lon], geo_ref.at[G_PHI:G_ALL]),
        (sc_hbm, blk.at[0:n_sc]),
        (ve_hbm, blk.at[n_sc : 4 * n_sc]),
    ]
    copies = [pltpu.make_async_copy(a, b, sems.at[i]) for i, (a, b) in enumerate(moves)]
    for c in copies:
        c.start()
    for c in copies[:3]:
        c.wait()
    tables = [cr[...].astype(F32), cc[...].astype(F32), sw[0], sw[1]]
    lane = lax.broadcasted_iota(jnp.int32, (N_LON, NC), 1).astype(F32)
    for j in range(CAP):
        a, b, wt, wp = [jnp.broadcast_to(x[:, j : j + 1], (N_LON, NC)) for x in tables]
        along = jnp.where(lane == b, 1.0 - wp, jnp.where(lane == b + 1.0, wp, 0.0))
        first, second = along * (1.0 - wt), along * wt
        here = slice(N_LON * j, N_LON * j + N_LON)
        for k in range(NR):
            s = jnp.where(a == float(k), first, jnp.where(a == float(k - 1), second, 0.0))
            hi = s.astype(BF16)
            s_hi[here, k * NC : (k + 1) * NC] = hi
            s_lo[here, k * NC : (k + 1) * NC] = (s - hi.astype(F32)).astype(BF16)
    for c in copies[3:]:
        c.wait()
    at = geo_ref[G_FRAME : G_FRAME + 8, :].astype(jnp.int32)
    group = geo_ref[G_FRAME + 8 : G_FRAME + 16, :]
    g = jnp.full((8, NC), -1, jnp.int32)
    for i in range(5):
        end = min((i + 1) * NC, rs.shape[2])
        src = rs[0, :, i * NC : end]
        if end - i * NC < NC:
            src = jnp.concatenate([src, jnp.zeros((1, (i + 1) * NC - end), jnp.int32)], axis=1)
        src = jnp.broadcast_to(src, (8, NC))
        g = jnp.where(group == float(i), jnp.take_along_axis(src, at, axis=1), g)
    idx_ref[...] = g
    sphi, cphi = geo_ref[G_PHI : G_PHI + 1, :], geo_ref[G_PHI + 1 : G_PHI + 2, :]
    for k in range(NR):
        u = [blk[native_row(f, k), :] for f in range(8)]
        for f in range(8):
            put(own_ref, f * NR + k, u[f])
        for first, ref in ((0, dn_ref), (NR - 2, up_ref)):
            if k - first in (0, 1):
                for f in range(8):
                    put(ref, f * 2 + k - first, u[f])
        sin, cos = row_values(geo_ref, k + 2)[:2]
        c = [u[0], u[1]]
        for o in (2, 5):
            flat = u[o] * sin + u[o + 1] * cos
            c += [
                flat * cphi - u[o + 2] * sphi,
                flat * sphi + u[o + 2] * cphi,
                u[o] * cos - u[o + 1] * sin,
            ]
        c = jnp.concatenate(c, axis=0)
        hi = c.astype(BF16)
        c_hi[:, k * NC : (k + 1) * NC] = hi
        c_lo[:, k * NC : (k + 1) * NC] = (c - hi.astype(F32)).astype(BF16)

    def dot(x, y):
        return lax.dot_general(
            x[...], y[...], (((1,), (1,)), ((), ())), preferred_element_type=F32
        )

    sent = dot(s_hi, c_hi) + dot(s_hi, c_lo) + dot(s_lo, c_hi)
    sent_a[...] = sent[:, 0:NC]
    sent_b[:, 0:64] = sent[:, NC : NC + 64]
    for t in range(N_LON):
        mine = pl.ds(t, CAP, stride=N_LON)
        part = sent_b[mine, :]
        pay_ref[t, 24:32, :] = jnp.zeros((8, NC), F32)
        pay_ref[t, 0:CAP, :] = sent_a[mine, :]
        pay_ref[t, 19:29, 0:64] = part[0:10, 0:64]
        pay_ref[t, 19:28, 64:128] = part[10:19, 0:64]


def row_of(own_ref, top_ref, bot_ref, f, e):
    if isinstance(e, int) and e < 2:
        return tile(top_ref, f * 2 + e)
    if isinstance(e, int) and e >= NR + 2:
        return tile(bot_ref, f * 2 + e - NR - 2)
    return tile(own_ref, f * NR + e - 2)


def dense(fields, first, place):
    out = []
    for o in range(0, 8, 3):
        group = None
        for j, x in enumerate(fields[o : o + 3]):
            at = (first + 2 * j) % 6
            x = lane_roll(x, at - first)
            mine = (place == at) | (place == at + 1)
            group = x if group is None else jnp.where(mine, x, group)
        out.append(group)
    return out


def undense(group, first, j):
    return lane_roll(group, first - (first + 2 * j) % 6)


def pack_kernel(own_ref, top_ref, bot_ref, left_ref, right_ref, go_left_ref, go_right_ref):
    lane = lax.broadcasted_iota(jnp.int32, (SH, NC), 1)
    place = lane % 6
    lefts, rights = [], []
    for f in range(8):
        left = jnp.zeros((SH, NC), F32)
        right = jnp.zeros((SH, NC), F32)
        for e in range(EXT):
            x = lane_roll(row_of(own_ref, top_ref, bot_ref, f, e), 6 * e + 2)
            base = 6 * e
            left = jnp.where((lane >= base + 2) & (lane < base + 6), x, left)
            if e == 0:
                right = jnp.where((lane >= NC - 2) | (lane < 2), x, right)
            else:
                right = jnp.where((lane >= base - 2) & (lane < base + 2), x, right)
        put(left_ref, f, left)
        put(right_ref, f, right)
        lefts.append(left)
        rights.append(right)
    for i, x in enumerate(dense(lefts, 2, place)):
        put(go_left_ref, i, x)
    for i, x in enumerate(dense(rights, 0, place)):
        put(go_right_ref, i, x)


def main_kernel(own_ref, top_ref, bot_ref, geo_ref, out_hbm, near_ref, out_ref, q_ref, r_ref, sems):
    k0 = jnp.where(lax.axis_index("lat") == 0, 0, NR - 4)
    for f in range(8):
        for j in range(4):
            put(near_ref, f * 4 + j, tile(own_ref, f * NR + k0 + j))
    yang = lax.axis_index("panel").astype(F32)
    edges = shell_edges()

    def one(e, full):
        def fields(step):
            return [row_of(own_ref, top_ref, bot_ref, f, e + step) for f in range(8)]

        geo = row_geo(geo_ref, e, yang)
        scal = rows_one(fields, q_ref, r_ref, EXT, geo, edges, e, full)
        if full:
            for i in range(2):
                put(out_ref, (e - 2) * 8 + i, scal[i])

    @pl.loop(3, NR + 1)
    def _(e):
        one(e, True)

    one(1, False)
    one(2, True)
    one(NR + 1, True)
    one(NR + 2, False)

    sends = []
    for part in range(4):
        k0 = part * (NR // 4)

        @pl.loop(k0 + 2, k0 + NR // 4 + 2)
        def _(e):
            vec = rows_two(q_ref, r_ref, EXT, row_geo(geo_ref, e, yang), edges, e)
            for i in range(6):
                put(out_ref, (e - 2) * 8 + 2 + i, vec[i])

        span = pl.ds(k0 * 8 * SH, NR // 4 * 8 * SH)
        sends.append(
            pltpu.make_async_copy(out_ref.at[span], out_hbm.at[span], sems.at[part])
        )
        sends[-1].start()
    for c in sends:
        c.wait()


def to_spherical(x, y, z, sin, cos, sphi, cphi):
    flat = x * cphi + y * sphi
    return [flat * sin + z * cos, flat * cos - z * sin, y * cphi - x * sphi]


def border_fields(w, sin, cos, sphi, cphi):
    out = [w[0], w[1]]
    for o in (2, 5):
        out += to_spherical(-w[o], w[o + 2], w[o + 1], sin, cos, sphi, cphi)
    return out


STRIP = 6


def edge_kernel(near_ref, left_ref, right_ref, fromleft_ref, fromright_ref,
                don_ref, idx_ref, geo_ref, int_hbm, osc_hbm, ove_hbm,
                int_ref, out_ref, bord_ref, u_ref, q_ref, r_ref, sems):
    yang = lax.axis_index("panel").astype(F32)
    lat = lax.axis_index("lat")
    lon = lax.axis_index("lon")
    edges = shell_edges()
    row_edge = (lat == 0) | (lat == N_LAT - 1)
    col_edge = (lon == 0) | (lon == N_LON - 1)
    per = SH * NR
    fetch = pltpu.make_async_copy(int_hbm, int_ref, sems.at[8])
    fetch.start()
    @pl.when(row_edge | col_edge)
    def _():
        recv = jnp.transpose(don_ref[...])
        hi = recv.astype(BF16)
        lo = (recv - hi.astype(F32)).astype(BF16)
        at = lax.broadcasted_iota(jnp.int32, (N_LON * CHUNK, NC), 0)
        for col in range(4):
            g = idx_ref[col : col + 1, :]
            donor = jnp.floor((g.astype(F32) + 0.5) * (1.0 / CAP)).astype(jnp.int32)
            slot = g - donor * CAP
            first = donor * CHUNK + slot
            here = jnp.where(g >= 0, first, -1)
            low = jnp.where((g >= 0) & (slot < 10), first + 19, -1)
            high = jnp.where((g >= 0) & (slot >= 10), first + 9, -1)

            def pick(where, lo_row, hi_row):
                hot = jnp.where(at == where, 1.0, 0.0).astype(BF16)
                return jnp.dot(hi[lo_row:hi_row], hot, preferred_element_type=F32) + jnp.dot(
                    lo[lo_row:hi_row], hot, preferred_element_type=F32
                )

            here_at = slice(col * NC, (col + 1) * NC)
            bord_ref[0:NC, here_at] = pick(here, 0, NC)
            bord_ref[NC : NC + 64, here_at] = pick(low, 0, 64) + pick(high, 64, NC)

    def border(col, sin, cos, sphi, cphi):
        w = [bord_ref[f * SH : f * SH + SH, col * NC : (col + 1) * NC] for f in range(8)]
        return border_fields(w, sin, cos, sphi, cphi)

    lane = lax.broadcasted_iota(jnp.int32, (SH, NC), 1)
    place = lane % 6
    merged = None
    for side in range(2):
        own, other = (left_ref, fromleft_ref) if side == 0 else (right_ref, fromright_ref)
        theirs = (place < 2) if side == 0 else ((place == 2) | (place == 3))
        at = G_PACK + 4 * side
        th = [geo_ref[at + j : at + j + 1, :] for j in range(4)]
        at = G_PHI + 2 + 2 * side
        ph = [geo_ref[at + j : at + j + 1, :] for j in range(2)]
        g = jnp.broadcast_to(idx_ref[2 + side : 3 + side, :], (SH, NC))
        donated = border(2 + side, th[0], th[1], ph[0], ph[1])
        u = []
        for f in range(8):
            x = undense(tile(other, f // 3), 2 * side, f % 3)
            x = jnp.where(theirs, x, tile(own, f))
            u.append(jnp.where(g >= 0, donated[f], x))
        geo = Geo(geo_ref, *th, *ph, yang)

        def diff_six(x):
            return lane_roll(x, -6) - lane_roll(x, 6)

        level, rest, scal = stage_one(u, lambda fn: diff_six(fn(u)), geo, edges, True)
        vec = stage_two(level, lambda i: diff_six(level[i]), rest, geo, edges)
        vals = list(scal) + vec
        if side == 0:
            merged = vals
        else:
            merged = [jnp.where(place < 2, y, x) for x, y in zip(merged, vals)]
    for f in range(8):
        put(u_ref, 8 * STRIP + f, merged[f])

    @pl.when(row_edge)
    def _():
        top = lat == 0
        e0 = jnp.where(top, 0, NR - 2)
        for i in range(2):
            sc = row_values(geo_ref, jnp.where(top, i, NR + 2 + i))
            phi = [geo_ref[G_PHI + j : G_PHI + j + 1, :] for j in range(2)]
            w = border(i, sc[0], sc[1], phi[0], phi[1])
            for f in range(8):
                put(u_ref, f * STRIP + jnp.where(top, i, 4 + i), w[f])
        for j in range(4):
            for f in range(8):
                x = tile(near_ref, f * 4 + j)
                put(u_ref, f * STRIP + jnp.where(top, 2 + j, j), x)

        for slot in (1, 2, 3, 4):
            def fields(step, slot=slot):
                return [tile(u_ref, f * STRIP + slot + step) for f in range(8)]

            full = slot in (2, 3)
            geo = row_geo(geo_ref, e0 + slot, yang)
            scal = rows_one(fields, q_ref, r_ref, STRIP, geo, edges, slot, full)
            if full:
                for i in range(2):
                    put(r_ref, (4 + i) * STRIP + slot, scal[i])
        for slot in (2, 3):
            vec = rows_two(q_ref, r_ref, STRIP, row_geo(geo_ref, e0 + slot, yang), edges, slot)
            for i in range(6):
                put(r_ref, (6 + i) * STRIP + slot, vec[i])

    edge_lane = (lane < 2) | (lane >= NC - 2)
    sends = []
    fetch.wait()
    for f in range(8):
        cols = tile(u_ref, 8 * STRIP + f)
        for k in range(NR):
            x = lane_roll(cols, -(6 * (k + 2) + 2))
            out_ref[native_row(f, k), :] = jnp.where(edge_lane, x, tile(int_ref, k * 8 + f))

        @pl.when(row_edge)
        def _(f=f):
            k0 = jnp.where(lat == 0, 0, NR - 2)
            for j in range(2):
                at = native_row(f, k0 + j)
                val = tile(r_ref, (4 + f) * STRIP + 2 + j)
                out_ref[at, :] = jnp.where(edge_lane, out_ref[at, :], val)

        dst = osc_hbm.at[pl.ds(f * per, per)] if f < 2 else ove_hbm.at[pl.ds((f - 2) * per, per)]
        sends.append(pltpu.make_async_copy(out_ref.at[pl.ds(f * per, per)], dst, sems.at[f]))
        sends[-1].start()
    for c in sends:
        c.wait()


VM = pl.BlockSpec(memory_space=pltpu.VMEM)
HBM = pl.BlockSpec(memory_space=pltpu.HBM)
PINNED = pl.BlockSpec(memory_space=pltpu.HBM)


def call(kernel, ins, outs, scratch, name, flops, mib):
    return pl.pallas_call(
        kernel,
        out_shape=[
            pltpu.HBM(s, t) if m is PINNED else jax.ShapeDtypeStruct(s, t) for s, t, m in outs
        ],
        in_specs=ins,
        out_specs=[o[2] for o in outs],
        scratch_shapes=scratch,
        name=name,
        compiler_params=pltpu.CompilerParams(vmem_limit_bytes=mib * 1024 * 1024),
        cost_estimate=pl.CostEstimate(flops=flops, bytes_accessed=100000, transcendentals=0),
    )


def rows(n):
    return pltpu.VMEM((n * SH, NC), F32)


def shifted(x, axis, step):
    n = lax.axis_size(axis)
    return lax.ppermute(x, axis, [(i, (i + step) % n) for i in range(n)])


def body(scalars, vectors, corner_rows, corner_cols, send_weights, recv_source):
    sc = scalars.reshape(2 * SH * NR, NC)
    ve = vectors.reshape(6 * SH * NR, NC)
    halo = ((8 * 2 * SH, NC), F32, VM)
    pack = ((8 * SH, NC), F32, VM)
    block = ((8 * NR * SH, NC), F32, VM)
    table = pltpu.VMEM((N_LON, CAP), jnp.int32)

    def in_hbm(*arrays):
        return [pltpu.with_memory_space_constraint(a, pltpu.HBM) for a in arrays]

    pay, up, dn, own, geo, idx = call(
        donor_kernel, [HBM] * 8,
        [
            ((N_LON, CHUNK, NC), F32, VM), halo, halo, block,
            ((G_ALL, NC), F32, VM), ((8, NC), jnp.int32, VM),
        ],
        [
            rows(8 * NR), table, table,
            pltpu.VMEM((2, N_LON, CAP), F32),
            pltpu.VMEM((1, 1, 592), jnp.int32),
            pltpu.VMEM((CAP * N_LON, NR * NC), BF16),
            pltpu.VMEM((CAP * N_LON, NR * NC), BF16),
            pltpu.VMEM((8 * SH, NR * NC), BF16),
            pltpu.VMEM((8 * SH, NR * NC), BF16),
            pltpu.VMEM((CAP * N_LON, NC), F32),
            pltpu.VMEM((CAP * N_LON, NC), F32),
            pltpu.SemaphoreType.DMA((8,)),
        ],
        "donor", 400000000, 20,
    )(*in_hbm(sc, ve, corner_rows, corner_cols, send_weights, recv_source,
              jnp.asarray(lat_table()), jnp.asarray(lon_table())))
    pay = lax.ppermute(pay, "panel", [(0, 1), (1, 0)])
    don = lax.all_to_all(pay, "lon", 0, 0, tiled=True).reshape(N_LON * CHUNK, NC)
    top = shifted(up, "lat", 1)
    bot = shifted(dn, "lat", -1)
    thin = ((3 * SH, NC), F32, VM)
    left, right, go_left, go_right = call(pack_kernel, [VM] * 3, [pack, pack, thin, thin], [], "packs", 50000000000, 12)(
        own, top, bot
    )
    from_left = shifted(go_right, "lon", 1)
    from_right = shifted(go_left, "lon", -1)
    inner, near = call(
        main_kernel, [VM] * 4, [block[:2] + (PINNED,), ((8 * 4 * SH, NC), F32, VM)],
        [rows(8 * NR), rows(12 * EXT), rows(4 * EXT), pltpu.SemaphoreType.DMA((4,))],
        "interior", 300000, 16,
    )(own, top, bot, geo)
    osc, ove = call(
        edge_kernel, [VM] * 8 + [HBM],
        [(sc.shape, F32, HBM), (ve.shape, F32, HBM)],
        [
            rows(8 * NR), rows(8 * NR),
            pltpu.VMEM((8 * SH, 4 * NC), F32),
            rows(8 * STRIP + 8), rows(12 * STRIP), rows(12 * STRIP),
            pltpu.SemaphoreType.DMA((9,)),
        ],
        "edges", 10000000, 16,
    )(near, left, right, from_left, from_right, don, idx, geo, *in_hbm(inner))
    return osc.reshape(scalars.shape), ove.reshape(vectors.shape)


def solution(mesh):
    return jax.shard_map(
        body,
        mesh=mesh,
        in_specs=(
            P("panel", None, None, "lat", "lon"),
            P("panel", None, None, "lat", "lon"),
            P("lat", "lon", None, None),
            P("lat", "lon", None, None),
            P(None, "lat", "lon", None, None),
            P("lat", "lon", None),
        ),
        out_specs=(P("panel", None, None, "lat", "lon"), P("panel", None, None, "lat", "lon")),
        check_vma=False,
    )
```

```python
import math

import jax
import jax.numpy as jnp
import numpy as np
from jax import lax
from jax.experimental import pallas as pl
from jax.experimental.pallas import tpu as pltpu
from jax.sharding import PartitionSpec as P

GAMMA = 5.0 / 3.0
F32 = jnp.float32
BF16 = jnp.bfloat16
SH = 24
NR = 16
NC = 128
N_LAT = 8
N_LON = 16
CAP = 19
CHUNK = 32
EXT = NR + 4
ROW_SCALARS = 4

D_TH = 0.5 * math.pi / (NR * N_LAT)
D_PH = 1.5 * math.pi / (NC * N_LON)
D_R = 0.6 * D_TH
DT = 0.3 * min(D_R, 0.6 * math.sin(0.25 * math.pi - 2.0 * D_TH) * D_PH)
MU = DT / 0.9
GRAV = 0.036 / DT
OMEGA = 0.05 / DT


def theta_of(k):
    return 0.25 * math.pi + (k + 0.5) * D_TH


def phi_of(m):
    return -0.75 * math.pi + (m + 0.5) * D_PH


def lane_rows(shift):
    lane = (np.arange(NC) + shift) % NC
    return lane // 6, lane % 6


G_ROWS = 0
G_RAD = EXT * ROW_SCALARS
G_PACK = G_RAD + 3 * SH
G_FRAME = G_PACK + 8
G_PHI = G_FRAME + 16
G_ALL = G_PHI + 8


def frame_table(i):
    wide = NC + 4
    at = np.full((4, NC), -1)
    row = 0 if i == 0 else 2
    for j in range(2):
        at[j] = (row + j) * wide + 2 + np.arange(NC)
    for side in range(2):
        r, c = lane_rows(2 * side)
        for lane in range(NC):
            col = c[lane] if side == 0 else NC - 2 + c[lane]
            if r[lane] in (0, 1):
                at[2 + side, lane] = r[lane] * wide + col
            elif r[lane] in (EXT - 2, EXT - 1):
                at[2 + side, lane] = (r[lane] - NR) * wide + col
            elif r[lane] < EXT and side == 0 and c[lane] < 2:
                at[2, lane] = 4 * wide + 2 * (r[lane] - 2) + c[lane]
            elif r[lane] < EXT and side == 1 and c[lane] >= 4:
                at[3, lane] = 4 * wide + 2 * NR + 2 * (r[lane] - 2) + c[lane] - 4
    out = np.zeros((16, NC))
    out[8:] = -1
    out[0:4] = np.where(at >= 0, at % NC, 0)
    out[8:12] = np.where(at >= 0, at // NC, -1)
    return out


def lat_table():
    out = np.zeros((N_LAT, G_PHI, NC))
    s = np.arange(SH, dtype=np.float64)
    r = 0.6 + (s + 0.5) * D_R
    ratio = np.ones(SH)
    ratio[0] = r[0] / (0.6 - 0.5 * D_R)
    ratio[-1] = r[-1] / (0.6 + (SH + 0.5) * D_R)
    out[:, G_RAD:G_PACK] = np.concatenate([1.0 / r, ratio, DT * GRAV / (r * r)])[:, None]

    def four(th):
        return np.stack([np.sin(th), np.cos(th), np.cos(th) / np.sin(th), 1.0 / np.sin(th)])

    for i in range(N_LAT):
        th = theta_of(i * NR - 2 + np.arange(EXT))
        out[i, G_ROWS:G_RAD] = four(th).T.reshape(-1)[:, None]
        for side in range(2):
            rr, _ = lane_rows(2 * side)
            at = G_PACK + 4 * side
            out[i, at : at + 4] = four(theta_of(i * NR - 2 + np.minimum(rr, EXT - 1)))
        out[i, G_FRAME:G_PHI] = frame_table(i)
    return out.astype(np.float32)


def lon_table():
    out = np.zeros((N_LON, 8, NC))
    for q in range(N_LON):
        ph = phi_of(q * NC + np.arange(NC))
        out[q, 0], out[q, 1] = np.sin(ph), np.cos(ph)
        for side in range(2):
            _, c = lane_rows(2 * side)
            ph = phi_of(q * NC + (c - 2 if side == 0 else c + NC - 4))
            out[q, 2 + 2 * side], out[q, 3 + 2 * side] = np.sin(ph), np.cos(ph)
    return out.astype(np.float32)


class Geo:
    def __init__(self, geo_ref, sin, cos, cot, isin, sphi, cphi, yang):
        self.rinv = geo_ref[G_RAD : G_RAD + SH, :]
        self.ratio = geo_ref[G_RAD + SH : G_RAD + 2 * SH, :]
        self.grav = geo_ref[G_RAD + 2 * SH : G_RAD + 3 * SH, :]
        self.ct = self.rinv * (0.5 / D_TH)
        self.cp = self.rinv * (0.5 / D_PH) * isin
        self.cotr = self.rinv * cot
        self.n_r = (1.0 - yang) * cos + yang * (sin * sphi)
        self.n_t = (yang - 1.0) * sin + yang * (cos * sphi)
        self.n_p = yang * cphi


def lane_roll(x, shift):
    return pltpu.roll(x, shift % NC, 1)


def diff_p(x):
    return lane_roll(x, -1) - lane_roll(x, 1)


def diff_r(x, ghost, edges):
    first, last = edges
    return jnp.where(last, ghost, pltpu.roll(x, SH - 1, 0)) - jnp.where(
        first, ghost, pltpu.roll(x, 1, 0)
    )


def cross(a, b):
    return (
        a[1] * b[2] - a[2] * b[1],
        a[2] * b[0] - a[0] * b[2],
        a[0] * b[1] - a[1] * b[0],
    )


def stage_one(u, diff_t, geo, edges, full):
    rinv, ct, cp, cotr = geo.rinv, geo.ct, geo.cp, geo.cotr
    cr = 0.5 / D_R
    rho, pr = u[0], u[1]
    v, b = u[2:5], u[5:8]

    def d_r(x):
        return diff_r(x, x, edges) * cr

    def d_t(fn):
        return diff_t(fn) * ct

    def d_p(x):
        return diff_p(x) * cp

    bt_r, bp_r = d_r(b[1]), d_r(b[2])
    j_r = d_t(lambda w: w[7]) + b[2] * cotr - d_p(b[1])
    jt_ang = d_p(b[0]) - b[2] * rinv
    jp_ang = b[1] * rinv - d_t(lambda w: w[5])
    jj = (j_r, jt_ang - bp_r, bt_r + jp_ang)
    vr = [d_r(x) for x in v]
    vt = [d_t(lambda w, i=i: w[2 + i]) for i in range(3)]
    vp = [d_p(x) for x in v]
    wt_ang = vp[0] - v[2] * rinv
    wp_ang = v[1] * rinv - vt[0]
    ww = (vt[2] + v[2] * cotr - vp[1], wt_ang - vr[2], vr[1] + wp_ang)
    e_ang = 2.0 * v[0] * rinv + vt[1] + v[1] * cotr + vp[2]
    ee = vr[0] + e_ang
    vxb = cross(v, b)
    el = [vxb[i] - MU * jj[i] for i in range(3)]
    ratio = geo.ratio
    level = list(ww) + [ee] + el
    level += [
        wt_ang * ratio,
        wp_ang * ratio,
        e_ang * ratio,
        vxb[1] - MU * (jt_ang * ratio),
        vxb[2] - MU * (jp_ang * ratio),
    ]
    if not full:
        return level, None, None
    fr, fp = rho * v[0], rho * v[2]
    mass = (
        d_r(fr)
        + 2.0 * fr * rinv
        + d_t(lambda w: w[0] * w[3])
        + rho * v[1] * cotr
        + d_p(fp)
    )
    gp = (d_r(pr), d_t(lambda w: w[1]), d_p(pr))
    press = -(v[0] * gp[0] + v[1] * gp[1] + v[2] * gp[2]) - GAMMA * pr * ee
    lor = cross(jj, b)
    spin = cross(v, (geo.n_r, geo.n_t, geo.n_p))
    curv = (
        -(v[1] * v[1] + v[2] * v[2]) * rinv,
        v[0] * v[1] * rinv - v[2] * v[2] * cotr,
        v[0] * v[2] * rinv + v[1] * v[2] * cotr,
    )
    irho = DT / rho
    rest = []
    for i in range(3):
        adv = v[0] * vr[i] + v[1] * vt[i] + v[2] * vp[i] + curv[i]
        x = (lor[i] - gp[i]) * irho - DT * adv + (2.0 * OMEGA * DT) * spin[i]
        rest.append(x - geo.grav if i == 0 else x)
    rest.append(irho * MU)
    return level, rest, (-DT * mass, DT * press)


def stage_two(q, diff_t, rest, geo, edges):
    rinv, ct, cp, cotr = geo.rinv, geo.ct, geo.cp, geo.cotr
    cr = 0.5 / D_R

    def d_r(i, g):
        return diff_r(q[i], q[g], edges) * cr

    def d_t(i):
        return diff_t(i) * ct

    def d_p(i):
        return diff_p(q[i]) * cp

    def curl(o, gt, gp):
        return (
            d_t(o + 2) + q[o + 2] * cotr - d_p(o + 1),
            d_p(o) - d_r(o + 2, gp) - q[o + 2] * rinv,
            d_r(o + 1, gt) + q[o + 1] * rinv - d_t(o),
        )

    cw = curl(0, 7, 8)
    grad_e = (d_r(3, 9), d_t(3), d_p(3))
    ce = curl(4, 10, 11)
    acc = [rest[i] + rest[3] * (4.0 / 3.0 * grad_e[i] - cw[i]) for i in range(3)]
    return acc + [DT * ce[i] for i in range(3)]


def shell_edges():
    s = lax.broadcasted_iota(jnp.int32, (SH, NC), 0)
    return s == 0, s == SH - 1


def aligned(i):
    return i if isinstance(i, int) else pl.multiple_of(i, 8)


def tile(ref, i):
    return ref[pl.ds(aligned(i * SH), SH), :]


def put(ref, i, val):
    ref[pl.ds(aligned(i * SH), SH), :] = val


def row_values(geo_ref, e):
    return [geo_ref[pl.ds(e * ROW_SCALARS + j, 1), :] for j in range(ROW_SCALARS)]


def row_geo(geo_ref, e, yang):
    return Geo(
        geo_ref, *row_values(geo_ref, e), geo_ref[G_PHI : G_PHI + 1, :],
        geo_ref[G_PHI + 1 : G_PHI + 2, :], yang,
    )


def rows_one(fields, q_ref, r_ref, depth, geo, edges, slot, full):
    up, dn = fields(1), fields(-1)
    level, rest, scal = stage_one(fields(0), lambda fn: fn(up) - fn(dn), geo, edges, full)
    for i, x in enumerate(level):
        put(q_ref, i * depth + slot, x)
    if full:
        for i, x in enumerate(rest):
            put(r_ref, i * depth + slot, x)
    return scal


def rows_two(q_ref, r_ref, depth, geo, edges, slot):
    q = [tile(q_ref, i * depth + slot) for i in range(12)]

    def diff_t(i):
        return tile(q_ref, i * depth + slot + 1) - tile(q_ref, i * depth + slot - 1)

    rest = [tile(r_ref, i * depth + slot) for i in range(4)]
    return stage_two(q, diff_t, rest, geo, edges)


def is_even(axis):
    return lax.rem(lax.axis_index(axis), 2) == 0


def native_row(f, k):
    return pl.ds(f * (SH * NR) + k, SH, stride=NR)


def donor_kernel(sc_hbm, ve_hbm, cr_hbm, cc_hbm, sw_hbm, rs_hbm, lat_hbm, lon_hbm,
                 pay_ref, pair_ref, other_ref, own_ref, geo_ref, idx_ref,
                 blk, cr, cc, sw, rs, s_all, c_hi, c_lo, sent_a, sent_b, sems):
    lat, lon = lax.axis_index("lat"), lax.axis_index("lon")
    n_sc = 2 * SH * NR
    moves = [
        (cr_hbm.at[0, 0], cr),
        (cc_hbm.at[0, 0], cc),
        (sw_hbm.at[:, 0, 0], sw),
        (rs_hbm, rs),
        (lat_hbm.at[lat], geo_ref.at[0:G_PHI]),
        (lon_hbm.at[lon], geo_ref.at[G_PHI:G_ALL]),
        (sc_hbm, blk.at[0:n_sc]),
        (ve_hbm, blk.at[n_sc : 4 * n_sc]),
    ]
    copies = [pltpu.make_async_copy(a, b, sems.at[i]) for i, (a, b) in enumerate(moves)]
    for c in copies:
        c.start()
    for c in copies[:3]:
        c.wait()
    tables = [cr[...].astype(F32), cc[...].astype(F32), sw[0], sw[1]]
    lane = lax.broadcasted_iota(jnp.int32, (N_LON, NC), 1).astype(F32)
    for j in range(CAP):
        a, b, wt, wp = [jnp.broadcast_to(x[:, j : j + 1], (N_LON, NC)) for x in tables]
        along = jnp.where(lane == b, 1.0 - wp, jnp.where(lane == b + 1.0, wp, 0.0))
        first, second = along * (1.0 - wt), along * wt
        here = slice(N_LON * j, N_LON * j + N_LON)
        below = slice(N_LON * (CAP + j), N_LON * (CAP + j) + N_LON)
        for k in range(NR):
            s = jnp.where(a == float(k), first, jnp.where(a == float(k - 1), second, 0.0))
            hi = s.astype(BF16)
            s_all[here, k * NC : (k + 1) * NC] = hi
            s_all[below, k * NC : (k + 1) * NC] = (s - hi.astype(F32)).astype(BF16)
    for c in copies[3:]:
        c.wait()
    at = geo_ref[G_FRAME : G_FRAME + 8, :].astype(jnp.int32)
    group = geo_ref[G_FRAME + 8 : G_FRAME + 16, :]
    g = jnp.full((8, NC), -1, jnp.int32)
    for i in range(5):
        end = min((i + 1) * NC, rs.shape[2])
        src = rs[0, :, i * NC : end]
        if end - i * NC < NC:
            src = jnp.concatenate([src, jnp.zeros((1, (i + 1) * NC - end), jnp.int32)], axis=1)
        src = jnp.broadcast_to(src, (8, NC))
        g = jnp.where(group == float(i), jnp.take_along_axis(src, at, axis=1), g)
    idx_ref[...] = g
    sphi, cphi = geo_ref[G_PHI : G_PHI + 1, :], geo_ref[G_PHI + 1 : G_PHI + 2, :]
    for k in range(NR):
        u = [blk[native_row(f, k), :] for f in range(8)]
        for f in range(8):
            put(own_ref, f * NR + k, u[f])
        sin, cos = row_values(geo_ref, k + 2)[:2]
        c = [u[0], u[1]]
        for o in (2, 5):
            flat = u[o] * sin + u[o + 1] * cos
            c += [
                flat * cphi - u[o + 2] * sphi,
                flat * sphi + u[o + 2] * cphi,
                u[o] * cos - u[o + 1] * sin,
            ]
        c = jnp.concatenate(c, axis=0)
        hi = c.astype(BF16)
        c_hi[:, k * NC : (k + 1) * NC] = hi
        c_lo[:, k * NC : (k + 1) * NC] = (c - hi.astype(F32)).astype(BF16)

    last = jnp.where(is_even("lat"), NR - 2, 0)
    for ref, k0 in ((pair_ref, last), (other_ref, NR - 2 - last)):
        for f in range(8):
            for j in range(2):
                put(ref, f * 2 + j, tile(own_ref, f * NR + k0 + j))

    def dot(x, y):
        return lax.dot_general(
            x[...], y[...], (((1,), (1,)), ((), ())), preferred_element_type=F32
        )

    slots = CAP * N_LON
    both = dot(s_all, c_hi)
    sent = both[:slots] + both[slots:] + dot(s_all.at[:slots], c_lo)
    sent_a[...] = sent[:, 0:NC]
    sent_b[:, 0:64] = sent[:, NC : NC + 64]
    for t in range(N_LON):
        mine = pl.ds(t, CAP, stride=N_LON)
        part = sent_b[mine, :]
        pay_ref[t, 24:32, :] = jnp.zeros((8, NC), F32)
        pay_ref[t, 0:CAP, :] = sent_a[mine, :]
        pay_ref[t, 19:29, 0:64] = part[0:10, 0:64]
        pay_ref[t, 19:28, 64:128] = part[10:19, 0:64]


def row_of(own_ref, pair_ref, other_ref, f, e):
    if isinstance(e, int) and e < 2:
        at = f * 2 + e
        return jnp.where(is_even("lat"), tile(other_ref, at), tile(pair_ref, at))
    if isinstance(e, int) and e >= NR + 2:
        at = f * 2 + e - NR - 2
        return jnp.where(is_even("lat"), tile(pair_ref, at), tile(other_ref, at))
    return tile(own_ref, f * NR + e - 2)


def dense(fields, first, place):
    out = []
    for o in range(0, 8, 3):
        group = None
        for j, x in enumerate(fields[o : o + 3]):
            at = (first + 2 * j) % 6
            x = lane_roll(x, at - first)
            mine = (place == at) | (place == at + 1)
            group = x if group is None else jnp.where(mine, x, group)
        out.append(group)
    return out


def undense(group, first, j):
    return lane_roll(group, first - (first + 2 * j) % 6)


def pack_kernel(own_ref, top_ref, bot_ref, left_ref, right_ref, pair_ref, other_ref):
    lane = lax.broadcasted_iota(jnp.int32, (SH, NC), 1)
    place = lane % 6
    lefts, rights = [], []
    for f in range(8):
        left = jnp.zeros((SH, NC), F32)
        right = jnp.zeros((SH, NC), F32)
        for e in range(EXT):
            x = lane_roll(row_of(own_ref, top_ref, bot_ref, f, e), 6 * e + 2)
            base = 6 * e
            left = jnp.where((lane >= base + 2) & (lane < base + 6), x, left)
            if e == 0:
                right = jnp.where((lane >= NC - 2) | (lane < 2), x, right)
            else:
                right = jnp.where((lane >= base - 2) & (lane < base + 2), x, right)
        put(left_ref, f, left)
        put(right_ref, f, right)
        lefts.append(left)
        rights.append(right)
    even = is_even("lon")
    for i, (x, y) in enumerate(zip(dense(lefts, 2, place), dense(rights, 0, place))):
        put(pair_ref, i, jnp.where(even, y, x))
        put(other_ref, i, jnp.where(even, x, y))


def main_kernel(own_ref, top_ref, bot_ref, geo_ref, out_hbm, near_ref, out_ref, q_ref, r_ref, sems):
    k0 = jnp.where(lax.axis_index("lat") == 0, 0, NR - 4)
    for f in range(8):
        for j in range(4):
            put(near_ref, f * 4 + j, tile(own_ref, f * NR + k0 + j))
    yang = lax.axis_index("panel").astype(F32)
    edges = shell_edges()

    def one(e, full):
        def fields(step):
            return [row_of(own_ref, top_ref, bot_ref, f, e + step) for f in range(8)]

        geo = row_geo(geo_ref, e, yang)
        scal = rows_one(fields, q_ref, r_ref, EXT, geo, edges, e, full)
        if full:
            for i in range(2):
                put(out_ref, (e - 2) * 8 + i, scal[i])

    def two(e):
        vec = rows_two(q_ref, r_ref, EXT, row_geo(geo_ref, e, yang), edges, e)
        for i in range(6):
            put(out_ref, (e - 2) * 8 + 2 + i, vec[i])

    one(1, False)
    one(2, True)
    sends = []
    quarter = NR // 4
    for part in range(4):
        first = 3 + part * quarter

        @pl.loop(first, min(first + quarter, NR + 1))
        def _(e):
            one(e, True)
            two(e - 1)

        if part == 3:
            one(NR + 1, True)
            two(NR)
            one(NR + 2, False)
            two(NR + 1)
        span = pl.ds(part * quarter * 8 * SH, quarter * 8 * SH)
        sends.append(
            pltpu.make_async_copy(out_ref.at[span], out_hbm.at[span], sems.at[part])
        )
        sends[-1].start()
    for c in sends:
        c.wait()


def to_spherical(x, y, z, sin, cos, sphi, cphi):
    flat = x * cphi + y * sphi
    return [flat * sin + z * cos, flat * cos - z * sin, y * cphi - x * sphi]


def border_fields(w, sin, cos, sphi, cphi):
    out = [w[0], w[1]]
    for o in (2, 5):
        out += to_spherical(-w[o], w[o + 2], w[o + 1], sin, cos, sphi, cphi)
    return out


STRIP = 6


def edge_kernel(near_ref, left_ref, right_ref, pair_ref, other_ref,
                don_ref, idx_ref, geo_ref, int_hbm, osc_hbm, ove_hbm,
                wide_ref, thin_ref, int_ref, out_ref, bord_ref, u_ref, q_ref, r_ref, sems):
    yang = lax.axis_index("panel").astype(F32)
    lat = lax.axis_index("lat")
    lon = lax.axis_index("lon")
    edges = shell_edges()
    row_edge = (lat == 0) | (lat == N_LAT - 1)
    col_edge = (lon == 0) | (lon == N_LON - 1)
    per = SH * NR
    fetch = pltpu.make_async_copy(int_hbm, int_ref, sems.at[8])
    fetch.start()
    @pl.when(row_edge | col_edge)
    def _():
        for q in range(N_LON):
            wide_ref[24 * q : 24 * q + 24, :] = don_ref[CHUNK * q : CHUNK * q + 24, :]
            rest = don_ref[CHUNK * q + 16 : CHUNK * q + CHUNK, 0:64]
            turned = don_ref[CHUNK * q + 16 : CHUNK * q + CHUNK, 64:NC]
            thin_ref[24 * q + 16 : 24 * q + 24, :] = jnp.zeros((8, NC), F32)
            thin_ref[24 * q : 24 * q + 10, 0:64] = rest[3:13]
            thin_ref[24 * q + 10 : 24 * q + 19, 0:64] = turned[3:12]
        recv = jnp.concatenate(
            [jnp.transpose(wide_ref[...]), jnp.transpose(thin_ref[...])[0:64]], axis=0
        )
        hi = recv.astype(BF16)
        lo = (recv - hi.astype(F32)).astype(BF16)
        at = lax.broadcasted_iota(jnp.int32, (N_LON * 24, NC), 0)
        for col in range(4):
            g = idx_ref[col : col + 1, :]
            donor = jnp.floor((g.astype(F32) + 0.5) * (1.0 / CAP)).astype(jnp.int32)
            where = jnp.where(g >= 0, g + donor * (24 - CAP), -1)
            hot = jnp.where(at == where, 1.0, 0.0).astype(BF16)
            bord_ref[:, col * NC : (col + 1) * NC] = jnp.dot(
                hi, hot, preferred_element_type=F32
            ) + jnp.dot(lo, hot, preferred_element_type=F32)

    def border(col, sin, cos, sphi, cphi):
        w = [bord_ref[f * SH : f * SH + SH, col * NC : (col + 1) * NC] for f in range(8)]
        return border_fields(w, sin, cos, sphi, cphi)

    lane = lax.broadcasted_iota(jnp.int32, (SH, NC), 1)
    place = lane % 6
    merged = None
    for side in range(2):
        own = left_ref if side == 0 else right_ref
        paired = is_even("lon") if side == 1 else ~is_even("lon")
        theirs = (place < 2) if side == 0 else ((place == 2) | (place == 3))
        at = G_PACK + 4 * side
        th = [geo_ref[at + j : at + j + 1, :] for j in range(4)]
        at = G_PHI + 2 + 2 * side
        ph = [geo_ref[at + j : at + j + 1, :] for j in range(2)]
        g = jnp.broadcast_to(idx_ref[2 + side : 3 + side, :], (SH, NC))
        donated = border(2 + side, th[0], th[1], ph[0], ph[1])
        u = []
        for f in range(8):
            x = jnp.where(paired, tile(pair_ref, f // 3), tile(other_ref, f // 3))
            x = undense(x, 2 * side, f % 3)
            x = jnp.where(theirs, x, tile(own, f))
            u.append(jnp.where(g >= 0, donated[f], x))
        geo = Geo(geo_ref, *th, *ph, yang)

        def diff_six(x):
            return lane_roll(x, -6) - lane_roll(x, 6)

        level, rest, scal = stage_one(u, lambda fn: diff_six(fn(u)), geo, edges, True)
        vec = stage_two(level, lambda i: diff_six(level[i]), rest, geo, edges)
        vals = list(scal) + vec
        if side == 0:
            merged = vals
        else:
            merged = [jnp.where(place < 2, y, x) for x, y in zip(merged, vals)]
    for f in range(8):
        put(u_ref, 8 * STRIP + f, merged[f])

    @pl.when(row_edge)
    def _():
        top = lat == 0
        e0 = jnp.where(top, 0, NR - 2)
        for i in range(2):
            sc = row_values(geo_ref, jnp.where(top, i, NR + 2 + i))
            phi = [geo_ref[G_PHI + j : G_PHI + j + 1, :] for j in range(2)]
            w = border(i, sc[0], sc[1], phi[0], phi[1])
            for f in range(8):
                put(u_ref, f * STRIP + jnp.where(top, i, 4 + i), w[f])
        for j in range(4):
            for f in range(8):
                x = tile(near_ref, f * 4 + j)
                put(u_ref, f * STRIP + jnp.where(top, 2 + j, j), x)

        for slot in (1, 2, 3, 4):
            def fields(step, slot=slot):
                return [tile(u_ref, f * STRIP + slot + step) for f in range(8)]

            full = slot in (2, 3)
            geo = row_geo(geo_ref, e0 + slot, yang)
            scal = rows_one(fields, q_ref, r_ref, STRIP, geo, edges, slot, full)
            if full:
                for i in range(2):
                    put(r_ref, (4 + i) * STRIP + slot, scal[i])
        for slot in (2, 3):
            vec = rows_two(q_ref, r_ref, STRIP, row_geo(geo_ref, e0 + slot, yang), edges, slot)
            for i in range(6):
                put(r_ref, (6 + i) * STRIP + slot, vec[i])

    edge_lane = (lane < 2) | (lane >= NC - 2)
    sends = []
    fetch.wait()
    for f in range(8):
        cols = tile(u_ref, 8 * STRIP + f)
        for k in range(NR):
            x = lane_roll(cols, -(6 * (k + 2) + 2))
            out_ref[native_row(f, k), :] = jnp.where(edge_lane, x, tile(int_ref, k * 8 + f))

        @pl.when(row_edge)
        def _(f=f):
            k0 = jnp.where(lat == 0, 0, NR - 2)
            for j in range(2):
                at = native_row(f, k0 + j)
                val = tile(r_ref, (4 + f) * STRIP + 2 + j)
                out_ref[at, :] = jnp.where(edge_lane, out_ref[at, :], val)

        dst = osc_hbm.at[pl.ds(f * per, per)] if f < 2 else ove_hbm.at[pl.ds((f - 2) * per, per)]
        sends.append(pltpu.make_async_copy(out_ref.at[pl.ds(f * per, per)], dst, sems.at[f]))
        sends[-1].start()
    for c in sends:
        c.wait()


VM = pl.BlockSpec(memory_space=pltpu.VMEM)
HBM = pl.BlockSpec(memory_space=pltpu.HBM)
PINNED = pl.BlockSpec(memory_space=pltpu.HBM)


def call(kernel, ins, outs, scratch, name, flops, mib):
    return pl.pallas_call(
        kernel,
        out_shape=[
            pltpu.HBM(s, t) if m is PINNED else jax.ShapeDtypeStruct(s, t) for s, t, m in outs
        ],
        in_specs=ins,
        out_specs=[o[2] for o in outs],
        scratch_shapes=scratch,
        name=name,
        compiler_params=pltpu.CompilerParams(vmem_limit_bytes=mib * 1024 * 1024),
        cost_estimate=pl.CostEstimate(flops=flops, bytes_accessed=100000, transcendentals=0),
    )


def rows(n):
    return pltpu.VMEM((n * SH, NC), F32)


def swapped(x, axis, first):
    n = lax.axis_size(axis)
    pairs = [(i, (i + 1) % n) for i in range(first, n, 2)]
    return lax.ppermute(x, axis, pairs + [(b, a) for a, b in pairs])


def body(scalars, vectors, corner_rows, corner_cols, send_weights, recv_source):
    sc = scalars.reshape(2 * SH * NR, NC)
    ve = vectors.reshape(6 * SH * NR, NC)
    halo = ((8 * 2 * SH, NC), F32, VM)
    pack = ((8 * SH, NC), F32, VM)
    block = ((8 * NR * SH, NC), F32, VM)
    table = pltpu.VMEM((N_LON, CAP), jnp.int32)

    def in_hbm(*arrays):
        return [pltpu.with_memory_space_constraint(a, pltpu.HBM) for a in arrays]

    pay, low, high, own, geo, idx = call(
        donor_kernel, [HBM] * 8,
        [
            ((N_LON, CHUNK, NC), F32, VM), halo, halo, block,
            ((G_ALL, NC), F32, VM), ((8, NC), jnp.int32, VM),
        ],
        [
            rows(8 * NR), table, table,
            pltpu.VMEM((2, N_LON, CAP), F32),
            pltpu.VMEM((1, 1, 592), jnp.int32),
            pltpu.VMEM((2 * CAP * N_LON, NR * NC), BF16),
            pltpu.VMEM((8 * SH, NR * NC), BF16),
            pltpu.VMEM((8 * SH, NR * NC), BF16),
            pltpu.VMEM((CAP * N_LON, NC), F32),
            pltpu.VMEM((CAP * N_LON, NC), F32),
            pltpu.SemaphoreType.DMA((8,)),
        ],
        "donor", 400000000, 20,
    )(*in_hbm(sc, ve, corner_rows, corner_cols, send_weights, recv_source,
              jnp.asarray(lat_table()), jnp.asarray(lon_table())))
    pay = lax.ppermute(pay, "panel", [(0, 1), (1, 0)])
    don = lax.all_to_all(pay, "lon", 0, 0, tiled=True).reshape(N_LON * CHUNK, NC)
    low, high = swapped(low, "lat", 0), swapped(high, "lat", 1)
    thin = ((3 * SH, NC), F32, VM)
    left, right, near_lon, far_lon = call(pack_kernel, [VM] * 3, [pack, pack, thin, thin], [], "packs", 50000000000, 12)(
        own, low, high
    )
    near_lon, far_lon = swapped(near_lon, "lon", 0), swapped(far_lon, "lon", 1)
    inner, near = call(
        main_kernel, [VM] * 4, [block[:2] + (PINNED,), ((8 * 4 * SH, NC), F32, VM)],
        [rows(8 * NR), rows(12 * EXT), rows(4 * EXT), pltpu.SemaphoreType.DMA((4,))],
        "interior", 300000, 16,
    )(own, low, high, geo)
    osc, ove = call(
        edge_kernel, [VM] * 8 + [HBM],
        [(sc.shape, F32, HBM), (ve.shape, F32, HBM)],
        [
            rows(N_LON), rows(N_LON), rows(8 * NR), rows(8 * NR),
            pltpu.VMEM((8 * SH, 4 * NC), F32),
            rows(8 * STRIP + 8), rows(12 * STRIP), rows(12 * STRIP),
            pltpu.SemaphoreType.DMA((9,)),
        ],
        "edges", 10000000, 16,
    )(near, left, right, near_lon, far_lon, don, idx, geo, *in_hbm(inner))
    return osc.reshape(scalars.shape), ove.reshape(vectors.shape)


def solution(mesh):
    return jax.shard_map(
        body,
        mesh=mesh,
        in_specs=(
            P("panel", None, None, "lat", "lon"),
            P("panel", None, None, "lat", "lon"),
            P("lat", "lon", None, None),
            P("lat", "lon", None, None),
            P(None, "lat", "lon", None, None),
            P("lat", "lon", None),
        ),
        out_specs=(P("panel", None, None, "lat", "lon"), P("panel", None, None, "lat", "lon")),
        check_vma=False,
    )
```

```python
import math

import jax
import jax.numpy as jnp
import numpy as np
from jax import lax
from jax.experimental import pallas as pl
from jax.experimental.pallas import tpu as pltpu
from jax.sharding import PartitionSpec as P

GAMMA = 5.0 / 3.0
F32 = jnp.float32
BF16 = jnp.bfloat16
SH = 24
NR = 16
NC = 128
N_LAT = 8
N_LON = 16
CAP = 19
CHUNK = 32
EXT = NR + 4
ROW_SCALARS = 4

D_TH = 0.5 * math.pi / (NR * N_LAT)
D_PH = 1.5 * math.pi / (NC * N_LON)
D_R = 0.6 * D_TH
DT = 0.3 * min(D_R, 0.6 * math.sin(0.25 * math.pi - 2.0 * D_TH) * D_PH)
MU = DT / 0.9
GRAV = 0.036 / DT
OMEGA = 0.05 / DT


def theta_of(k):
    return 0.25 * math.pi + (k + 0.5) * D_TH


def phi_of(m):
    return -0.75 * math.pi + (m + 0.5) * D_PH


def lane_rows(shift):
    lane = (np.arange(NC) + shift) % NC
    return lane // 6, lane % 6


G_ROWS = 0
G_RAD = EXT * ROW_SCALARS
G_PACK = G_RAD + 3 * SH
G_FRAME = G_PACK + 8
G_PHI = G_FRAME + 16
G_ALL = G_PHI + 8


def frame_table(i):
    wide = NC + 4
    at = np.full((4, NC), -1)
    row = 0 if i == 0 else 2
    for j in range(2):
        at[j] = (row + j) * wide + 2 + np.arange(NC)
    for side in range(2):
        r, c = lane_rows(2 * side)
        for lane in range(NC):
            col = c[lane] if side == 0 else NC - 2 + c[lane]
            if r[lane] in (0, 1):
                at[2 + side, lane] = r[lane] * wide + col
            elif r[lane] in (EXT - 2, EXT - 1):
                at[2 + side, lane] = (r[lane] - NR) * wide + col
            elif r[lane] < EXT and side == 0 and c[lane] < 2:
                at[2, lane] = 4 * wide + 2 * (r[lane] - 2) + c[lane]
            elif r[lane] < EXT and side == 1 and c[lane] >= 4:
                at[3, lane] = 4 * wide + 2 * NR + 2 * (r[lane] - 2) + c[lane] - 4
    out = np.zeros((16, NC))
    out[8:] = -1
    out[0:4] = np.where(at >= 0, at % NC, 0)
    out[8:12] = np.where(at >= 0, at // NC, -1)
    return out


def lat_table():
    out = np.zeros((N_LAT, G_PHI, NC))
    s = np.arange(SH, dtype=np.float64)
    r = 0.6 + (s + 0.5) * D_R
    ratio = np.ones(SH)
    ratio[0] = r[0] / (0.6 - 0.5 * D_R)
    ratio[-1] = r[-1] / (0.6 + (SH + 0.5) * D_R)
    out[:, G_RAD:G_PACK] = np.concatenate([1.0 / r, ratio, DT * GRAV / (r * r)])[:, None]

    def four(th):
        return np.stack([np.sin(th), np.cos(th), np.cos(th) / np.sin(th), 1.0 / np.sin(th)])

    for i in range(N_LAT):
        th = theta_of(i * NR - 2 + np.arange(EXT))
        out[i, G_ROWS:G_RAD] = four(th).T.reshape(-1)[:, None]
        for side in range(2):
            rr, _ = lane_rows(2 * side)
            at = G_PACK + 4 * side
            out[i, at : at + 4] = four(theta_of(i * NR - 2 + np.minimum(rr, EXT - 1)))
        out[i, G_FRAME:G_PHI] = frame_table(i)
    return out.astype(np.float32)


def lon_table():
    out = np.zeros((N_LON, 8, NC))
    for q in range(N_LON):
        ph = phi_of(q * NC + np.arange(NC))
        out[q, 0], out[q, 1] = np.sin(ph), np.cos(ph)
        for side in range(2):
            _, c = lane_rows(2 * side)
            ph = phi_of(q * NC + (c - 2 if side == 0 else c + NC - 4))
            out[q, 2 + 2 * side], out[q, 3 + 2 * side] = np.sin(ph), np.cos(ph)
    return out.astype(np.float32)


class Geo:
    def __init__(self, geo_ref, sin, cos, cot, isin, sphi, cphi, yang):
        self.rinv = geo_ref[G_RAD : G_RAD + SH, :]
        self.ratio = geo_ref[G_RAD + SH : G_RAD + 2 * SH, :]
        self.grav = geo_ref[G_RAD + 2 * SH : G_RAD + 3 * SH, :]
        self.ct = self.rinv * (0.5 / D_TH)
        self.cp = self.rinv * (0.5 / D_PH) * isin
        self.cotr = self.rinv * cot
        self.n_r = (1.0 - yang) * cos + yang * (sin * sphi)
        self.n_t = (yang - 1.0) * sin + yang * (cos * sphi)
        self.n_p = yang * cphi


def lane_roll(x, shift):
    return pltpu.roll(x, shift % NC, 1)


def diff_p(x):
    return lane_roll(x, -1) - lane_roll(x, 1)


def diff_r(x, ghost, edges):
    first, last = edges
    return jnp.where(last, ghost, pltpu.roll(x, SH - 1, 0)) - jnp.where(
        first, ghost, pltpu.roll(x, 1, 0)
    )


def cross(a, b):
    return (
        a[1] * b[2] - a[2] * b[1],
        a[2] * b[0] - a[0] * b[2],
        a[0] * b[1] - a[1] * b[0],
    )


def stage_one(u, diff_t, geo, edges, full):
    rinv, ct, cp, cotr = geo.rinv, geo.ct, geo.cp, geo.cotr
    cr = 0.5 / D_R
    rho, pr = u[0], u[1]
    v, b = u[2:5], u[5:8]

    def d_r(x):
        return diff_r(x, x, edges) * cr

    def d_t(fn):
        return diff_t(fn) * ct

    def d_p(x):
        return diff_p(x) * cp

    bt_r, bp_r = d_r(b[1]), d_r(b[2])
    j_r = d_t(lambda w: w[7]) + b[2] * cotr - d_p(b[1])
    jt_ang = d_p(b[0]) - b[2] * rinv
    jp_ang = b[1] * rinv - d_t(lambda w: w[5])
    jj = (j_r, jt_ang - bp_r, bt_r + jp_ang)
    vr = [d_r(x) for x in v]
    vt = [d_t(lambda w, i=i: w[2 + i]) for i in range(3)]
    vp = [d_p(x) for x in v]
    wt_ang = vp[0] - v[2] * rinv
    wp_ang = v[1] * rinv - vt[0]
    ww = (vt[2] + v[2] * cotr - vp[1], wt_ang - vr[2], vr[1] + wp_ang)
    e_ang = 2.0 * v[0] * rinv + vt[1] + v[1] * cotr + vp[2]
    ee = vr[0] + e_ang
    vxb = cross(v, b)
    el = [vxb[i] - MU * jj[i] for i in range(3)]
    ratio = geo.ratio
    level = list(ww) + [ee] + el
    level += [
        wt_ang * ratio,
        wp_ang * ratio,
        e_ang * ratio,
        vxb[1] - MU * (jt_ang * ratio),
        vxb[2] - MU * (jp_ang * ratio),
    ]
    if not full:
        return level, None, None
    fr, fp = rho * v[0], rho * v[2]
    mass = (
        d_r(fr)
        + 2.0 * fr * rinv
        + d_t(lambda w: w[0] * w[3])
        + rho * v[1] * cotr
        + d_p(fp)
    )
    gp = (d_r(pr), d_t(lambda w: w[1]), d_p(pr))
    press = -(v[0] * gp[0] + v[1] * gp[1] + v[2] * gp[2]) - GAMMA * pr * ee
    lor = cross(jj, b)
    spin = cross(v, (geo.n_r, geo.n_t, geo.n_p))
    curv = (
        -(v[1] * v[1] + v[2] * v[2]) * rinv,
        v[0] * v[1] * rinv - v[2] * v[2] * cotr,
        v[0] * v[2] * rinv + v[1] * v[2] * cotr,
    )
    irho = DT / rho
    rest = []
    for i in range(3):
        adv = v[0] * vr[i] + v[1] * vt[i] + v[2] * vp[i] + curv[i]
        x = (lor[i] - gp[i]) * irho - DT * adv + (2.0 * OMEGA * DT) * spin[i]
        rest.append(x - geo.grav if i == 0 else x)
    rest.append(irho * MU)
    return level, rest, (-DT * mass, DT * press)


def stage_two(q, diff_t, rest, geo, edges):
    rinv, ct, cp, cotr = geo.rinv, geo.ct, geo.cp, geo.cotr
    cr = 0.5 / D_R

    def d_r(i, g):
        return diff_r(q[i], q[g], edges) * cr

    def d_t(i):
        return diff_t(i) * ct

    def d_p(i):
        return diff_p(q[i]) * cp

    def curl(o, gt, gp):
        return (
            d_t(o + 2) + q[o + 2] * cotr - d_p(o + 1),
            d_p(o) - d_r(o + 2, gp) - q[o + 2] * rinv,
            d_r(o + 1, gt) + q[o + 1] * rinv - d_t(o),
        )

    cw = curl(0, 7, 8)
    grad_e = (d_r(3, 9), d_t(3), d_p(3))
    ce = curl(4, 10, 11)
    acc = [rest[i] + rest[3] * (4.0 / 3.0 * grad_e[i] - cw[i]) for i in range(3)]
    return acc + [DT * ce[i] for i in range(3)]


def shell_edges():
    s = lax.broadcasted_iota(jnp.int32, (SH, NC), 0)
    return s == 0, s == SH - 1


def aligned(i):
    return i if isinstance(i, int) else pl.multiple_of(i, 8)


def tile(ref, i):
    return ref[pl.ds(aligned(i * SH), SH), :]


def put(ref, i, val):
    ref[pl.ds(aligned(i * SH), SH), :] = val


def row_values(geo_ref, e):
    return [geo_ref[pl.ds(e * ROW_SCALARS + j, 1), :] for j in range(ROW_SCALARS)]


def row_geo(geo_ref, e, yang):
    return Geo(
        geo_ref, *row_values(geo_ref, e), geo_ref[G_PHI : G_PHI + 1, :],
        geo_ref[G_PHI + 1 : G_PHI + 2, :], yang,
    )


def rows_one(fields, q_ref, r_ref, depth, geo, edges, slot, full):
    up, dn = fields(1), fields(-1)
    level, rest, scal = stage_one(fields(0), lambda fn: fn(up) - fn(dn), geo, edges, full)
    for i, x in enumerate(level):
        put(q_ref, i * depth + slot, x)
    if full:
        for i, x in enumerate(rest):
            put(r_ref, i * depth + slot, x)
    return scal


def rows_two(q_ref, r_ref, depth, geo, edges, slot):
    q = [tile(q_ref, i * depth + slot) for i in range(12)]

    def diff_t(i):
        return tile(q_ref, i * depth + slot + 1) - tile(q_ref, i * depth + slot - 1)

    rest = [tile(r_ref, i * depth + slot) for i in range(4)]
    return stage_two(q, diff_t, rest, geo, edges)


def is_even(axis):
    return lax.rem(lax.axis_index(axis), 2) == 0


def native_row(f, k):
    return pl.ds(f * (SH * NR) + k, SH, stride=NR)


def donor_kernel(sc_hbm, ve_hbm, cr_hbm, cc_hbm, sw_hbm, rs_hbm, lat_hbm, lon_hbm,
                 pay_ref, pair_ref, other_ref, own_ref, geo_ref, idx_ref,
                 blk, cr, cc, sw, rs, s_all, c_hi, c_lo, sent_a, sent_b, chunk, sems):
    lat, lon = lax.axis_index("lat"), lax.axis_index("lon")
    n_sc = 2 * SH * NR
    moves = [
        (cr_hbm.at[0, 0], cr),
        (cc_hbm.at[0, 0], cc),
        (sw_hbm.at[:, 0, 0], sw),
        (rs_hbm, rs),
        (lat_hbm.at[lat], geo_ref.at[0:G_PHI]),
        (lon_hbm.at[lon], geo_ref.at[G_PHI:G_ALL]),
        (sc_hbm, blk.at[0:n_sc]),
        (ve_hbm, blk.at[n_sc : 4 * n_sc]),
    ]
    copies = [pltpu.make_async_copy(a, b, sems.at[i]) for i, (a, b) in enumerate(moves)]
    for c in copies:
        c.start()
    for c in copies[:3]:
        c.wait()
    tables = [cr[...].astype(F32), cc[...].astype(F32), sw[0], sw[1]]
    lane = lax.broadcasted_iota(jnp.int32, (N_LON, NC), 1).astype(F32)
    for j in range(CAP):
        a, b, wt, wp = [jnp.broadcast_to(x[:, j : j + 1], (N_LON, NC)) for x in tables]
        along = jnp.where(lane == b, 1.0 - wp, jnp.where(lane == b + 1.0, wp, 0.0))
        first, second = along * (1.0 - wt), along * wt
        here = slice(N_LON * j, N_LON * j + N_LON)
        below = slice(N_LON * (CAP + j), N_LON * (CAP + j) + N_LON)
        for k in range(NR):
            s = jnp.where(a == float(k), first, jnp.where(a == float(k - 1), second, 0.0))
            hi = s.astype(BF16)
            s_all[here, k * NC : (k + 1) * NC] = hi
            s_all[below, k * NC : (k + 1) * NC] = (s - hi.astype(F32)).astype(BF16)
    for c in copies[3:]:
        c.wait()
    at = geo_ref[G_FRAME : G_FRAME + 8, :].astype(jnp.int32)
    group = geo_ref[G_FRAME + 8 : G_FRAME + 16, :]
    g = jnp.full((8, NC), -1, jnp.int32)
    for i in range(5):
        end = min((i + 1) * NC, rs.shape[2])
        src = rs[0, :, i * NC : end]
        if end - i * NC < NC:
            src = jnp.concatenate([src, jnp.zeros((1, (i + 1) * NC - end), jnp.int32)], axis=1)
        src = jnp.broadcast_to(src, (8, NC))
        g = jnp.where(group == float(i), jnp.take_along_axis(src, at, axis=1), g)
    idx_ref[...] = g
    sphi, cphi = geo_ref[G_PHI : G_PHI + 1, :], geo_ref[G_PHI + 1 : G_PHI + 2, :]
    for k in range(NR):
        u = [blk[native_row(f, k), :] for f in range(8)]
        for f in range(8):
            put(own_ref, f * NR + k, u[f])
        sin, cos = row_values(geo_ref, k + 2)[:2]
        c = [u[0], u[1]]
        for o in (2, 5):
            flat = u[o] * sin + u[o + 1] * cos
            c += [
                flat * cphi - u[o + 2] * sphi,
                flat * sphi + u[o + 2] * cphi,
                u[o] * cos - u[o + 1] * sin,
            ]
        c = jnp.concatenate(c, axis=0)
        hi = c.astype(BF16)
        c_hi[:, k * NC : (k + 1) * NC] = hi
        c_lo[:, k * NC : (k + 1) * NC] = (c - hi.astype(F32)).astype(BF16)

    last = jnp.where(is_even("lat"), NR - 2, 0)
    for ref, k0 in ((pair_ref, last), (other_ref, NR - 2 - last)):
        for f in range(8):
            for j in range(2):
                put(ref, f * 2 + j, tile(own_ref, f * NR + k0 + j))

    def dot(x, y):
        return lax.dot_general(
            x[...], y[...], (((1,), (1,)), ((), ())), preferred_element_type=F32
        )

    slots = CAP * N_LON
    both = dot(s_all, c_hi)
    sent = both[:slots] + both[slots:] + dot(s_all.at[:slots], c_lo)
    sent_a[0:slots, :] = sent[:, 0:NC]
    sent_b[0:slots, 0:64] = sent[:, NC : NC + 64]
    for t in range(N_LON):
        mine = pl.ds(t, CAP, stride=N_LON)
        part = sent_b[mine, :]
        at = CHUNK * t
        chunk[at + 24 : at + 32, :] = jnp.zeros((8, NC), F32)
        chunk[at : at + CAP, :] = sent_a[mine, :]
        chunk[at + 19 : at + 29, 0:64] = part[0:10, 0:64]
        chunk[at + 19 : at + 28, 64:128] = part[10:19, 0:64]
        pay_ref[t] = chunk[at : at + CHUNK, :]


def row_of(own_ref, pair_ref, other_ref, f, e):
    if isinstance(e, int) and e < 2:
        at = f * 2 + e
        return jnp.where(is_even("lat"), tile(other_ref, at), tile(pair_ref, at))
    if isinstance(e, int) and e >= NR + 2:
        at = f * 2 + e - NR - 2
        return jnp.where(is_even("lat"), tile(pair_ref, at), tile(other_ref, at))
    return tile(own_ref, f * NR + e - 2)


def dense(fields, first, place):
    out = []
    for o in range(0, 8, 3):
        group = None
        for j, x in enumerate(fields[o : o + 3]):
            at = (first + 2 * j) % 6
            x = lane_roll(x, at - first)
            mine = (place == at) | (place == at + 1)
            group = x if group is None else jnp.where(mine, x, group)
        out.append(group)
    return out


def undense(group, first, j):
    return lane_roll(group, first - (first + 2 * j) % 6)


def pack_kernel(own_ref, top_ref, bot_ref, left_ref, right_ref, pair_ref, other_ref):
    lane = lax.broadcasted_iota(jnp.int32, (SH, NC), 1)
    place = lane % 6
    lefts, rights = [], []
    for f in range(8):
        left = jnp.zeros((SH, NC), F32)
        right = jnp.zeros((SH, NC), F32)
        for e in range(EXT):
            x = lane_roll(row_of(own_ref, top_ref, bot_ref, f, e), 6 * e + 2)
            base = 6 * e
            left = jnp.where((lane >= base + 2) & (lane < base + 6), x, left)
            if e == 0:
                right = jnp.where((lane >= NC - 2) | (lane < 2), x, right)
            else:
                right = jnp.where((lane >= base - 2) & (lane < base + 2), x, right)
        put(left_ref, f, left)
        put(right_ref, f, right)
        lefts.append(left)
        rights.append(right)
    even = is_even("lon")
    for i, (x, y) in enumerate(zip(dense(lefts, 2, place), dense(rights, 0, place))):
        put(pair_ref, i, jnp.where(even, y, x))
        put(other_ref, i, jnp.where(even, x, y))


def main_kernel(own_ref, top_ref, bot_ref, geo_ref, out_hbm, near_ref, out_ref, q_ref, r_ref, sems):
    k0 = jnp.where(lax.axis_index("lat") == 0, 0, NR - 4)
    for f in range(8):
        for j in range(4):
            put(near_ref, f * 4 + j, tile(own_ref, f * NR + k0 + j))
    yang = lax.axis_index("panel").astype(F32)
    edges = shell_edges()

    def one(e, full):
        def fields(step):
            return [row_of(own_ref, top_ref, bot_ref, f, e + step) for f in range(8)]

        geo = row_geo(geo_ref, e, yang)
        scal = rows_one(fields, q_ref, r_ref, EXT, geo, edges, e, full)
        if full:
            for i in range(2):
                put(out_ref, (e - 2) * 8 + i, scal[i])

    def two(e):
        vec = rows_two(q_ref, r_ref, EXT, row_geo(geo_ref, e, yang), edges, e)
        for i in range(6):
            put(out_ref, (e - 2) * 8 + 2 + i, vec[i])

    one(1, False)
    one(2, True)
    sends = []
    quarter = NR // 4
    for part in range(4):
        first = 3 + part * quarter

        @pl.loop(first, min(first + quarter, NR + 1))
        def _(e):
            one(e, True)
            two(e - 1)

        if part == 3:
            one(NR + 1, True)
            two(NR)
            one(NR + 2, False)
            two(NR + 1)
        span = pl.ds(part * quarter * 8 * SH, quarter * 8 * SH)
        sends.append(
            pltpu.make_async_copy(out_ref.at[span], out_hbm.at[span], sems.at[part])
        )
        sends[-1].start()
    for c in sends:
        c.wait()


def to_spherical(x, y, z, sin, cos, sphi, cphi):
    flat = x * cphi + y * sphi
    return [flat * sin + z * cos, flat * cos - z * sin, y * cphi - x * sphi]


def border_fields(w, sin, cos, sphi, cphi):
    out = [w[0], w[1]]
    for o in (2, 5):
        out += to_spherical(-w[o], w[o + 2], w[o + 1], sin, cos, sphi, cphi)
    return out


STRIP = 6


def edge_kernel(near_ref, left_ref, right_ref, pair_ref, other_ref,
                don_ref, idx_ref, geo_ref, int_hbm, osc_hbm, ove_hbm,
                wide_ref, thin_ref, int_ref, out_ref, bord_ref, u_ref, q_ref, r_ref, sems):
    yang = lax.axis_index("panel").astype(F32)
    lat = lax.axis_index("lat")
    lon = lax.axis_index("lon")
    edges = shell_edges()
    row_edge = (lat == 0) | (lat == N_LAT - 1)
    col_edge = (lon == 0) | (lon == N_LON - 1)
    per = SH * NR
    fetch = pltpu.make_async_copy(int_hbm, int_ref, sems.at[8])
    fetch.start()
    @pl.when(row_edge | col_edge)
    def _():
        for q in range(N_LON):
            wide_ref[24 * q : 24 * q + 24, :] = don_ref[CHUNK * q : CHUNK * q + 24, :]
            rest = don_ref[CHUNK * q + 16 : CHUNK * q + CHUNK, 0:64]
            turned = don_ref[CHUNK * q + 16 : CHUNK * q + CHUNK, 64:NC]
            thin_ref[24 * q + 16 : 24 * q + 24, :] = jnp.zeros((8, NC), F32)
            thin_ref[24 * q : 24 * q + 10, 0:64] = rest[3:13]
            thin_ref[24 * q + 10 : 24 * q + 19, 0:64] = turned[3:12]
        recv = jnp.concatenate(
            [jnp.transpose(wide_ref[...]), jnp.transpose(thin_ref[0 : 24 * N_LON, :])[0:64]], axis=0
        )
        hi = recv.astype(BF16)
        lo = (recv - hi.astype(F32)).astype(BF16)
        at = lax.broadcasted_iota(jnp.int32, (N_LON * 24, NC), 0)
        for col in range(4):
            g = idx_ref[col : col + 1, :]
            donor = jnp.floor((g.astype(F32) + 0.5) * (1.0 / CAP)).astype(jnp.int32)
            where = jnp.where(g >= 0, g + donor * (24 - CAP), -1)
            hot = jnp.where(at == where, 1.0, 0.0).astype(BF16)
            bord_ref[:, col * NC : (col + 1) * NC] = jnp.dot(
                hi, hot, preferred_element_type=F32
            ) + jnp.dot(lo, hot, preferred_element_type=F32)

    def border(col, sin, cos, sphi, cphi):
        w = [bord_ref[f * SH : f * SH + SH, col * NC : (col + 1) * NC] for f in range(8)]
        return border_fields(w, sin, cos, sphi, cphi)

    lane = lax.broadcasted_iota(jnp.int32, (SH, NC), 1)
    place = lane % 6
    merged = None
    for side in range(2):
        own = left_ref if side == 0 else right_ref
        paired = is_even("lon") if side == 1 else ~is_even("lon")
        theirs = (place < 2) if side == 0 else ((place == 2) | (place == 3))
        at = G_PACK + 4 * side
        th = [geo_ref[at + j : at + j + 1, :] for j in range(4)]
        at = G_PHI + 2 + 2 * side
        ph = [geo_ref[at + j : at + j + 1, :] for j in range(2)]
        g = jnp.broadcast_to(idx_ref[2 + side : 3 + side, :], (SH, NC))
        donated = border(2 + side, th[0], th[1], ph[0], ph[1])
        u = []
        for f in range(8):
            x = jnp.where(paired, tile(pair_ref, f // 3), tile(other_ref, f // 3))
            x = undense(x, 2 * side, f % 3)
            x = jnp.where(theirs, x, tile(own, f))
            u.append(jnp.where(g >= 0, donated[f], x))
        geo = Geo(geo_ref, *th, *ph, yang)

        def diff_six(x):
            return lane_roll(x, -6) - lane_roll(x, 6)

        level, rest, scal = stage_one(u, lambda fn: diff_six(fn(u)), geo, edges, True)
        vec = stage_two(level, lambda i: diff_six(level[i]), rest, geo, edges)
        vals = list(scal) + vec
        if side == 0:
            merged = vals
        else:
            merged = [jnp.where(place < 2, y, x) for x, y in zip(merged, vals)]
    for f in range(8):
        put(u_ref, 8 * STRIP + f, merged[f])

    @pl.when(row_edge)
    def _():
        top = lat == 0
        e0 = jnp.where(top, 0, NR - 2)
        for i in range(2):
            sc = row_values(geo_ref, jnp.where(top, i, NR + 2 + i))
            phi = [geo_ref[G_PHI + j : G_PHI + j + 1, :] for j in range(2)]
            w = border(i, sc[0], sc[1], phi[0], phi[1])
            for f in range(8):
                put(u_ref, f * STRIP + jnp.where(top, i, 4 + i), w[f])
        for j in range(4):
            for f in range(8):
                x = tile(near_ref, f * 4 + j)
                put(u_ref, f * STRIP + jnp.where(top, 2 + j, j), x)

        for slot in (1, 2, 3, 4):
            def fields(step, slot=slot):
                return [tile(u_ref, f * STRIP + slot + step) for f in range(8)]

            full = slot in (2, 3)
            geo = row_geo(geo_ref, e0 + slot, yang)
            scal = rows_one(fields, q_ref, r_ref, STRIP, geo, edges, slot, full)
            if full:
                for i in range(2):
                    put(r_ref, (4 + i) * STRIP + slot, scal[i])
        for slot in (2, 3):
            vec = rows_two(q_ref, r_ref, STRIP, row_geo(geo_ref, e0 + slot, yang), edges, slot)
            for i in range(6):
                put(r_ref, (6 + i) * STRIP + slot, vec[i])

    edge_lane = (lane < 2) | (lane >= NC - 2)
    sends = []
    fetch.wait()
    for f in range(8):
        cols = tile(u_ref, 8 * STRIP + f)
        for k in range(NR):
            x = lane_roll(cols, -(6 * (k + 2) + 2))
            out_ref[native_row(f, k), :] = jnp.where(edge_lane, x, tile(int_ref, k * 8 + f))

        @pl.when(row_edge)
        def _(f=f):
            k0 = jnp.where(lat == 0, 0, NR - 2)
            for j in range(2):
                at = native_row(f, k0 + j)
                val = tile(r_ref, (4 + f) * STRIP + 2 + j)
                out_ref[at, :] = jnp.where(edge_lane, out_ref[at, :], val)

        dst = osc_hbm.at[pl.ds(f * per, per)] if f < 2 else ove_hbm.at[pl.ds((f - 2) * per, per)]
        sends.append(pltpu.make_async_copy(out_ref.at[pl.ds(f * per, per)], dst, sems.at[f]))
        sends[-1].start()
    for c in sends:
        c.wait()


VM = pl.BlockSpec(memory_space=pltpu.VMEM)
HBM = pl.BlockSpec(memory_space=pltpu.HBM)
PINNED = pl.BlockSpec(memory_space=pltpu.HBM)


def call(kernel, ins, outs, scratch, name, flops, mib):
    return pl.pallas_call(
        kernel,
        out_shape=[
            pltpu.HBM(s, t) if m is PINNED else jax.ShapeDtypeStruct(s, t) for s, t, m in outs
        ],
        in_specs=ins,
        out_specs=[o[2] for o in outs],
        scratch_shapes=scratch,
        name=name,
        compiler_params=pltpu.CompilerParams(vmem_limit_bytes=mib * 1024 * 1024),
        cost_estimate=pl.CostEstimate(flops=flops, bytes_accessed=100000, transcendentals=0),
    )


def rows(n):
    return pltpu.VMEM((n * SH, NC), F32)


def swapped(x, axis, first):
    n = lax.axis_size(axis)
    pairs = [(i, (i + 1) % n) for i in range(first, n, 2)]
    return lax.ppermute(x, axis, pairs + [(b, a) for a, b in pairs])


def body(scalars, vectors, corner_rows, corner_cols, send_weights, recv_source):
    sc = scalars.reshape(2 * SH * NR, NC)
    ve = vectors.reshape(6 * SH * NR, NC)
    halo = ((8 * 2 * SH, NC), F32, VM)
    pack = ((8 * SH, NC), F32, VM)
    block = ((8 * NR * SH, NC), F32, VM)
    table = pltpu.VMEM((N_LON, CAP), jnp.int32)

    def in_hbm(*arrays):
        return [pltpu.with_memory_space_constraint(a, pltpu.HBM) for a in arrays]

    pay, low, high, own, geo, idx = call(
        donor_kernel, [HBM] * 8,
        [
            ((N_LON, CHUNK, NC), F32, VM), halo, halo, block,
            ((G_ALL, NC), F32, VM), ((8, NC), jnp.int32, VM),
        ],
        [
            rows(8 * NR), table, table,
            pltpu.VMEM((2, N_LON, CAP), F32),
            pltpu.VMEM((1, 1, 592), jnp.int32),
            pltpu.VMEM((2 * CAP * N_LON, NR * NC), BF16),
            pltpu.VMEM((8 * SH, NR * NC), BF16),
            pltpu.VMEM((8 * SH, NR * NC), BF16),
            rows(N_LON), rows(N_LON),
            pltpu.VMEM((CHUNK * (N_LON + 1), NC), F32),
            pltpu.SemaphoreType.DMA((8,)),
        ],
        "donor", 400000000, 20,
    )(*in_hbm(sc, ve, corner_rows, corner_cols, send_weights, recv_source,
              jnp.asarray(lat_table()), jnp.asarray(lon_table())))
    pay = lax.ppermute(pay, "panel", [(0, 1), (1, 0)])
    don = lax.all_to_all(pay, "lon", 0, 0, tiled=True).reshape(N_LON * CHUNK, NC)
    low, high = swapped(low, "lat", 0), swapped(high, "lat", 1)
    thin = ((3 * SH, NC), F32, VM)
    left, right, near_lon, far_lon = call(pack_kernel, [VM] * 3, [pack, pack, thin, thin], [], "packs", 50000000000, 12)(
        own, low, high
    )
    near_lon, far_lon = swapped(near_lon, "lon", 0), swapped(far_lon, "lon", 1)
    inner, near = call(
        main_kernel, [VM] * 4, [block[:2] + (PINNED,), ((8 * 4 * SH, NC), F32, VM)],
        [rows(8 * NR), rows(12 * EXT), rows(4 * EXT), pltpu.SemaphoreType.DMA((4,))],
        "interior", 300000, 16,
    )(own, low, high, geo)
    osc, ove = call(
        edge_kernel, [VM] * 8 + [HBM],
        [(sc.shape, F32, HBM), (ve.shape, F32, HBM)],
        [
            rows(N_LON), rows(N_LON + 1), rows(8 * NR), rows(8 * NR),
            pltpu.VMEM((8 * SH, 4 * NC), F32),
            rows(8 * STRIP + 8), rows(12 * STRIP), rows(12 * STRIP),
            pltpu.SemaphoreType.DMA((9,)),
        ],
        "edges", 10000000, 16,
    )(near, left, right, near_lon, far_lon, don, idx, geo, *in_hbm(inner))
    return osc.reshape(scalars.shape), ove.reshape(vectors.shape)


def solution(mesh):
    return jax.shard_map(
        body,
        mesh=mesh,
        in_specs=(
            P("panel", None, None, "lat", "lon"),
            P("panel", None, None, "lat", "lon"),
            P("lat", "lon", None, None),
            P("lat", "lon", None, None),
            P(None, "lat", "lon", None, None),
            P("lat", "lon", None),
        ),
        out_specs=(P("panel", None, None, "lat", "lon"), P("panel", None, None, "lat", "lon")),
        check_vma=False,
    )
```

```python
import math

import jax
import jax.numpy as jnp
import numpy as np
from jax import lax
from jax.experimental import pallas as pl
from jax.experimental.pallas import tpu as pltpu
from jax.sharding import PartitionSpec as P

GAMMA = 5.0 / 3.0
F32 = jnp.float32
BF16 = jnp.bfloat16
SH = 24
NR = 16
NC = 128
N_LAT = 8
N_LON = 16
CAP = 19
CHUNK = 32
EXT = NR + 4
ROW_SCALARS = 4

D_TH = 0.5 * math.pi / (NR * N_LAT)
D_PH = 1.5 * math.pi / (NC * N_LON)
D_R = 0.6 * D_TH
DT = 0.3 * min(D_R, 0.6 * math.sin(0.25 * math.pi - 2.0 * D_TH) * D_PH)
MU = DT / 0.9
GRAV = 0.036 / DT
OMEGA = 0.05 / DT


def theta_of(k):
    return 0.25 * math.pi + (k + 0.5) * D_TH


def phi_of(m):
    return -0.75 * math.pi + (m + 0.5) * D_PH


def lane_rows(shift):
    lane = (np.arange(NC) + shift) % NC
    return lane // 6, lane % 6


G_ROWS = 0
G_RAD = EXT * ROW_SCALARS
G_PACK = G_RAD + 3 * SH
G_FRAME = G_PACK + 8
G_PHI = G_FRAME + 16
G_ALL = G_PHI + 8


def frame_table(i):
    wide = NC + 4
    at = np.full((4, NC), -1)
    row = 0 if i == 0 else 2
    for j in range(2):
        at[j] = (row + j) * wide + 2 + np.arange(NC)
    for side in range(2):
        r, c = lane_rows(2 * side)
        for lane in range(NC):
            col = c[lane] if side == 0 else NC - 2 + c[lane]
            if r[lane] in (0, 1):
                at[2 + side, lane] = r[lane] * wide + col
            elif r[lane] in (EXT - 2, EXT - 1):
                at[2 + side, lane] = (r[lane] - NR) * wide + col
            elif r[lane] < EXT and side == 0 and c[lane] < 2:
                at[2, lane] = 4 * wide + 2 * (r[lane] - 2) + c[lane]
            elif r[lane] < EXT and side == 1 and c[lane] >= 4:
                at[3, lane] = 4 * wide + 2 * NR + 2 * (r[lane] - 2) + c[lane] - 4
    out = np.zeros((16, NC))
    out[8:] = -1
    out[0:4] = np.where(at >= 0, at % NC, 0)
    out[8:12] = np.where(at >= 0, at // NC, -1)
    return out


def lat_table():
    out = np.zeros((N_LAT, G_PHI, NC))
    s = np.arange(SH, dtype=np.float64)
    r = 0.6 + (s + 0.5) * D_R
    ratio = np.ones(SH)
    ratio[0] = r[0] / (0.6 - 0.5 * D_R)
    ratio[-1] = r[-1] / (0.6 + (SH + 0.5) * D_R)
    out[:, G_RAD:G_PACK] = np.concatenate([1.0 / r, ratio, DT * GRAV / (r * r)])[:, None]

    def four(th):
        return np.stack([np.sin(th), np.cos(th), np.cos(th) / np.sin(th), 1.0 / np.sin(th)])

    for i in range(N_LAT):
        th = theta_of(i * NR - 2 + np.arange(EXT))
        out[i, G_ROWS:G_RAD] = four(th).T.reshape(-1)[:, None]
        for side in range(2):
            rr, _ = lane_rows(2 * side)
            at = G_PACK + 4 * side
            out[i, at : at + 4] = four(theta_of(i * NR - 2 + np.minimum(rr, EXT - 1)))
        out[i, G_FRAME:G_PHI] = frame_table(i)
    return out.astype(np.float32)


def lon_table():
    out = np.zeros((N_LON, 8, NC))
    for q in range(N_LON):
        ph = phi_of(q * NC + np.arange(NC))
        out[q, 0], out[q, 1] = np.sin(ph), np.cos(ph)
        for side in range(2):
            _, c = lane_rows(2 * side)
            ph = phi_of(q * NC + (c - 2 if side == 0 else c + NC - 4))
            out[q, 2 + 2 * side], out[q, 3 + 2 * side] = np.sin(ph), np.cos(ph)
    return out.astype(np.float32)


class Geo:
    def __init__(self, geo_ref, sin, cos, cot, isin, sphi, cphi, yang):
        self.rinv = geo_ref[G_RAD : G_RAD + SH, :]
        self.ratio = geo_ref[G_RAD + SH : G_RAD + 2 * SH, :]
        self.grav = geo_ref[G_RAD + 2 * SH : G_RAD + 3 * SH, :]
        self.ct = self.rinv * (0.5 / D_TH)
        self.cp = self.rinv * (0.5 / D_PH) * isin
        self.cotr = self.rinv * cot
        self.n_r = (1.0 - yang) * cos + yang * (sin * sphi)
        self.n_t = (yang - 1.0) * sin + yang * (cos * sphi)
        self.n_p = yang * cphi


def lane_roll(x, shift):
    return pltpu.roll(x, shift % NC, 1)


def diff_p(x):
    return lane_roll(x, -1) - lane_roll(x, 1)


def diff_r(x, ghost, edges):
    first, last = edges
    return jnp.where(last, ghost, pltpu.roll(x, SH - 1, 0)) - jnp.where(
        first, ghost, pltpu.roll(x, 1, 0)
    )


def cross(a, b):
    return (
        a[1] * b[2] - a[2] * b[1],
        a[2] * b[0] - a[0] * b[2],
        a[0] * b[1] - a[1] * b[0],
    )


def stage_one(u, diff_t, geo, edges, full):
    rinv, ct, cp, cotr = geo.rinv, geo.ct, geo.cp, geo.cotr
    cr = 0.5 / D_R
    rho, pr = u[0], u[1]
    v, b = u[2:5], u[5:8]

    def d_r(x):
        return diff_r(x, x, edges) * cr

    def d_t(fn):
        return diff_t(fn) * ct

    def d_p(x):
        return diff_p(x) * cp

    bt_r, bp_r = d_r(b[1]), d_r(b[2])
    j_r = d_t(lambda w: w[7]) + b[2] * cotr - d_p(b[1])
    jt_ang = d_p(b[0]) - b[2] * rinv
    jp_ang = b[1] * rinv - d_t(lambda w: w[5])
    jj = (j_r, jt_ang - bp_r, bt_r + jp_ang)
    vr = [d_r(x) for x in v]
    vt = [d_t(lambda w, i=i: w[2 + i]) for i in range(3)]
    vp = [d_p(x) for x in v]
    wt_ang = vp[0] - v[2] * rinv
    wp_ang = v[1] * rinv - vt[0]
    ww = (vt[2] + v[2] * cotr - vp[1], wt_ang - vr[2], vr[1] + wp_ang)
    e_ang = 2.0 * v[0] * rinv + vt[1] + v[1] * cotr + vp[2]
    ee = vr[0] + e_ang
    vxb = cross(v, b)
    el = [vxb[i] - MU * jj[i] for i in range(3)]
    ratio = geo.ratio
    level = list(ww) + [ee] + el
    level += [
        wt_ang * ratio,
        wp_ang * ratio,
        e_ang * ratio,
        vxb[1] - MU * (jt_ang * ratio),
        vxb[2] - MU * (jp_ang * ratio),
    ]
    if not full:
        return level, None, None
    fr, fp = rho * v[0], rho * v[2]
    mass = (
        d_r(fr)
        + 2.0 * fr * rinv
        + d_t(lambda w: w[0] * w[3])
        + rho * v[1] * cotr
        + d_p(fp)
    )
    gp = (d_r(pr), d_t(lambda w: w[1]), d_p(pr))
    press = -(v[0] * gp[0] + v[1] * gp[1] + v[2] * gp[2]) - GAMMA * pr * ee
    lor = cross(jj, b)
    spin = cross(v, (geo.n_r, geo.n_t, geo.n_p))
    curv = (
        -(v[1] * v[1] + v[2] * v[2]) * rinv,
        v[0] * v[1] * rinv - v[2] * v[2] * cotr,
        v[0] * v[2] * rinv + v[1] * v[2] * cotr,
    )
    irho = DT / rho
    rest = []
    for i in range(3):
        adv = v[0] * vr[i] + v[1] * vt[i] + v[2] * vp[i] + curv[i]
        x = (lor[i] - gp[i]) * irho - DT * adv + (2.0 * OMEGA * DT) * spin[i]
        rest.append(x - geo.grav if i == 0 else x)
    rest.append(irho * MU)
    return level, rest, (-DT * mass, DT * press)


def stage_two(q, diff_t, rest, geo, edges):
    rinv, ct, cp, cotr = geo.rinv, geo.ct, geo.cp, geo.cotr
    cr = 0.5 / D_R

    def d_r(i, g):
        return diff_r(q[i], q[g], edges) * cr

    def d_t(i):
        return diff_t(i) * ct

    def d_p(i):
        return diff_p(q[i]) * cp

    def curl(o, gt, gp):
        return (
            d_t(o + 2) + q[o + 2] * cotr - d_p(o + 1),
            d_p(o) - d_r(o + 2, gp) - q[o + 2] * rinv,
            d_r(o + 1, gt) + q[o + 1] * rinv - d_t(o),
        )

    cw = curl(0, 7, 8)
    grad_e = (d_r(3, 9), d_t(3), d_p(3))
    ce = curl(4, 10, 11)
    acc = [rest[i] + rest[3] * (4.0 / 3.0 * grad_e[i] - cw[i]) for i in range(3)]
    return acc + [DT * ce[i] for i in range(3)]


def shell_edges():
    s = lax.broadcasted_iota(jnp.int32, (SH, NC), 0)
    return s == 0, s == SH - 1


def aligned(i):
    return i if isinstance(i, int) else pl.multiple_of(i, 8)


def tile(ref, i):
    return ref[pl.ds(aligned(i * SH), SH), :]


def put(ref, i, val):
    ref[pl.ds(aligned(i * SH), SH), :] = val


def row_values(geo_ref, e):
    return [geo_ref[pl.ds(e * ROW_SCALARS + j, 1), :] for j in range(ROW_SCALARS)]


def row_geo(geo_ref, e, yang):
    return Geo(
        geo_ref, *row_values(geo_ref, e), geo_ref[G_PHI : G_PHI + 1, :],
        geo_ref[G_PHI + 1 : G_PHI + 2, :], yang,
    )


def rows_one(fields, q_ref, r_ref, depth, geo, edges, slot, full):
    up, dn = fields(1), fields(-1)
    level, rest, scal = stage_one(fields(0), lambda fn: fn(up) - fn(dn), geo, edges, full)
    for i, x in enumerate(level):
        put(q_ref, i * depth + slot, x)
    if full:
        for i, x in enumerate(rest):
            put(r_ref, i * depth + slot, x)
    return scal


def rows_two(q_ref, r_ref, depth, geo, edges, slot):
    q = [tile(q_ref, i * depth + slot) for i in range(12)]

    def diff_t(i):
        return tile(q_ref, i * depth + slot + 1) - tile(q_ref, i * depth + slot - 1)

    rest = [tile(r_ref, i * depth + slot) for i in range(4)]
    return stage_two(q, diff_t, rest, geo, edges)


def is_even(axis):
    return lax.rem(lax.axis_index(axis), 2) == 0


def native_row(f, k):
    return pl.ds(f * (SH * NR) + k, SH, stride=NR)


def donor_kernel(sc_hbm, ve_hbm, cr_hbm, cc_hbm, sw_hbm, rs_hbm, lat_hbm, lon_hbm,
                 pay_ref, pair_ref, other_ref, own_ref, geo_ref, idx_ref,
                 blk, cr, cc, sw, rs, s_all, c_hi, c_lo, sent_a, sent_b, chunk, sems):
    lat, lon = lax.axis_index("lat"), lax.axis_index("lon")
    n_sc = 2 * SH * NR
    moves = [
        (cr_hbm.at[0, 0], cr),
        (cc_hbm.at[0, 0], cc),
        (sw_hbm.at[:, 0, 0], sw),
        (rs_hbm, rs),
        (lat_hbm.at[lat], geo_ref.at[0:G_PHI]),
        (lon_hbm.at[lon], geo_ref.at[G_PHI:G_ALL]),
        (sc_hbm, blk.at[0:n_sc]),
        (ve_hbm, blk.at[n_sc : 4 * n_sc]),
    ]
    copies = [pltpu.make_async_copy(a, b, sems.at[i]) for i, (a, b) in enumerate(moves)]
    for c in copies:
        c.start()
    for c in copies[:3]:
        c.wait()
    tables = [cr[...].astype(F32), cc[...].astype(F32), sw[0], sw[1]]
    lane = lax.broadcasted_iota(jnp.int32, (N_LON, NC), 1).astype(F32)
    for j in range(CAP):
        a, b, wt, wp = [jnp.broadcast_to(x[:, j : j + 1], (N_LON, NC)) for x in tables]
        along = jnp.where(lane == b, 1.0 - wp, jnp.where(lane == b + 1.0, wp, 0.0))
        first, second = along * (1.0 - wt), along * wt
        here = slice(N_LON * j, N_LON * j + N_LON)
        below = slice(N_LON * (CAP + j), N_LON * (CAP + j) + N_LON)
        for k in range(NR):
            s = jnp.where(a == float(k), first, jnp.where(a == float(k - 1), second, 0.0))
            hi = s.astype(BF16)
            s_all[here, k * NC : (k + 1) * NC] = hi
            s_all[below, k * NC : (k + 1) * NC] = (s - hi.astype(F32)).astype(BF16)
    for c in copies[3:]:
        c.wait()
    at = geo_ref[G_FRAME : G_FRAME + 8, :].astype(jnp.int32)
    group = geo_ref[G_FRAME + 8 : G_FRAME + 16, :]
    g = jnp.full((8, NC), -1, jnp.int32)
    for i in range(5):
        end = min((i + 1) * NC, rs.shape[2])
        src = rs[0, :, i * NC : end]
        if end - i * NC < NC:
            src = jnp.concatenate([src, jnp.zeros((1, (i + 1) * NC - end), jnp.int32)], axis=1)
        src = jnp.broadcast_to(src, (8, NC))
        g = jnp.where(group == float(i), jnp.take_along_axis(src, at, axis=1), g)
    idx_ref[...] = g
    sphi, cphi = geo_ref[G_PHI : G_PHI + 1, :], geo_ref[G_PHI + 1 : G_PHI + 2, :]
    for k in range(NR):
        u = [blk[native_row(f, k), :] for f in range(8)]
        for f in range(8):
            put(own_ref, f * NR + k, u[f])
        sin, cos = row_values(geo_ref, k + 2)[:2]
        c = [u[0], u[1]]
        for o in (2, 5):
            flat = u[o] * sin + u[o + 1] * cos
            c += [
                flat * cphi - u[o + 2] * sphi,
                flat * sphi + u[o + 2] * cphi,
                u[o] * cos - u[o + 1] * sin,
            ]
        c = jnp.concatenate(c, axis=0)
        hi = c.astype(BF16)
        c_hi[:, k * NC : (k + 1) * NC] = hi
        c_lo[:, k * NC : (k + 1) * NC] = (c - hi.astype(F32)).astype(BF16)

    last = jnp.where(is_even("lat"), NR - 2, 0)
    for ref, k0 in ((pair_ref, last), (other_ref, NR - 2 - last)):
        for f in range(8):
            for j in range(2):
                put(ref, f * 2 + j, tile(own_ref, f * NR + k0 + j))

    def dot(x, y):
        return lax.dot_general(
            x[...], y[...], (((1,), (1,)), ((), ())), preferred_element_type=F32
        )

    slots = CAP * N_LON
    both = dot(s_all, c_hi)
    sent = both[:slots] + both[slots:] + dot(s_all.at[:slots], c_lo)
    sent_a[0:slots, :] = sent[:, 0:NC]
    sent_b[0:slots, 0:64] = sent[:, NC : NC + 64]
    for t in range(N_LON):
        mine = pl.ds(t, CAP, stride=N_LON)
        part = sent_b[mine, :]
        at = CHUNK * t
        chunk[at + 24 : at + 32, :] = jnp.zeros((8, NC), F32)
        chunk[at : at + CAP, :] = sent_a[mine, :]
        chunk[at + 19 : at + 29, 0:64] = part[0:10, 0:64]
        chunk[at + 19 : at + 28, 64:128] = part[10:19, 0:64]
        pay_ref[t] = chunk[at : at + CHUNK, :]


def row_of(own_ref, pair_ref, other_ref, f, e):
    if isinstance(e, int) and e < 2:
        at = f * 2 + e
        return jnp.where(is_even("lat"), tile(other_ref, at), tile(pair_ref, at))
    if isinstance(e, int) and e >= NR + 2:
        at = f * 2 + e - NR - 2
        return jnp.where(is_even("lat"), tile(pair_ref, at), tile(other_ref, at))
    return tile(own_ref, f * NR + e - 2)


def dense(fields, first, place):
    out = []
    for o in range(0, 8, 3):
        group = None
        for j, x in enumerate(fields[o : o + 3]):
            at = (first + 2 * j) % 6
            x = lane_roll(x, at - first)
            mine = (place == at) | (place == at + 1)
            group = x if group is None else jnp.where(mine, x, group)
        out.append(group)
    return out


def undense(group, first, j):
    return lane_roll(group, first - (first + 2 * j) % 6)


def pack_kernel(own_ref, top_ref, bot_ref, left_ref, right_ref, pair_ref, other_ref):
    lane = lax.broadcasted_iota(jnp.int32, (SH, NC), 1)
    place = lane % 6
    lefts, rights = [], []
    for f in range(8):
        left = jnp.zeros((SH, NC), F32)
        right = jnp.zeros((SH, NC), F32)
        for e in range(EXT):
            x = lane_roll(row_of(own_ref, top_ref, bot_ref, f, e), 6 * e + 2)
            base = 6 * e
            left = jnp.where((lane >= base + 2) & (lane < base + 6), x, left)
            if e == 0:
                right = jnp.where((lane >= NC - 2) | (lane < 2), x, right)
            else:
                right = jnp.where((lane >= base - 2) & (lane < base + 2), x, right)
        put(left_ref, f, left)
        put(right_ref, f, right)
        lefts.append(left)
        rights.append(right)
    even = is_even("lon")
    for i, (x, y) in enumerate(zip(dense(lefts, 2, place), dense(rights, 0, place))):
        put(pair_ref, i, jnp.where(even, y, x))
        put(other_ref, i, jnp.where(even, x, y))


def main_kernel(own_ref, top_ref, bot_ref, geo_ref, out_hbm, near_ref, out_ref, q_ref, r_ref, sems):
    k0 = jnp.where(lax.axis_index("lat") == 0, 0, NR - 4)
    for f in range(8):
        for j in range(4):
            put(near_ref, f * 4 + j, tile(own_ref, f * NR + k0 + j))
    yang = lax.axis_index("panel").astype(F32)
    edges = shell_edges()

    def one(e, full):
        def fields(step):
            return [row_of(own_ref, top_ref, bot_ref, f, e + step) for f in range(8)]

        geo = row_geo(geo_ref, e, yang)
        scal = rows_one(fields, q_ref, r_ref, EXT, geo, edges, e, full)
        if full:
            for i in range(2):
                put(out_ref, (e - 2) * 8 + i, scal[i])

    def two(e):
        vec = rows_two(q_ref, r_ref, EXT, row_geo(geo_ref, e, yang), edges, e)
        for i in range(6):
            put(out_ref, (e - 2) * 8 + 2 + i, vec[i])

    one(1, False)
    one(2, True)
    sends = []
    quarter = NR // 4
    for part in range(4):
        first = 3 + part * quarter

        @pl.loop(first, min(first + quarter, NR + 1))
        def _(e):
            one(e, True)
            two(e - 1)

        if part == 3:
            one(NR + 1, True)
            two(NR)
            one(NR + 2, False)
            two(NR + 1)
        span = pl.ds(part * quarter * 8 * SH, quarter * 8 * SH)
        sends.append(
            pltpu.make_async_copy(out_ref.at[span], out_hbm.at[span], sems.at[part])
        )
        sends[-1].start()
    for c in sends:
        c.wait()


def to_spherical(x, y, z, sin, cos, sphi, cphi):
    flat = x * cphi + y * sphi
    return [flat * sin + z * cos, flat * cos - z * sin, y * cphi - x * sphi]


def border_fields(w, sin, cos, sphi, cphi):
    out = [w[0], w[1]]
    for o in (2, 5):
        out += to_spherical(-w[o], w[o + 2], w[o + 1], sin, cos, sphi, cphi)
    return out


STRIP = 6


def edge_kernel(near_ref, left_ref, right_ref, pair_ref, other_ref,
                don_ref, idx_ref, geo_ref, int_hbm, osc_hbm, ove_hbm,
                wide_ref, thin_ref, int_ref, out_ref, bord_ref, u_ref, q_ref, r_ref, sems):
    yang = lax.axis_index("panel").astype(F32)
    lat = lax.axis_index("lat")
    lon = lax.axis_index("lon")
    edges = shell_edges()
    row_edge = (lat == 0) | (lat == N_LAT - 1)
    col_edge = (lon == 0) | (lon == N_LON - 1)
    per = SH * NR
    fetch = pltpu.make_async_copy(int_hbm, int_ref, sems.at[8])
    fetch.start()
    @pl.when(row_edge | col_edge)
    def _():
        for q in range(N_LON):
            wide_ref[24 * q : 24 * q + 24, :] = don_ref[CHUNK * q : CHUNK * q + 24, :]
            rest = don_ref[CHUNK * q + 16 : CHUNK * q + CHUNK, 0:64]
            turned = don_ref[CHUNK * q + 16 : CHUNK * q + CHUNK, 64:NC]
            thin_ref[24 * q + 16 : 24 * q + 24, :] = jnp.zeros((8, NC), F32)
            thin_ref[24 * q : 24 * q + 10, 0:64] = rest[3:13]
            thin_ref[24 * q + 10 : 24 * q + 19, 0:64] = turned[3:12]
        recv = jnp.concatenate(
            [jnp.transpose(wide_ref[...]), jnp.transpose(thin_ref[0 : 24 * N_LON, :])[0:64]], axis=0
        )
        hi = recv.astype(BF16)
        halves = jnp.concatenate([hi, (recv - hi.astype(F32)).astype(BF16)], axis=0)
        at = lax.broadcasted_iota(jnp.int32, (N_LON * 24, NC), 0)
        for col in range(4):
            g = idx_ref[col : col + 1, :]
            donor = jnp.floor((g.astype(F32) + 0.5) * (1.0 / CAP)).astype(jnp.int32)
            where = jnp.where(g >= 0, g + donor * (24 - CAP), -1)
            hot = jnp.where(at == where, 1.0, 0.0).astype(BF16)
            both = jnp.dot(halves, hot, preferred_element_type=F32)
            bord_ref[:, col * NC : (col + 1) * NC] = both[: 8 * SH] + both[8 * SH :]

    def border(col, sin, cos, sphi, cphi):
        w = [bord_ref[f * SH : f * SH + SH, col * NC : (col + 1) * NC] for f in range(8)]
        return border_fields(w, sin, cos, sphi, cphi)

    lane = lax.broadcasted_iota(jnp.int32, (SH, NC), 1)
    place = lane % 6
    merged = None
    for side in range(2):
        own = left_ref if side == 0 else right_ref
        paired = is_even("lon") if side == 1 else ~is_even("lon")
        theirs = (place < 2) if side == 0 else ((place == 2) | (place == 3))
        at = G_PACK + 4 * side
        th = [geo_ref[at + j : at + j + 1, :] for j in range(4)]
        at = G_PHI + 2 + 2 * side
        ph = [geo_ref[at + j : at + j + 1, :] for j in range(2)]
        g = jnp.broadcast_to(idx_ref[2 + side : 3 + side, :], (SH, NC))
        donated = border(2 + side, th[0], th[1], ph[0], ph[1])
        u = []
        for f in range(8):
            x = jnp.where(paired, tile(pair_ref, f // 3), tile(other_ref, f // 3))
            x = undense(x, 2 * side, f % 3)
            x = jnp.where(theirs, x, tile(own, f))
            u.append(jnp.where(g >= 0, donated[f], x))
        geo = Geo(geo_ref, *th, *ph, yang)

        def diff_six(x):
            return lane_roll(x, -6) - lane_roll(x, 6)

        level, rest, scal = stage_one(u, lambda fn: diff_six(fn(u)), geo, edges, True)
        vec = stage_two(level, lambda i: diff_six(level[i]), rest, geo, edges)
        vals = list(scal) + vec
        if side == 0:
            merged = vals
        else:
            merged = [jnp.where(place < 2, y, x) for x, y in zip(merged, vals)]
    for f in range(8):
        put(u_ref, 8 * STRIP + f, merged[f])

    @pl.when(row_edge)
    def _():
        top = lat == 0
        e0 = jnp.where(top, 0, NR - 2)
        for i in range(2):
            sc = row_values(geo_ref, jnp.where(top, i, NR + 2 + i))
            phi = [geo_ref[G_PHI + j : G_PHI + j + 1, :] for j in range(2)]
            w = border(i, sc[0], sc[1], phi[0], phi[1])
            for f in range(8):
                put(u_ref, f * STRIP + jnp.where(top, i, 4 + i), w[f])
        for j in range(4):
            for f in range(8):
                x = tile(near_ref, f * 4 + j)
                put(u_ref, f * STRIP + jnp.where(top, 2 + j, j), x)

        for slot in (1, 2, 3, 4):
            def fields(step, slot=slot):
                return [tile(u_ref, f * STRIP + slot + step) for f in range(8)]

            full = slot in (2, 3)
            geo = row_geo(geo_ref, e0 + slot, yang)
            scal = rows_one(fields, q_ref, r_ref, STRIP, geo, edges, slot, full)
            if full:
                for i in range(2):
                    put(r_ref, (4 + i) * STRIP + slot, scal[i])
        for slot in (2, 3):
            vec = rows_two(q_ref, r_ref, STRIP, row_geo(geo_ref, e0 + slot, yang), edges, slot)
            for i in range(6):
                put(r_ref, (6 + i) * STRIP + slot, vec[i])

    edge_lane = (lane < 2) | (lane >= NC - 2)
    sends = []
    fetch.wait()
    for f in range(8):
        cols = tile(u_ref, 8 * STRIP + f)
        for k in range(NR):
            x = lane_roll(cols, -(6 * (k + 2) + 2))
            out_ref[native_row(f, k), :] = jnp.where(edge_lane, x, tile(int_ref, k * 8 + f))

        @pl.when(row_edge)
        def _(f=f):
            k0 = jnp.where(lat == 0, 0, NR - 2)
            for j in range(2):
                at = native_row(f, k0 + j)
                val = tile(r_ref, (4 + f) * STRIP + 2 + j)
                out_ref[at, :] = jnp.where(edge_lane, out_ref[at, :], val)

        dst = osc_hbm.at[pl.ds(f * per, per)] if f < 2 else ove_hbm.at[pl.ds((f - 2) * per, per)]
        sends.append(pltpu.make_async_copy(out_ref.at[pl.ds(f * per, per)], dst, sems.at[f]))
        sends[-1].start()
    for c in sends:
        c.wait()


VM = pl.BlockSpec(memory_space=pltpu.VMEM)
HBM = pl.BlockSpec(memory_space=pltpu.HBM)
PINNED = pl.BlockSpec(memory_space=pltpu.HBM)


def call(kernel, ins, outs, scratch, name, flops, mib):
    return pl.pallas_call(
        kernel,
        out_shape=[
            pltpu.HBM(s, t) if m is PINNED else jax.ShapeDtypeStruct(s, t) for s, t, m in outs
        ],
        in_specs=ins,
        out_specs=[o[2] for o in outs],
        scratch_shapes=scratch,
        name=name,
        compiler_params=pltpu.CompilerParams(vmem_limit_bytes=mib * 1024 * 1024),
        cost_estimate=pl.CostEstimate(flops=flops, bytes_accessed=100000, transcendentals=0),
    )


def rows(n):
    return pltpu.VMEM((n * SH, NC), F32)


def swapped(x, axis, first):
    n = lax.axis_size(axis)
    pairs = [(i, (i + 1) % n) for i in range(first, n, 2)]
    return lax.ppermute(x, axis, pairs + [(b, a) for a, b in pairs])


def body(scalars, vectors, corner_rows, corner_cols, send_weights, recv_source):
    sc = scalars.reshape(2 * SH * NR, NC)
    ve = vectors.reshape(6 * SH * NR, NC)
    halo = ((8 * 2 * SH, NC), F32, VM)
    pack = ((8 * SH, NC), F32, VM)
    block = ((8 * NR * SH, NC), F32, VM)
    table = pltpu.VMEM((N_LON, CAP), jnp.int32)

    def in_hbm(*arrays):
        return [pltpu.with_memory_space_constraint(a, pltpu.HBM) for a in arrays]

    pay, low, high, own, geo, idx = call(
        donor_kernel, [HBM] * 8,
        [
            ((N_LON, CHUNK, NC), F32, VM), halo, halo, block,
            ((G_ALL, NC), F32, VM), ((8, NC), jnp.int32, VM),
        ],
        [
            rows(8 * NR), table, table,
            pltpu.VMEM((2, N_LON, CAP), F32),
            pltpu.VMEM((1, 1, 592), jnp.int32),
            pltpu.VMEM((2 * CAP * N_LON, NR * NC), BF16),
            pltpu.VMEM((8 * SH, NR * NC), BF16),
            pltpu.VMEM((8 * SH, NR * NC), BF16),
            rows(N_LON), rows(N_LON),
            pltpu.VMEM((CHUNK * (N_LON + 1), NC), F32),
            pltpu.SemaphoreType.DMA((8,)),
        ],
        "donor", 400000000, 20,
    )(*in_hbm(sc, ve, corner_rows, corner_cols, send_weights, recv_source,
              jnp.asarray(lat_table()), jnp.asarray(lon_table())))
    pay = lax.ppermute(pay, "panel", [(0, 1), (1, 0)])
    don = lax.all_to_all(pay, "lon", 0, 0, tiled=True).reshape(N_LON * CHUNK, NC)
    low, high = swapped(low, "lat", 0), swapped(high, "lat", 1)
    thin = ((3 * SH, NC), F32, VM)
    left, right, near_lon, far_lon = call(pack_kernel, [VM] * 3, [pack, pack, thin, thin], [], "packs", 50000000000, 12)(
        own, low, high
    )
    near_lon, far_lon = swapped(near_lon, "lon", 0), swapped(far_lon, "lon", 1)
    inner, near = call(
        main_kernel, [VM] * 4, [block[:2] + (PINNED,), ((8 * 4 * SH, NC), F32, VM)],
        [rows(8 * NR), rows(12 * EXT), rows(4 * EXT), pltpu.SemaphoreType.DMA((4,))],
        "interior", 300000, 16,
    )(own, low, high, geo)
    osc, ove = call(
        edge_kernel, [VM] * 8 + [HBM],
        [(sc.shape, F32, HBM), (ve.shape, F32, HBM)],
        [
            rows(N_LON), rows(N_LON + 1), rows(8 * NR), rows(8 * NR),
            pltpu.VMEM((8 * SH, 4 * NC), F32),
            rows(8 * STRIP + 8), rows(12 * STRIP), rows(12 * STRIP),
            pltpu.SemaphoreType.DMA((9,)),
        ],
        "edges", 10000000, 16,
    )(near, left, right, near_lon, far_lon, don, idx, geo, *in_hbm(inner))
    return osc.reshape(scalars.shape), ove.reshape(vectors.shape)


def solution(mesh):
    return jax.shard_map(
        body,
        mesh=mesh,
        in_specs=(
            P("panel", None, None, "lat", "lon"),
            P("panel", None, None, "lat", "lon"),
            P("lat", "lon", None, None),
            P("lat", "lon", None, None),
            P(None, "lat", "lon", None, None),
            P("lat", "lon", None),
        ),
        out_specs=(P("panel", None, None, "lat", "lon"), P("panel", None, None, "lat", "lon")),
        check_vma=False,
    )
```
